32 devices in a mesh: ctx: 4 (over y, x), head: 4 (over z), pipe: 2 (over core).
Axes of the slice: x: 2, y: 2, z: 4, core: 2. Of those that a mesh axis runs over, the one named last changes fastest.
Arguments:
- queries: bfloat16 [2, 512, 8192], P('pipe', 'ctx', 'head'), may hold values from -6 to 6
- keys: bfloat16 [2, 512, 8192], P('pipe', 'ctx', 'head'), may hold values from -6 to 6
- values: bfloat16 [2, 512, 8192], P('pipe', 'ctx', 'head'), may hold values from -6 to 6
- gates: bfloat16 [2, 512, 8192], P('pipe', 'ctx', 'head'), may hold values from -6 to 6
- log_decay: float32 [2, 512, 64], P('pipe', 'ctx', 'head'), may hold values from -1 to 0
- segment_ids: int32 [2, 512], P('pipe', 'ctx'), may hold values from 0 to 7, never falling along the last dimension, each value on 1 to 128 neighbouring positions
- norm_gain: float32 [2, 8192], P('pipe', 'head'), may hold values from 0.1 to 1.9
- out_weight: bfloat16 [2, 8192, 6144], P('pipe', 'head', 'ctx'), may hold values from -0.0625 to 0.0625
Outputs:
- handed: bfloat16 [2, 512, 6144], P('pipe', 'ctx', 'head')
The draws below stay inside these ranges and needn't reach their ends.
Inputs may be any that keep to these rules, and one draw needn't show every extreme that they name: `segment_ids`: along each section's tokens the ids never fall; a document has at most a quarter of 512 tokens, and one has exactly that many.
All inputs are finite; a program needn't handle non-finite values.
Results may differ from the reference program's by a relative error of at most 0.02.
Values may be sent and summed in bfloat16 or wider, within the bound.
No kernel may reach another device: no remote copies, remote signals or barrier semaphores. Data moves between devices by JAX's collectives and lax.ppermute only.
A program may use at most 128 MiB of HBM per device.

```python
import math
import jax
import jax.numpy as jnp
import numpy as np
from jax import lax

D = 6144
DH = 128
HEADS = 64
TOK_DEV = 128
TOKENS = 512
SECTIONS = 2
N_HEAD = 4


def draw_log_decay(key, part):
    streams = jax.random.split(key, 6)
    head_shape = (SECTIONS, 1, HEADS)
    slow_share = 0.5
    chooser = jax.random.uniform(streams[0], head_shape)
    slow_rate = jnp.exp(jax.random.uniform(streams[1], head_shape, minval=math.log(0.2), maxval=math.log(1.0))) / TOKENS
    fast_rate = jnp.exp(jax.random.uniform(streams[2], head_shape, minval=math.log(1.0 / 50.0), maxval=math.log(1.0 / 30.0)))
    base_rate = jnp.where(chooser < slow_share, slow_rate, fast_rate)
    shard_factor = jnp.exp(jax.random.uniform(streams[3], (SECTIONS, TOKENS // TOK_DEV, 1, HEADS), minval=-0.7, maxval=0.7))
    shard_factor = jnp.broadcast_to(shard_factor, (SECTIONS, TOKENS // TOK_DEV, TOK_DEV, HEADS)).reshape(SECTIONS, TOKENS, HEADS)
    token_factor = jnp.exp(jax.random.uniform(streams[4], (SECTIONS, TOKENS, HEADS), minval=-0.7, maxval=0.7))
    rates = base_rate * shard_factor * token_factor
    spots = jax.random.randint(streams[5], (SECTIONS, 2), 0, TOKENS)
    hits = jnp.any(jnp.arange(TOKENS)[None, :, None] == spots[:, None, :], axis=2)
    drops = jnp.log(jax.random.uniform(jax.random.fold_in(key, 7), (SECTIONS, TOKENS, HEADS), minval=0.5, maxval=0.8))
    return jnp.where(hits[:, :, None], drops - rates, -rates).astype(jnp.float32)


def block_levels(stream_key, extent, cuts, least, high):
    loudness, own = 1.0, jax.random.fold_in(stream_key, 6)
    for position, shards_of in cuts:
        heights = jnp.exp(jax.random.uniform(jax.random.fold_in(own, position), (shards_of,), jnp.float32, least / len(cuts), high / len(cuts)))
        loudness = loudness * jnp.repeat(heights, extent[position] // shards_of).reshape([-1 if axis == position else 1 for axis in range(len(extent))])
    return loudness


def split_up(number_of, total, most, slope):
    loads = [(1 << 20) // math.isqrt(rank ** slope) + 1 for rank in range(2, number_of + 1)]
    surplus, given = total - most - (number_of - 1), [1] * (number_of - 1)
    while surplus > 0:
        free = [i for i in range(number_of - 1) if given[i] < most]
        mass, budget = sum([loads[i] for i in free]), surplus
        for i in free:
            extra = min(most - given[i], max(1, budget * loads[i] // mass), surplus)
            given[i] = given[i] + extra
            surplus = surplus - extra
    return np.array([most] + given)


def uneven(stream_key, amount, total, reach, skew):
    if amount == 2:
        one = jax.random.randint(stream_key, (), max(1, total - reach), min(reach, total - 1) + 1)
        return jnp.stack([one, total - one])
    sizes = jnp.asarray(split_up(amount, total, reach, skew), jnp.int32)
    couples = (amount - 1) // 2
    source_of, sink = sizes[1:1 + 2 * couples:2], sizes[2:2 + 2 * couples:2]
    margin = jnp.minimum(source_of - 1, reach - sink)
    shifted = jax.random.randint(jax.random.fold_in(stream_key, 1), (couples,), 0, 1 << 20) % (margin + 1)
    sizes = sizes.at[1:1 + 2 * couples:2].set(source_of - shifted).at[2:2 + 2 * couples:2].set(sink + shifted)
    return sizes[jax.random.permutation(jax.random.fold_in(stream_key, 2), amount)]


def normal_values(rng, shape, deviation, reach, cuts=(), kind=jnp.bfloat16):
    factor_of = block_levels(rng, shape, cuts, -0.22, 0.18) if cuts else 1.0
    values = jax.random.normal(rng, shape, jnp.float32) * deviation * factor_of
    return jnp.minimum(jnp.maximum(values, -reach), reach).astype(kind)


def setup_inputs(seed: int = 0) -> dict:
    splits = jax.random.split(jax.random.key(seed), 9)
    queries = normal_values(splits[0], (SECTIONS, TOKENS, HEADS * DH), 1.0, 6.0, ((0, 2), (1, 4), (2, 4)))
    keys = normal_values(splits[1], (SECTIONS, TOKENS, HEADS * DH), 1.0, 6.0, ((0, 2), (1, 4), (2, 4)))
    values = normal_values(splits[2], (SECTIONS, TOKENS, HEADS * DH), 1.0, 6.0, ((0, 2), (1, 4), (2, 4)))
    gates = normal_values(splits[3], (SECTIONS, TOKENS, HEADS * DH), 1.5, 6.0, ((0, 2), (1, 4), (2, 4)))
    log_decay = draw_log_decay(jax.random.fold_in(splits[8], 71), 0)
    segment_ids = jax.vmap(lambda own: jnp.searchsorted(jnp.cumsum(uneven(own, 8, TOKENS, TOKENS // 4, 2)), jnp.arange(TOKENS), side="right"))(jax.random.split(splits[5], SECTIONS)).reshape((SECTIONS, TOKENS)).astype(jnp.int32)
    norm_gain = jnp.clip(1.0 + 0.18 * jax.random.normal(splits[6], (SECTIONS, HEADS * DH), jnp.float32), 0.1, 1.9)
    out_weight = normal_values(splits[7], (SECTIONS, HEADS * DH, D), (HEADS * DH) ** -0.5, 0.0625, ((0, 2), (1, 4), (2, 4)))
    return dict(queries=queries, keys=keys, values=values, gates=gates, log_decay=log_decay, segment_ids=segment_ids, norm_gain=norm_gain, out_weight=out_weight)


highest = lax.Precision.HIGHEST

def block_step(carried, pieces):
    kv_state, doc_id = carried
    query_rows, key_rows, value_rows, rate_rows, doc_rows = pieces
    length = doc_rows.shape[0]
    running = jnp.cumsum(rate_rows, axis=0)
    running_t = running.T
    causal = lax.broadcasted_iota(jnp.int32, (length, length), 0) >= lax.broadcasted_iota(jnp.int32, (length, length), 1)
    allowed = causal & (doc_rows[:, None] == doc_rows[None, :])
    log_gaps = running_t[:, :, None] - running_t[:, None, :]
    weights = jnp.where(allowed[None], jnp.exp(jnp.where(allowed[None], log_gaps, 0.0)), 0.0)
    scores = jnp.einsum('ihd,jhd->hij', query_rows, key_rows, preferred_element_type=jnp.float32)
    mixed = (scores * weights).astype(jnp.bfloat16)
    inside = jnp.einsum('hij,jhd->ihd', mixed, value_rows, preferred_element_type=jnp.float32)
    query_full = query_rows.astype(jnp.float32)
    key_full = key_rows.astype(jnp.float32)
    value_full = value_rows.astype(jnp.float32)
    reaches = jnp.exp(running) * (doc_rows == doc_id).astype(jnp.float32)[:, None]
    carried_part = jnp.einsum('ihd,hde->ihe', query_full * reaches[:, :, None], kv_state, precision=highest)
    final_doc = doc_rows[-1]
    retain = (doc_id == final_doc).astype(jnp.float32)
    fading = jnp.exp(running[-1][None, :] - running) * (doc_rows == final_doc).astype(jnp.float32)[:, None]
    fresh_part = jnp.einsum('jhd,jhe->hde', key_full * fading[:, :, None], value_full, precision=highest)
    new_state = retain * jnp.exp(running[-1])[:, None, None] * kv_state + fresh_part
    return ((new_state, final_doc), inside + carried_part)

def section_layer(query_rows, key_rows, value_rows, gate_rows, rate_rows, doc_ids, gain_row, weight_rows):
    block_len = min(512, TOK_DEV)
    block_count = TOKENS // block_len
    pieces = (query_rows.reshape(block_count, block_len, HEADS, DH), key_rows.reshape(block_count, block_len, HEADS, DH), value_rows.reshape(block_count, block_len, HEADS, DH), rate_rows.reshape(block_count, block_len, HEADS), doc_ids.astype(jnp.float32).reshape(block_count, block_len))
    start_carry = (jnp.zeros((HEADS, DH, DH), jnp.float32), jnp.array(-1.0, jnp.float32))
    finished, attended = lax.scan(block_step, start_carry, pieces)
    attended = attended.reshape(TOKENS, HEADS, DH)
    scaling = lax.rsqrt(lax.optimization_barrier(jnp.mean(attended * attended, axis=-1, keepdims=True)) + 1e-06)
    normed = ((attended * scaling).reshape(TOKENS, HEADS * DH) * gain_row[None, :] * jax.nn.sigmoid(gate_rows.astype(jnp.float32))).astype(jnp.bfloat16)
    group_width = HEADS * DH // N_HEAD
    summed = jnp.zeros((TOKENS, D), jnp.float32)
    for group_index in range(N_HEAD):
        lower = group_index * group_width
        partial_value = jnp.dot(normed[:, lower:lower + group_width], weight_rows[lower:lower + group_width], preferred_element_type=jnp.float32)
        rounded = lax.optimization_barrier(partial_value.astype(jnp.bfloat16))
        summed = summed + rounded.astype(jnp.float32)
    return summed.astype(jnp.bfloat16)

def reference(queries, keys, values, gates, log_decay, segment_ids, norm_gain, out_weight):
    outputs = []
    for section_index in range(SECTIONS):
        outputs.append(section_layer(queries[section_index], keys[section_index], values[section_index], gates[section_index], log_decay[section_index], segment_ids[section_index], norm_gain[section_index], out_weight[section_index]))
    return jnp.roll(jnp.stack(outputs), 1, axis=0)
```

```python
import functools
import math

import jax
import jax.numpy as jnp
from jax import lax
from jax.experimental import pallas as pl
from jax.experimental.pallas import tpu as pltpu
from jax.sharding import PartitionSpec as P

DH = 128
EXTRA = 16
VMEM = pl.BlockSpec(memory_space=pltpu.VMEM)
ANY = pl.BlockSpec(memory_space=pl.ANY)
HBM = pl.BlockSpec(memory_space=pltpu.HBM)


def dot(a, b, contract=((1,), (0,)), precision=None):
    return lax.dot_general(
        a, b, (contract, ((), ())), preferred_element_type=jnp.float32, precision=precision
    )


def running_sums(rate):
    rows = rate.shape[1]
    upper = (
        lax.broadcasted_iota(jnp.int32, (rows, rows), 0)
        <= lax.broadcasted_iota(jnp.int32, (rows, rows), 1)
    ).astype(jnp.float32)
    across = dot(rate, upper, precision=lax.Precision.HIGHEST)
    columns = dot(upper, rate, ((0,), (1,)), precision=lax.Precision.HIGHEST)
    return columns, across


def state_kernel(
    first,
    key_hbm,
    value_hbm,
    rate_hbm,
    doc_hbm,
    *refs,
):
    out_ref, key_ref, value_ref, rate_ref, doc_ref, sems, small = refs[-7:]
    rows = rate_ref.shape[1]
    wide = key_ref.shape[1]
    heads = wide // DH
    parts = sems.shape[0]
    piece = wide // parts
    copies = [
        pltpu.make_async_copy(rate_hbm.at[0], rate_ref, small.at[0]),
        pltpu.make_async_copy(doc_hbm, doc_ref, small.at[1]),
    ]
    pieces = []
    for part in range(parts):
        source = pl.ds(first * DH + part * piece, piece)
        span = pl.ds(part * piece, piece)
        pieces.append(
            [
                pltpu.make_async_copy(
                    key_hbm.at[0, :, source], key_ref.at[:, span], sems.at[part, 0]
                ),
                pltpu.make_async_copy(
                    value_hbm.at[0, :, source], value_ref.at[:, span], sems.at[part, 1]
                ),
            ]
        )
    for copy in copies + sum(pieces, []):
        copy.start()
    for copy in copies:
        copy.wait()
    columns, across = running_sums(rate_ref[...])
    doc = doc_ref[...]
    last_doc = doc[:, rows - 1 :]
    fading = jnp.where(doc == last_doc, jnp.exp(across[:, rows - 1 :] - across), 0.0)
    fading_columns = fading.T
    out_ref[wide:, :] = jnp.broadcast_to(
        (last_doc + 1).astype(jnp.float32), (EXTRA, DH)
    ).astype(jnp.bfloat16)
    for part in range(parts):
        for copy in pieces[part]:
            copy.wait()
        for k in range(part * heads // parts, (part + 1) * heads // parts):
            span = slice(k * DH, (k + 1) * DH)
            h = first + k
            faded = (key_ref[:, span].astype(jnp.float32) * fading_columns[:, h : h + 1]).astype(
                jnp.bfloat16
            )
            out_ref[span, :] = dot(faded, value_ref[:, span], ((0,), (0,))).astype(jnp.bfloat16)


def inside_kernel(
    query_hbm,
    key_hbm,
    value_hbm,
    gate_hbm,
    rate_hbm,
    doc_hbm,
    gain_hbm,
    weight_hbm,
    out_ref,
    factor_ref,
    reach_ref,
    doc_out_ref,
    query_ref,
    weight_ref,
    key_ref,
    value_ref,
    gate_ref,
    rate_ref,
    doc_ref,
    gain_ref,
    sems,
):
    sources = [rate_hbm.at[0], doc_hbm, gain_hbm, query_hbm.at[0], key_hbm.at[0], value_hbm.at[0]]
    sources += [gate_hbm.at[0], weight_hbm.at[0]]
    targets = [rate_ref, doc_ref, gain_ref, query_ref, key_ref, value_ref, gate_ref, weight_ref]
    copies = [
        pltpu.make_async_copy(source, target, sems.at[i])
        for i, (source, target) in enumerate(zip(sources, targets))
    ]
    for copy in copies:
        copy.start()
    for copy in copies[:3]:
        copy.wait()
    heads, rows = rate_ref.shape
    columns, across = running_sums(rate_ref[...])
    reach_ref[...] = jnp.exp(columns)
    doc_across = jnp.broadcast_to(doc_ref[...].astype(jnp.float32) + 1.0, (rows, rows))
    doc_out_ref[...] = doc_across.T
    allowed = (
        lax.broadcasted_iota(jnp.int32, (rows, rows), 0)
        >= lax.broadcasted_iota(jnp.int32, (rows, rows), 1)
    ) & (doc_across == doc_across.T)
    for copy in copies[3:6]:
        copy.wait()
    for h in range(heads):
        span = slice(h * DH, (h + 1) * DH)
        gaps = columns[:, h : h + 1] - across[h : h + 1, :]
        weights = jnp.where(allowed, jnp.exp(jnp.where(allowed, gaps, 0.0)), 0.0)
        scores = dot(query_ref[:, span], key_ref[:, span], ((1,), (1,)))
        mixed = (scores * weights).astype(jnp.bfloat16)
        out_ref[:, span] = dot(mixed, value_ref[:, span])
    copies[6].wait()
    for h in range(heads):
        span = slice(h * DH, (h + 1) * DH)
        gate = jax.nn.sigmoid(gate_ref[:, span].astype(jnp.float32))
        factor_ref[:, span] = gain_ref[:, span] * gate
    copies[7].wait()


def finish_kernel(
    first, inside_ref, factor_ref, reach_ref, doc_ref, query_ref, state_ref, *refs
):
    out_ref = refs[-1]
    wide = out_ref.shape[1]
    incoming = state_ref[wide:, :].astype(jnp.float32)[0:1, :]
    reached = (doc_ref[...] == incoming).astype(jnp.float32)
    for k in range(wide // DH):
        h = first + k
        span = slice(h * DH, (h + 1) * DH)
        own = slice(k * DH, (k + 1) * DH)
        reaches = reach_ref[:, h : h + 1] * reached
        attended = inside_ref[:, span] + reaches * dot(query_ref[:, span], state_ref[own, :])
        scaling = lax.rsqrt(jnp.mean(attended * attended, axis=-1, keepdims=True) + 1e-06)
        out_ref[:, own] = (attended * scaling * factor_ref[:, span]).astype(jnp.bfloat16)


def project_kernel(sides, other, *refs):
    out_ref = refs[-1]
    count = sides * out_ref.shape[0]
    pieces, weight_ref = refs[:count], refs[count]
    blocks, rows, columns = out_ref.shape
    half = (lax.axis_index("head") & 1) ^ other
    wide = math.gcd(columns, 256)
    depth = pieces[0].shape[1]
    everything = [
        jnp.concatenate([piece[...] for piece in pieces[i::sides]], axis=0) for i in range(sides)
    ]
    for start in range(0, columns, wide):
        span = pl.ds(pl.multiple_of(half * columns + start, wide), wide)
        result = sum(
            dot(everything[i], weight_ref[i * depth : (i + 1) * depth, span]) for i in range(sides)
        ).astype(jnp.bfloat16)
        for j in range(blocks):
            out_ref[j, :, start : start + wide] = result[j * rows : (j + 1) * rows]


def merge_kernel(keep_ref, arrived_ref, *refs):
    for i, out_ref in enumerate(refs[-keep_ref.shape[0] :]):
        total = keep_ref[i].astype(jnp.float32) + arrived_ref[i].astype(jnp.float32)
        out_ref[...] = total.astype(jnp.bfloat16)


def pick_kernel(*refs):
    block_refs, out_refs = refs[: len(refs) // 2], refs[len(refs) // 2 :]
    at = lax.axis_index("ctx") ^ lax.axis_index("head")
    for m, out_ref in enumerate(out_refs):
        for j, block_ref in enumerate(block_refs):

            @pl.when((at ^ m) == j)
            def _(out_ref=out_ref, block_ref=block_ref):
                out_ref[...] = block_ref[...]


def last_kernel(*refs):
    out_ref = refs[-1]
    wide = refs[0].shape[1]
    for m in range(2):
        total = refs[m][...].astype(jnp.float32) + refs[m + 2][...].astype(jnp.float32)
        half = (lax.axis_index("head") & 1) ^ m
        out_ref[0, :, pl.ds(pl.multiple_of(half * wide, wide), wide)] = total.astype(jnp.bfloat16)


def call(kernel, out_shape, name, limit=24, **more):
    return pl.pallas_call(
        kernel,
        out_shape=out_shape,
        compiler_params=pltpu.CompilerParams(vmem_limit_bytes=limit * 2**20),
        cost_estimate=pl.CostEstimate(flops=1, bytes_accessed=1, transcendentals=0),
        name=name,
        **more,
    )


def on_device(sizes, queries, keys, values, gates, log_decay, segment_ids, norm_gain, out_weight):
    n_ctx, n_head, n_pipe = sizes
    rows, width = queries.shape[1:]
    heads = width // DH
    tokens = rows * n_ctx
    hops = min(n_ctx - 1, -(-(tokens // 4 - 1) // rows))

    def stay(array):
        return pltpu.with_memory_space_constraint(array, pltpu.HBM)

    rates = stay(jnp.swapaxes(log_decay, 1, 2))
    queries, keys, values, gates = map(stay, (queries, keys, values, gates))
    segment_ids, norm_gain, out_weight = map(stay, (segment_ids, norm_gain, out_weight))
    columns = out_weight.shape[2]
    sides = 2
    side = heads // sides
    wide = side * DH

    def from_before(array, by):
        return lax.ppermute(array, "ctx", [(i, i + by) for i in range(n_ctx - by)])

    def state_of(first, after):
        parts = 2 if side % 2 == 0 else 1
        return call(
            functools.partial(state_kernel, first),
            jax.ShapeDtypeStruct((wide + EXTRA, DH), jnp.bfloat16),
            "shard_state",
            in_specs=[HBM] * 4 + [ANY] * len(after),
            scratch_shapes=[
                pltpu.VMEM((rows, wide), jnp.bfloat16),
                pltpu.VMEM((rows, wide), jnp.bfloat16),
                pltpu.VMEM((heads, rows), jnp.float32),
                pltpu.VMEM((1, rows), jnp.int32),
                pltpu.SemaphoreType.DMA((parts, 2)),
                pltpu.SemaphoreType.DMA((2,)),
            ],
        )(keys, values, rates, segment_ids, *after)

    def entering(state, first):
        incoming = from_before(state, 1)
        if hops > 1:
            decay = jnp.exp(jnp.sum(log_decay[0, :, first : first + side], axis=0))
            decay = decay.astype(jnp.bfloat16)
            total = incoming[:wide].reshape(side, DH, DH).astype(jnp.float32)
            through = jnp.ones((side,), jnp.float32)
            for by in range(2, hops + 1):
                through = through * from_before(decay, by - 1).astype(jnp.float32)
                far = from_before(state, by)
                same = jnp.where(far[wide, 0] == incoming[wide, 0], through, 0.0)
                far = far[:wide].reshape(side, DH, DH).astype(jnp.float32)
                total = total + same[:, None, None] * far
            total = total.reshape(wide, DH).astype(jnp.bfloat16)
            incoming = jnp.concatenate([total, incoming[wide:]], axis=0)
        return incoming

    states = []
    for i in range(sides):
        states.append(state_of(i * side, states))
    incoming = [entering(state, i * side) for i, state in enumerate(states)]

    inside, factor, reach, docs, query, weight = call(
        inside_kernel,
        (
            pltpu.VMEM((rows, width), jnp.float32),
            pltpu.VMEM((rows, width), jnp.float32),
            pltpu.VMEM((rows, heads), jnp.float32),
            pltpu.VMEM((rows, DH), jnp.float32),
            pltpu.VMEM((rows, width), jnp.bfloat16),
            pltpu.VMEM((width, columns), jnp.bfloat16),
        ),
        "inside",
        in_specs=[HBM] * 8,
        scratch_shapes=[
            pltpu.VMEM((rows, width), jnp.bfloat16),
            pltpu.VMEM((rows, width), jnp.bfloat16),
            pltpu.VMEM((rows, width), jnp.bfloat16),
            pltpu.VMEM((heads, rows), jnp.float32),
            pltpu.VMEM((1, rows), jnp.int32),
            pltpu.VMEM((1, width), jnp.float32),
            pltpu.SemaphoreType.DMA((8,)),
        ],
    )(queries, keys, values, gates, rates, segment_ids, norm_gain, out_weight)

    def finish(i, after):
        return call(
            functools.partial(finish_kernel, i * side),
            jax.ShapeDtypeStruct((rows, wide), jnp.bfloat16),
            "finish",
            in_specs=[VMEM] * 6 + [ANY] * len(after),
        )(inside, factor, reach, docs, query, incoming[i], *after)

    if n_ctx != 4 or n_head != 4 or n_pipe != 2:
        normed = jnp.concatenate([finish(i, ()) for i in range(sides)], axis=1)
        normed = lax.all_gather(normed, "ctx", axis=0, tiled=True)
        blocks = jnp.dot(normed, weight, preferred_element_type=jnp.float32).astype(jnp.bfloat16)
        blocks = lax.all_to_all(blocks.reshape(n_ctx, rows, columns), "ctx", 0, 0, tiled=True)
        blocks = blocks.reshape(n_head, n_ctx // n_head, rows, columns)
        blocks = lax.all_to_all(blocks, "head", 0, 0, tiled=True)
        total = jnp.sum(blocks.astype(jnp.float32), axis=0).astype(jnp.bfloat16)
        total = jnp.swapaxes(total, 0, 1).reshape(1, rows, -1)
        return lax.ppermute(total, "pipe", [(s, (s + 1) % n_pipe) for s in range(n_pipe)])

    def moved(array, target):
        names = ("ctx", "head", "pipe")
        spots = [(i, j, s) for i in range(n_ctx) for j in range(n_head) for s in range(n_pipe)]
        place = {spot: at for at, spot in enumerate(spots)}
        return lax.ppermute(array, names, [(place[spot], place[target(*spot)]) for spot in spots])

    def swapped(array, by):
        return moved(array, lambda i, j, s: (i ^ by, j, s))

    pieces = []
    for i in range(sides):
        own = finish(i, ())
        one, two = swapped(own, 1), swapped(own, 2)
        pieces.append([own, one, two, swapped(two, 1) if i % 2 else swapped(one, 2)])

    part = columns // 2
    single = jax.ShapeDtypeStruct((rows, part), jnp.bfloat16)

    def project(picked, other, after=()):
        shape = jax.ShapeDtypeStruct((len(picked), rows, part), jnp.bfloat16)
        kernel = functools.partial(project_kernel, sides, other)
        operands = [pieces[i][j] for j in picked for i in range(sides)]
        specs = [VMEM] * (len(operands) + 1) + [ANY] * len(after)
        return call(kernel, shape, "project", in_specs=specs)(*operands, weight, *after)

    blocks = [None] * n_ctx
    after, before = (pieces[0][2],), ()
    for picked in ((0,), (1, 2), (3,)):
        arrived = moved(project(picked, 1, after), lambda i, j, s: (i, j ^ 1, s))
        specs = [VMEM] * 2 + [ANY] * len(before)
        merged = call(merge_kernel, (single,) * len(picked), "merge", in_specs=specs)(
            project(picked, 0), arrived, *before
        )
        before = merged[:1]
        for k, block in zip(picked, merged):
            blocks[k] = swapped(block, k) if k else block
        after = (blocks[0],)
    picked = call(pick_kernel, (single,) * n_head, "pick")(*blocks)
    arrived = [
        moved(block, lambda i, j, s, m=m: (i, j ^ m, 1 - s)) for m, block in enumerate(picked)
    ]
    out = jax.ShapeDtypeStruct((1, rows, columns), jnp.bfloat16)
    return call(last_kernel, out, "last")(*arrived)


def solution(mesh):
    sizes = tuple(mesh.shape[axis] for axis in ("ctx", "head", "pipe"))
    return jax.shard_map(
        functools.partial(on_device, sizes),
        mesh=mesh,
        in_specs=(
            P("pipe", "ctx", "head"),
            P("pipe", "ctx", "head"),
            P("pipe", "ctx", "head"),
            P("pipe", "ctx", "head"),
            P("pipe", "ctx", "head"),
            P("pipe", "ctx"),
            P("pipe", "head"),
            P("pipe", "head", "ctx"),
        ),
        out_specs=P("pipe", "ctx", "head"),
        check_vma=False,
    )
```

```python
import functools
import math

import jax
import jax.numpy as jnp
from jax import lax
from jax.experimental import pallas as pl
from jax.experimental.pallas import tpu as pltpu
from jax.sharding import PartitionSpec as P

DH = 128
EXTRA = 16
VMEM = pl.BlockSpec(memory_space=pltpu.VMEM)
ANY = pl.BlockSpec(memory_space=pl.ANY)
HBM = pl.BlockSpec(memory_space=pltpu.HBM)


def dot(a, b, contract=((1,), (0,)), precision=None):
    return lax.dot_general(
        a, b, (contract, ((), ())), preferred_element_type=jnp.float32, precision=precision
    )


def running_sums(rate):
    rows = rate.shape[1]
    upper = (
        lax.broadcasted_iota(jnp.int32, (rows, rows), 0)
        <= lax.broadcasted_iota(jnp.int32, (rows, rows), 1)
    ).astype(jnp.float32)
    across = dot(rate, upper, precision=lax.Precision.HIGHEST)
    columns = dot(upper, rate, ((0,), (1,)), precision=lax.Precision.HIGHEST)
    return columns, across


def state_kernel(
    first,
    key_hbm,
    value_hbm,
    rate_hbm,
    doc_hbm,
    *refs,
):
    out_ref, key_ref, value_ref, rate_ref, doc_ref, sems, small = refs[-7:]
    rows = rate_ref.shape[1]
    wide = key_ref.shape[1]
    heads = wide // DH
    parts = sems.shape[0]
    piece = wide // parts
    copies = [
        pltpu.make_async_copy(rate_hbm.at[0], rate_ref, small.at[0]),
        pltpu.make_async_copy(doc_hbm, doc_ref, small.at[1]),
    ]
    pieces = []
    for part in range(parts):
        source = pl.ds(first * DH + part * piece, piece)
        span = pl.ds(part * piece, piece)
        pieces.append(
            [
                pltpu.make_async_copy(
                    key_hbm.at[0, :, source], key_ref.at[:, span], sems.at[part, 0]
                ),
                pltpu.make_async_copy(
                    value_hbm.at[0, :, source], value_ref.at[:, span], sems.at[part, 1]
                ),
            ]
        )
    for copy in copies + sum(pieces, []):
        copy.start()
    for copy in copies:
        copy.wait()
    columns, across = running_sums(rate_ref[...])
    doc = doc_ref[...]
    last_doc = doc[:, rows - 1 :]
    fading = jnp.where(doc == last_doc, jnp.exp(across[:, rows - 1 :] - across), 0.0)
    fading_columns = fading.T
    out_ref[wide:, :] = jnp.broadcast_to(
        (last_doc + 1).astype(jnp.float32), (EXTRA, DH)
    ).astype(jnp.bfloat16)
    for part in range(parts):
        for copy in pieces[part]:
            copy.wait()
        for k in range(part * heads // parts, (part + 1) * heads // parts):
            span = slice(k * DH, (k + 1) * DH)
            h = first + k
            faded = (key_ref[:, span].astype(jnp.float32) * fading_columns[:, h : h + 1]).astype(
                jnp.bfloat16
            )
            out_ref[span, :] = dot(faded, value_ref[:, span], ((0,), (0,))).astype(jnp.bfloat16)


def inside_kernel(
    query_hbm,
    key_hbm,
    value_hbm,
    gate_hbm,
    rate_hbm,
    doc_hbm,
    gain_hbm,
    weight_hbm,
    out_ref,
    factor_ref,
    reach_ref,
    doc_out_ref,
    query_ref,
    weight_ref,
    key_ref,
    value_ref,
    gate_ref,
    rate_ref,
    doc_ref,
    gain_ref,
    sems,
):
    sources = [rate_hbm.at[0], doc_hbm, gain_hbm, query_hbm.at[0], key_hbm.at[0], value_hbm.at[0]]
    sources += [gate_hbm.at[0], weight_hbm.at[0]]
    targets = [rate_ref, doc_ref, gain_ref, query_ref, key_ref, value_ref, gate_ref, weight_ref]
    copies = [
        pltpu.make_async_copy(source, target, sems.at[i])
        for i, (source, target) in enumerate(zip(sources, targets))
    ]
    for copy in copies:
        copy.start()
    for copy in copies[:3]:
        copy.wait()
    heads, rows = rate_ref.shape
    columns, across = running_sums(rate_ref[...])
    reach_ref[...] = jnp.exp(columns)
    doc_across = jnp.broadcast_to(doc_ref[...].astype(jnp.float32) + 1.0, (rows, rows))
    doc_out_ref[...] = doc_across.T
    allowed = (
        lax.broadcasted_iota(jnp.int32, (rows, rows), 0)
        >= lax.broadcasted_iota(jnp.int32, (rows, rows), 1)
    ) & (doc_across == doc_across.T)
    for copy in copies[3:6]:
        copy.wait()
    for h in range(heads):
        span = slice(h * DH, (h + 1) * DH)
        gaps = columns[:, h : h + 1] - across[h : h + 1, :]
        weights = jnp.where(allowed, jnp.exp(jnp.where(allowed, gaps, 0.0)), 0.0)
        scores = dot(query_ref[:, span], key_ref[:, span], ((1,), (1,)))
        mixed = (scores * weights).astype(jnp.bfloat16)
        out_ref[:, span] = dot(mixed, value_ref[:, span])
    copies[6].wait()
    for h in range(heads):
        span = slice(h * DH, (h + 1) * DH)
        gate = jax.nn.sigmoid(gate_ref[:, span].astype(jnp.float32))
        factor_ref[:, span] = gain_ref[:, span] * gate
    copies[7].wait()


def finish_kernel(
    first, inside_ref, factor_ref, reach_ref, doc_ref, query_ref, state_ref, *refs
):
    out_ref = refs[-1]
    wide = out_ref.shape[1]
    incoming = state_ref[wide:, :].astype(jnp.float32)[0:1, :]
    reached = (doc_ref[...] == incoming).astype(jnp.float32)
    for k in range(wide // DH):
        h = first + k
        span = slice(h * DH, (h + 1) * DH)
        own = slice(k * DH, (k + 1) * DH)
        reaches = reach_ref[:, h : h + 1] * reached
        attended = inside_ref[:, span] + reaches * dot(query_ref[:, span], state_ref[own, :])
        scaling = lax.rsqrt(jnp.mean(attended * attended, axis=-1, keepdims=True) + 1e-06)
        out_ref[:, own] = (attended * scaling * factor_ref[:, span]).astype(jnp.bfloat16)


def project_kernel(sides, other, *refs):
    out_ref = refs[-1]
    count = sides * out_ref.shape[0]
    pieces, weight_ref = refs[:count], refs[count]
    blocks, rows, columns = out_ref.shape
    half = (lax.axis_index("head") & 1) ^ other
    wide = math.gcd(columns, 256)
    depth = pieces[0].shape[1]
    everything = [
        jnp.concatenate([piece[...] for piece in pieces[i::sides]], axis=0) for i in range(sides)
    ]
    for start in range(0, columns, wide):
        span = pl.ds(pl.multiple_of(half * columns + start, wide), wide)
        result = sum(
            dot(everything[i], weight_ref[i * depth : (i + 1) * depth, span]) for i in range(sides)
        ).astype(jnp.bfloat16)
        for j in range(blocks):
            out_ref[j, :, start : start + wide] = result[j * rows : (j + 1) * rows]


def hold_kernel(source_ref, after_ref, out_ref):
    out_ref[...] = source_ref[...]


def merge_kernel(keep_ref, arrived_ref, *refs):
    for i, out_ref in enumerate(refs[-keep_ref.shape[0] :]):
        total = keep_ref[i].astype(jnp.float32) + arrived_ref[i].astype(jnp.float32)
        out_ref[...] = total.astype(jnp.bfloat16)


def pick_kernel(*refs):
    block_refs, out_refs = refs[: len(refs) // 2], refs[len(refs) // 2 :]
    at = lax.axis_index("ctx") ^ lax.axis_index("head")
    for m, out_ref in enumerate(out_refs):
        for j, block_ref in enumerate(block_refs):

            @pl.when((at ^ m) == j)
            def _(out_ref=out_ref, block_ref=block_ref):
                out_ref[...] = block_ref[...]


def last_kernel(*refs):
    out_ref = refs[-1]
    wide = refs[0].shape[1]
    for m in range(2):
        total = refs[m][...].astype(jnp.float32) + refs[m + 2][...].astype(jnp.float32)
        half = (lax.axis_index("head") & 1) ^ 1 ^ m
        out_ref[0, :, pl.ds(pl.multiple_of(half * wide, wide), wide)] = total.astype(jnp.bfloat16)


def call(kernel, out_shape, name, limit=24, **more):
    return pl.pallas_call(
        kernel,
        out_shape=out_shape,
        compiler_params=pltpu.CompilerParams(vmem_limit_bytes=limit * 2**20),
        cost_estimate=pl.CostEstimate(flops=1, bytes_accessed=1, transcendentals=0),
        name=name,
        **more,
    )


def on_device(sizes, queries, keys, values, gates, log_decay, segment_ids, norm_gain, out_weight):
    n_ctx, n_head, n_pipe = sizes
    rows, width = queries.shape[1:]
    heads = width // DH
    tokens = rows * n_ctx
    hops = min(n_ctx - 1, -(-(tokens // 4 - 1) // rows))

    def stay(array):
        return pltpu.with_memory_space_constraint(array, pltpu.HBM)

    rates = stay(jnp.swapaxes(log_decay, 1, 2))
    queries, keys, values, gates = map(stay, (queries, keys, values, gates))
    segment_ids, norm_gain, out_weight = map(stay, (segment_ids, norm_gain, out_weight))
    columns = out_weight.shape[2]
    sides = 2
    side = heads // sides
    wide = side * DH

    def from_before(array, by):
        return lax.ppermute(array, "ctx", [(i, i + by) for i in range(n_ctx - by)])

    def state_of(first, after):
        parts = 2 if side % 2 == 0 else 1
        return call(
            functools.partial(state_kernel, first),
            jax.ShapeDtypeStruct((wide + EXTRA, DH), jnp.bfloat16),
            "shard_state",
            in_specs=[HBM] * 4 + [ANY] * len(after),
            scratch_shapes=[
                pltpu.VMEM((rows, wide), jnp.bfloat16),
                pltpu.VMEM((rows, wide), jnp.bfloat16),
                pltpu.VMEM((heads, rows), jnp.float32),
                pltpu.VMEM((1, rows), jnp.int32),
                pltpu.SemaphoreType.DMA((parts, 2)),
                pltpu.SemaphoreType.DMA((2,)),
            ],
        )(keys, values, rates, segment_ids, *after)

    def entering(state, first):
        incoming = from_before(state, 1)
        if hops > 1:
            decay = jnp.exp(jnp.sum(log_decay[0, :, first : first + side], axis=0))
            decay = decay.astype(jnp.bfloat16)
            total = incoming[:wide].reshape(side, DH, DH).astype(jnp.float32)
            through = jnp.ones((side,), jnp.float32)
            for by in range(2, hops + 1):
                through = through * from_before(decay, by - 1).astype(jnp.float32)
                far = from_before(state, by)
                same = jnp.where(far[wide, 0] == incoming[wide, 0], through, 0.0)
                far = far[:wide].reshape(side, DH, DH).astype(jnp.float32)
                total = total + same[:, None, None] * far
            total = total.reshape(wide, DH).astype(jnp.bfloat16)
            incoming = jnp.concatenate([total, incoming[wide:]], axis=0)
        return incoming

    states = []
    for i in range(sides):
        states.append(state_of(i * side, states))
    incoming = [entering(state, i * side) for i, state in enumerate(states)]

    inside, factor, reach, docs, query, weight = call(
        inside_kernel,
        (
            pltpu.VMEM((rows, width), jnp.float32),
            pltpu.VMEM((rows, width), jnp.float32),
            pltpu.VMEM((rows, heads), jnp.float32),
            pltpu.VMEM((rows, DH), jnp.float32),
            pltpu.VMEM((rows, width), jnp.bfloat16),
            pltpu.VMEM((width, columns), jnp.bfloat16),
        ),
        "inside",
        in_specs=[HBM] * 8,
        scratch_shapes=[
            pltpu.VMEM((rows, width), jnp.bfloat16),
            pltpu.VMEM((rows, width), jnp.bfloat16),
            pltpu.VMEM((rows, width), jnp.bfloat16),
            pltpu.VMEM((heads, rows), jnp.float32),
            pltpu.VMEM((1, rows), jnp.int32),
            pltpu.VMEM((1, width), jnp.float32),
            pltpu.SemaphoreType.DMA((8,)),
        ],
    )(queries, keys, values, gates, rates, segment_ids, norm_gain, out_weight)

    def finish(i, after):
        return call(
            functools.partial(finish_kernel, i * side),
            jax.ShapeDtypeStruct((rows, wide), jnp.bfloat16),
            "finish",
            in_specs=[VMEM] * 6 + [ANY] * len(after),
        )(inside, factor, reach, docs, query, incoming[i], *after)

    if n_ctx != 4 or n_head != 4 or n_pipe != 2:
        normed = jnp.concatenate([finish(i, ()) for i in range(sides)], axis=1)
        normed = lax.all_gather(normed, "ctx", axis=0, tiled=True)
        blocks = jnp.dot(normed, weight, preferred_element_type=jnp.float32).astype(jnp.bfloat16)
        blocks = lax.all_to_all(blocks.reshape(n_ctx, rows, columns), "ctx", 0, 0, tiled=True)
        blocks = blocks.reshape(n_head, n_ctx // n_head, rows, columns)
        blocks = lax.all_to_all(blocks, "head", 0, 0, tiled=True)
        total = jnp.sum(blocks.astype(jnp.float32), axis=0).astype(jnp.bfloat16)
        total = jnp.swapaxes(total, 0, 1).reshape(1, rows, -1)
        return lax.ppermute(total, "pipe", [(s, (s + 1) % n_pipe) for s in range(n_pipe)])

    def moved(array, target):
        names = ("ctx", "head", "pipe")
        spots = [(i, j, s) for i in range(n_ctx) for j in range(n_head) for s in range(n_pipe)]
        place = {spot: at for at, spot in enumerate(spots)}
        return lax.ppermute(array, names, [(place[spot], place[target(*spot)]) for spot in spots])

    def swapped(array, by):
        return moved(array, lambda i, j, s: (i ^ by, j, s))

    pieces = []
    for i in range(sides):
        own = finish(i, ())
        pieces.append([own, swapped(own, 1), swapped(own, 2)])
    block = jax.ShapeDtypeStruct((rows, wide), jnp.bfloat16)
    held = call(hold_kernel, block, "hold", in_specs=[VMEM, ANY])(pieces[0][1], pieces[1][2])
    pieces[1].append(swapped(pieces[1][2], 1))
    pieces[0].append(swapped(held, 2))

    part = columns // 2
    single = jax.ShapeDtypeStruct((rows, part), jnp.bfloat16)

    def project(picked, other, after=()):
        shape = jax.ShapeDtypeStruct((len(picked), rows, part), jnp.bfloat16)
        kernel = functools.partial(project_kernel, sides, other)
        operands = [pieces[i][j] for j in picked for i in range(sides)]
        specs = [VMEM] * (len(operands) + 1) + [ANY] * len(after)
        return call(kernel, shape, "project", in_specs=specs)(*operands, weight, *after)

    blocks = [None] * n_ctx
    after, before = (pieces[0][2],), ()
    for picked in ((0,), (1, 2), (3,)):
        arrived = moved(project(picked, 1, after), lambda i, j, s: (i, j ^ 1, s))
        specs = [VMEM] * 2 + [ANY] * len(before)
        merged = call(merge_kernel, (single,) * len(picked), "merge", in_specs=specs)(
            project(picked, 0), arrived, *before
        )
        before = merged[:1]
        for k, block in zip(picked, merged):
            blocks[k] = swapped(block, k) if k else block
        after = (blocks[0],)
    picked = call(pick_kernel, (single,) * n_head, "pick")(*blocks)
    arrived = [
        moved(picked[m], lambda i, j, s, m=m: (i, j ^ m, 1 - s)) for m in reversed(range(n_head))
    ]
    out = jax.ShapeDtypeStruct((1, rows, columns), jnp.bfloat16)
    return call(last_kernel, out, "last")(*arrived)


def solution(mesh):
    sizes = tuple(mesh.shape[axis] for axis in ("ctx", "head", "pipe"))
    return jax.shard_map(
        functools.partial(on_device, sizes),
        mesh=mesh,
        in_specs=(
            P("pipe", "ctx", "head"),
            P("pipe", "ctx", "head"),
            P("pipe", "ctx", "head"),
            P("pipe", "ctx", "head"),
            P("pipe", "ctx", "head"),
            P("pipe", "ctx"),
            P("pipe", "head"),
            P("pipe", "head", "ctx"),
        ),
        out_specs=P("pipe", "ctx", "head"),
        check_vma=False,
    )
```

```python
import functools
import math

import jax
import jax.numpy as jnp
from jax import lax
from jax.experimental import pallas as pl
from jax.experimental.pallas import tpu as pltpu
from jax.sharding import PartitionSpec as P

DH = 128
EXTRA = 16
VMEM = pl.BlockSpec(memory_space=pltpu.VMEM)
ANY = pl.BlockSpec(memory_space=pl.ANY)
HBM = pl.BlockSpec(memory_space=pltpu.HBM)


def dot(a, b, contract=((1,), (0,)), precision=None):
    return lax.dot_general(
        a, b, (contract, ((), ())), preferred_element_type=jnp.float32, precision=precision
    )


def running_sums(rate):
    rows = rate.shape[1]
    upper = (
        lax.broadcasted_iota(jnp.int32, (rows, rows), 0)
        <= lax.broadcasted_iota(jnp.int32, (rows, rows), 1)
    ).astype(jnp.float32)
    across = dot(rate, upper, precision=lax.Precision.HIGHEST)
    columns = dot(upper, rate, ((0,), (1,)), precision=lax.Precision.HIGHEST)
    return columns, across


def own_fading(doc, across, key_ref, value_ref, first, out_ref):
    rows = doc.shape[1]
    wide = out_ref.shape[0] - EXTRA
    last_doc = doc[:, rows - 1 :]
    fading = jnp.where(doc == last_doc, jnp.exp(across[:, rows - 1 :] - across), 0.0)
    fading_columns = fading.T
    out_ref[wide:, :] = jnp.broadcast_to(
        (last_doc + 1).astype(jnp.float32), (EXTRA, DH)
    ).astype(jnp.bfloat16)
    for k in range(wide // DH):
        h = first + k
        span = slice(h * DH, (h + 1) * DH)
        faded = (key_ref[:, span].astype(jnp.float32) * fading_columns[:, h : h + 1]).astype(
            jnp.bfloat16
        )
        out_ref[k * DH : (k + 1) * DH, :] = dot(faded, value_ref[:, span], ((0,), (0,))).astype(
            jnp.bfloat16
        )


def state_kernel(
    key_hbm,
    value_hbm,
    rate_hbm,
    doc_hbm,
    *refs,
):
    out_ref, key_ref, value_ref, rate_ref, doc_ref, sems, small = refs[-7:]
    rows = rate_ref.shape[1]
    wide = key_ref.shape[1]
    parts = sems.shape[0]
    piece = wide // parts
    copies = [
        pltpu.make_async_copy(rate_hbm.at[0], rate_ref, small.at[0]),
        pltpu.make_async_copy(doc_hbm, doc_ref, small.at[1]),
    ]
    pieces = []
    for part in range(parts):
        span = pl.ds(part * piece, piece)
        pieces.append(
            [
                pltpu.make_async_copy(
                    key_hbm.at[0, :, span], key_ref.at[:, span], sems.at[part, 0]
                ),
                pltpu.make_async_copy(
                    value_hbm.at[0, :, span], value_ref.at[:, span], sems.at[part, 1]
                ),
            ]
        )
    for copy in copies + sum(pieces, []):
        copy.start()
    for copy in copies:
        copy.wait()
    columns, across = running_sums(rate_ref[...])
    for part in range(parts):
        for copy in pieces[part]:
            copy.wait()
    own_fading(doc_ref[...], across, key_ref, value_ref, 0, out_ref)


def inside_kernel(
    query_hbm,
    key_hbm,
    value_hbm,
    gate_hbm,
    rate_hbm,
    doc_hbm,
    gain_hbm,
    weight_hbm,
    out_ref,
    factor_ref,
    reach_ref,
    doc_out_ref,
    query_ref,
    weight_ref,
    key_ref,
    value_ref,
    gate_ref,
    rate_ref,
    doc_ref,
    gain_ref,
    sems,
):
    sources = [rate_hbm.at[0], doc_hbm, gain_hbm, query_hbm.at[0], key_hbm.at[0], value_hbm.at[0]]
    sources += [gate_hbm.at[0], weight_hbm.at[0]]
    targets = [rate_ref, doc_ref, gain_ref, query_ref, key_ref, value_ref, gate_ref, weight_ref]
    copies = [
        pltpu.make_async_copy(source, target, sems.at[i])
        for i, (source, target) in enumerate(zip(sources, targets))
    ]
    for copy in copies:
        copy.start()
    for copy in copies[:3]:
        copy.wait()
    heads, rows = rate_ref.shape
    columns, across = running_sums(rate_ref[...])
    reach_ref[...] = jnp.exp(columns)
    doc_across = jnp.broadcast_to(doc_ref[...].astype(jnp.float32) + 1.0, (rows, rows))
    doc_out_ref[...] = doc_across.T
    allowed = (
        lax.broadcasted_iota(jnp.int32, (rows, rows), 0)
        >= lax.broadcasted_iota(jnp.int32, (rows, rows), 1)
    ) & (doc_across == doc_across.T)
    for copy in copies[3:6]:
        copy.wait()
    for h in range(heads):
        span = slice(h * DH, (h + 1) * DH)
        gaps = columns[:, h : h + 1] - across[h : h + 1, :]
        weights = jnp.where(allowed, jnp.exp(jnp.where(allowed, gaps, 0.0)), 0.0)
        scores = dot(query_ref[:, span], key_ref[:, span], ((1,), (1,)))
        mixed = (scores * weights).astype(jnp.bfloat16)
        out_ref[:, span] = dot(mixed, value_ref[:, span])
    copies[6].wait()
    for h in range(heads):
        span = slice(h * DH, (h + 1) * DH)
        gate = jax.nn.sigmoid(gate_ref[:, span].astype(jnp.float32))
        factor_ref[:, span] = gain_ref[:, span] * gate
    copies[7].wait()


def finish_kernel(
    inside_ref, factor_ref, reach_ref, doc_ref, query_ref, state_ref, *out_refs
):
    heads = reach_ref.shape[1]
    part = out_refs[0].shape[0]
    incoming = state_ref[heads * DH :, :].astype(jnp.float32)[0:1, :]
    reached = (doc_ref[...] == incoming).astype(jnp.float32)
    for h in range(heads):
        span = slice(h * DH, (h + 1) * DH)
        reaches = reach_ref[:, h : h + 1] * reached
        attended = inside_ref[:, span] + reaches * dot(query_ref[:, span], state_ref[span, :])
        scaling = lax.rsqrt(jnp.mean(attended * attended, axis=-1, keepdims=True) + 1e-06)
        normed = (attended * scaling * factor_ref[:, span]).astype(jnp.bfloat16)
        for i, out_ref in enumerate(out_refs):
            out_ref[:, span] = normed[i * part : (i + 1) * part]


def project_kernel(other, *refs):
    out_ref = refs[-1]
    blocks, rows, columns = out_ref.shape
    pieces, weight_ref = refs[:blocks], refs[blocks]
    half = (lax.axis_index("head") & 1) ^ other
    wide = math.gcd(columns, 256)
    everything = jnp.concatenate([piece[...] for piece in pieces], axis=0)
    for start in range(0, columns, wide):
        span = pl.ds(pl.multiple_of(half * columns + start, wide), wide)
        result = dot(everything, weight_ref[:, span]).astype(jnp.bfloat16)
        for j in range(blocks):
            out_ref[j, :, start : start + wide] = result[j * rows : (j + 1) * rows]


def hold_kernel(upper_ref, lower_ref, *refs):
    for source_ref, out_ref in zip((upper_ref, lower_ref), refs[-2:]):
        out_ref[...] = source_ref[...]


def merge_kernel(layout, *refs):
    out_refs = refs[-len(layout) :]
    rows = refs[0].shape[1]
    for out_ref, places in zip(out_refs, layout):
        for i, (source, block) in enumerate(places):
            keep_ref, arrived_ref = refs[2 * source], refs[2 * source + 1]
            total = keep_ref[block].astype(jnp.float32) + arrived_ref[block].astype(jnp.float32)
            out_ref[i * rows : (i + 1) * rows, :] = total.astype(jnp.bfloat16)


def pick_kernel(*refs):
    block_refs, out_refs = refs[: len(refs) // 2], refs[len(refs) // 2 :]
    at = lax.axis_index("ctx") ^ lax.axis_index("head")
    for m, out_ref in enumerate(out_refs):
        for j, block_ref in enumerate(block_refs):

            @pl.when((at ^ m) == j)
            def _(out_ref=out_ref, block_ref=block_ref):
                out_ref[...] = block_ref[...]


def last_kernel(*refs):
    out_ref = refs[-1]
    wide = refs[0].shape[1]
    for m in range(2):
        total = refs[m][...].astype(jnp.float32) + refs[m + 2][...].astype(jnp.float32)
        half = (lax.axis_index("head") & 1) ^ 1 ^ m
        out_ref[0, :, pl.ds(pl.multiple_of(half * wide, wide), wide)] = total.astype(jnp.bfloat16)


def call(kernel, out_shape, name, limit=24, **more):
    return pl.pallas_call(
        kernel,
        out_shape=out_shape,
        compiler_params=pltpu.CompilerParams(vmem_limit_bytes=limit * 2**20),
        cost_estimate=pl.CostEstimate(flops=1, bytes_accessed=1, transcendentals=0),
        name=name,
        **more,
    )


def on_device(sizes, queries, keys, values, gates, log_decay, segment_ids, norm_gain, out_weight):
    n_ctx, n_head, n_pipe = sizes
    rows, width = queries.shape[1:]
    heads = width // DH
    tokens = rows * n_ctx
    hops = min(n_ctx - 1, -(-(tokens // 4 - 1) // rows))

    def stay(array):
        return pltpu.with_memory_space_constraint(array, pltpu.HBM)

    rates = stay(jnp.swapaxes(log_decay, 1, 2))
    queries, keys, values, gates = map(stay, (queries, keys, values, gates))
    segment_ids, norm_gain, out_weight = map(stay, (segment_ids, norm_gain, out_weight))
    columns = out_weight.shape[2]
    side = heads
    wide = width

    def from_before(array, by):
        return lax.ppermute(array, "ctx", [(i, i + by) for i in range(n_ctx - by)])

    parts = 4 if side % 4 == 0 else 1
    state_shape = jax.ShapeDtypeStruct((wide + EXTRA, DH), jnp.bfloat16)
    state = call(
        state_kernel,
        state_shape,
        "shard_state",
        in_specs=[HBM] * 4,
        scratch_shapes=[
            pltpu.VMEM((rows, wide), jnp.bfloat16),
            pltpu.VMEM((rows, wide), jnp.bfloat16),
            pltpu.VMEM((heads, rows), jnp.float32),
            pltpu.VMEM((1, rows), jnp.int32),
            pltpu.SemaphoreType.DMA((parts, 2)),
            pltpu.SemaphoreType.DMA((2,)),
        ],
    )(keys, values, rates, segment_ids)

    def entering(state, first):
        incoming = from_before(state, 1)
        if hops > 1:
            decay = jnp.exp(jnp.sum(log_decay[0, :, first : first + side], axis=0))
            decay = decay.astype(jnp.bfloat16)
            total = incoming[:wide].reshape(side, DH, DH).astype(jnp.float32)
            through = jnp.ones((side,), jnp.float32)
            for by in range(2, hops + 1):
                through = through * from_before(decay, by - 1).astype(jnp.float32)
                far = from_before(state, by)
                same = jnp.where(far[wide, 0] == incoming[wide, 0], through, 0.0)
                far = far[:wide].reshape(side, DH, DH).astype(jnp.float32)
                total = total + same[:, None, None] * far
            total = total.reshape(wide, DH).astype(jnp.bfloat16)
            incoming = jnp.concatenate([total, incoming[wide:]], axis=0)
        return incoming

    inside, factor, reach, docs, query, weight = call(
        inside_kernel,
        (
            pltpu.VMEM((rows, width), jnp.float32),
            pltpu.VMEM((rows, width), jnp.float32),
            pltpu.VMEM((rows, heads), jnp.float32),
            pltpu.VMEM((rows, DH), jnp.float32),
            pltpu.VMEM((rows, width), jnp.bfloat16),
            pltpu.VMEM((width, columns), jnp.bfloat16),
        ),
        "inside",
        in_specs=[HBM] * 8,
        scratch_shapes=[
            pltpu.VMEM((rows, width), jnp.bfloat16),
            pltpu.VMEM((rows, width), jnp.bfloat16),
            pltpu.VMEM((rows, width), jnp.bfloat16),
            pltpu.VMEM((heads, rows), jnp.float32),
            pltpu.VMEM((1, rows), jnp.int32),
            pltpu.VMEM((1, width), jnp.float32),
            pltpu.SemaphoreType.DMA((8,)),
        ],
    )(queries, keys, values, gates, rates, segment_ids, norm_gain, out_weight)
    incoming = entering(state, 0)

    part = rows // 2
    normed = call(
        finish_kernel,
        (jax.ShapeDtypeStruct((part, width), jnp.bfloat16),) * 2,
        "finish",
    )(inside, factor, reach, docs, query, incoming)

    if n_ctx != 4 or n_head != 4 or n_pipe != 2:
        normed = lax.all_gather(jnp.concatenate(normed, axis=0), "ctx", axis=0, tiled=True)
        blocks = jnp.dot(normed, weight, preferred_element_type=jnp.float32).astype(jnp.bfloat16)
        blocks = lax.all_to_all(blocks.reshape(n_ctx, rows, columns), "ctx", 0, 0, tiled=True)
        blocks = blocks.reshape(n_head, n_ctx // n_head, rows, columns)
        blocks = lax.all_to_all(blocks, "head", 0, 0, tiled=True)
        total = jnp.sum(blocks.astype(jnp.float32), axis=0).astype(jnp.bfloat16)
        total = jnp.swapaxes(total, 0, 1).reshape(1, rows, -1)
        return lax.ppermute(total, "pipe", [(s, (s + 1) % n_pipe) for s in range(n_pipe)])

    def moved(array, target):
        names = ("ctx", "head", "pipe")
        spots = [(i, j, s) for i in range(n_ctx) for j in range(n_head) for s in range(n_pipe)]
        place = {spot: at for at, spot in enumerate(spots)}
        return lax.ppermute(array, names, [(place[spot], place[target(*spot)]) for spot in spots])

    def swapped(array, by):
        return moved(array, lambda i, j, s: (i ^ by, j, s))

    single = jax.ShapeDtypeStruct((rows, columns // 2), jnp.bfloat16)

    def project(picked, other, after=()):
        shape = jax.ShapeDtypeStruct((len(picked), part, columns // 2), jnp.bfloat16)
        specs = [VMEM] * (len(picked) + 1) + [ANY] * len(after)
        kernel = functools.partial(project_kernel, other)
        return call(kernel, shape, "project", in_specs=specs)(*picked, weight, *after)

    def partner(send):
        return moved(send, lambda i, j, s: (i, j ^ 1, s))

    def merge(layout, sums, after=()):
        specs = [VMEM] * len(sums) + [ANY] * len(after)
        kernel = functools.partial(merge_kernel, layout)
        return call(kernel, (single,) * len(layout), "merge", in_specs=specs)(*sums, *after)

    upper, lower = normed
    upper_1, lower_2 = swapped(upper, 1), swapped(lower, 2)
    whole = (((0, 0), (0, 1)),)

    def hold(pair, after):
        shape = jax.ShapeDtypeStruct((part, width), jnp.bfloat16)
        specs = [VMEM] * 2 + [ANY] * len(after)
        return call(hold_kernel, (shape,) * 2, "hold", in_specs=specs)(*pair, *after)

    own_send = project((upper, lower), 1)
    own = merge(whole, (project((upper, lower), 0), partner(own_send)))
    upper, lower = hold((upper, lower), (own_send,))
    lower_1, upper_2 = swapped(lower, 1), swapped(upper, 2)
    held = hold((upper_1, lower_2), (lower_1, upper_2))
    beside = (upper_1, lower_1, upper_2, lower_2)
    beside = merge(
        (((0, 0), (0, 1)), ((0, 2), (0, 3))),
        (project(beside, 0), partner(project(beside, 1, own))),
    )
    across = (swapped(held[0], 2), swapped(held[1], 1))
    across = merge(whole, (project(across, 0), partner(project(across, 1))), beside[:1])
    blocks = [
        swapped(block, k) if k else block for k, block in enumerate((*own, *beside, *across))
    ]
    picked = call(pick_kernel, (single,) * n_head, "pick")(*blocks)
    arrived = [
        moved(picked[m], lambda i, j, s, m=m: (i, j ^ m, 1 - s)) for m in reversed(range(n_head))
    ]
    out = jax.ShapeDtypeStruct((1, rows, columns), jnp.bfloat16)
    return call(last_kernel, out, "last")(*arrived)


def solution(mesh):
    sizes = tuple(mesh.shape[axis] for axis in ("ctx", "head", "pipe"))
    return jax.shard_map(
        functools.partial(on_device, sizes),
        mesh=mesh,
        in_specs=(
            P("pipe", "ctx", "head"),
            P("pipe", "ctx", "head"),
            P("pipe", "ctx", "head"),
            P("pipe", "ctx", "head"),
            P("pipe", "ctx", "head"),
            P("pipe", "ctx"),
            P("pipe", "head"),
            P("pipe", "head", "ctx"),
        ),
        out_specs=P("pipe", "ctx", "head"),
        check_vma=False,
    )
```

```python
import functools
import math

import jax
import jax.numpy as jnp
from jax import lax
from jax.experimental import pallas as pl
from jax.experimental.pallas import tpu as pltpu
from jax.sharding import PartitionSpec as P

DH = 128
EXTRA = 16
VMEM = pl.BlockSpec(memory_space=pltpu.VMEM)
ANY = pl.BlockSpec(memory_space=pl.ANY)
HBM = pl.BlockSpec(memory_space=pltpu.HBM)


def dot(a, b, contract=((1,), (0,)), precision=None):
    return lax.dot_general(
        a, b, (contract, ((), ())), preferred_element_type=jnp.float32, precision=precision
    )


def running_sums(rate):
    rows = rate.shape[1]
    upper = (
        lax.broadcasted_iota(jnp.int32, (rows, rows), 0)
        <= lax.broadcasted_iota(jnp.int32, (rows, rows), 1)
    ).astype(jnp.float32)
    across = dot(rate, upper, precision=lax.Precision.HIGHEST)
    columns = dot(upper, rate, ((0,), (1,)), precision=lax.Precision.HIGHEST)
    return columns, across


def own_fading(doc, across, key_ref, value_ref, first, out_ref):
    rows = doc.shape[1]
    wide = out_ref.shape[0] - EXTRA
    last_doc = doc[:, rows - 1 :]
    fading = jnp.where(doc == last_doc, jnp.exp(across[:, rows - 1 :] - across), 0.0)
    fading_columns = fading.T
    out_ref[wide:, :] = jnp.broadcast_to(
        (last_doc + 1).astype(jnp.float32), (EXTRA, DH)
    ).astype(jnp.bfloat16)
    for k in range(wide // DH):
        h = first + k
        span = slice(h * DH, (h + 1) * DH)
        faded = (key_ref[:, span].astype(jnp.float32) * fading_columns[:, h : h + 1]).astype(
            jnp.bfloat16
        )
        out_ref[k * DH : (k + 1) * DH, :] = dot(faded, value_ref[:, span], ((0,), (0,))).astype(
            jnp.bfloat16
        )


def state_kernel(
    key_hbm,
    value_hbm,
    rate_hbm,
    doc_hbm,
    *refs,
):
    out_ref, key_ref, value_ref, rate_ref, doc_ref, sems, small = refs[-7:]
    rows = rate_ref.shape[1]
    wide = key_ref.shape[1]
    parts = sems.shape[0]
    piece = wide // parts
    copies = [
        pltpu.make_async_copy(rate_hbm.at[0], rate_ref, small.at[0]),
        pltpu.make_async_copy(doc_hbm, doc_ref, small.at[1]),
    ]
    pieces = []
    for part in range(parts):
        span = pl.ds(part * piece, piece)
        pieces.append(
            [
                pltpu.make_async_copy(
                    key_hbm.at[0, :, span], key_ref.at[:, span], sems.at[part, 0]
                ),
                pltpu.make_async_copy(
                    value_hbm.at[0, :, span], value_ref.at[:, span], sems.at[part, 1]
                ),
            ]
        )
    for copy in copies + sum(pieces, []):
        copy.start()
    for copy in copies:
        copy.wait()
    columns, across = running_sums(rate_ref[...])
    for part in range(parts):
        for copy in pieces[part]:
            copy.wait()
    own_fading(doc_ref[...], across, key_ref, value_ref, 0, out_ref)


def inside_kernel(
    query_hbm,
    key_hbm,
    value_hbm,
    gate_hbm,
    rate_hbm,
    doc_hbm,
    gain_hbm,
    weight_hbm,
    out_ref,
    factor_ref,
    reach_ref,
    doc_out_ref,
    query_ref,
    weight_ref,
    key_ref,
    value_ref,
    gate_ref,
    rate_ref,
    doc_ref,
    gain_ref,
    sems,
):
    sources = [rate_hbm.at[0], doc_hbm, gain_hbm, query_hbm.at[0], key_hbm.at[0], value_hbm.at[0]]
    sources += [gate_hbm.at[0], weight_hbm.at[0]]
    targets = [rate_ref, doc_ref, gain_ref, query_ref, key_ref, value_ref, gate_ref, weight_ref]
    copies = [
        pltpu.make_async_copy(source, target, sems.at[i])
        for i, (source, target) in enumerate(zip(sources, targets))
    ]
    for copy in copies:
        copy.start()
    for copy in copies[:3]:
        copy.wait()
    heads, rows = rate_ref.shape
    columns, across = running_sums(rate_ref[...])
    reach_ref[...] = jnp.exp(columns)
    doc_across = jnp.broadcast_to(doc_ref[...].astype(jnp.float32) + 1.0, (rows, rows))
    doc_out_ref[...] = doc_across.T
    allowed = (
        lax.broadcasted_iota(jnp.int32, (rows, rows), 0)
        >= lax.broadcasted_iota(jnp.int32, (rows, rows), 1)
    ) & (doc_across == doc_across.T)
    for copy in copies[3:6]:
        copy.wait()
    for h in range(heads):
        span = slice(h * DH, (h + 1) * DH)
        gaps = columns[:, h : h + 1] - across[h : h + 1, :]
        weights = jnp.where(allowed, jnp.exp(jnp.where(allowed, gaps, 0.0)), 0.0)
        scores = dot(query_ref[:, span], key_ref[:, span], ((1,), (1,)))
        mixed = (scores * weights).astype(jnp.bfloat16)
        out_ref[:, span] = dot(mixed, value_ref[:, span])
    copies[6].wait()
    for h in range(heads):
        span = slice(h * DH, (h + 1) * DH)
        gate = jax.nn.sigmoid(gate_ref[:, span].astype(jnp.float32))
        factor_ref[:, span] = gain_ref[:, span] * gate
    copies[7].wait()


def finish_kernel(
    inside_ref, factor_ref, reach_ref, doc_ref, query_ref, state_ref, *out_refs
):
    heads = reach_ref.shape[1]
    part = out_refs[0].shape[0]
    incoming = state_ref[heads * DH :, :].astype(jnp.float32)[0:1, :]
    reached = (doc_ref[...] == incoming).astype(jnp.float32)
    for h in range(heads):
        span = slice(h * DH, (h + 1) * DH)
        reaches = reach_ref[:, h : h + 1] * reached
        attended = inside_ref[:, span] + reaches * dot(query_ref[:, span], state_ref[span, :])
        scaling = lax.rsqrt(jnp.mean(attended * attended, axis=-1, keepdims=True) + 1e-06)
        normed = (attended * scaling * factor_ref[:, span]).astype(jnp.bfloat16)
        for i, out_ref in enumerate(out_refs):
            out_ref[:, span] = normed[i * part : (i + 1) * part]


def project_kernel(other, *refs):
    out_ref = refs[-1]
    blocks, rows, columns = out_ref.shape
    pieces, weight_ref = refs[:blocks], refs[blocks]
    half = (lax.axis_index("head") & 1) ^ other
    wide = math.gcd(columns, 256)
    everything = jnp.concatenate([piece[...] for piece in pieces], axis=0)
    for start in range(0, columns, wide):
        span = pl.ds(pl.multiple_of(half * columns + start, wide), wide)
        result = dot(everything, weight_ref[:, span]).astype(jnp.bfloat16)
        for j in range(blocks):
            out_ref[j, :, start : start + wide] = result[j * rows : (j + 1) * rows]


def hold_kernel(upper_ref, lower_ref, *refs):
    for source_ref, out_ref in zip((upper_ref, lower_ref), refs[-2:]):
        out_ref[...] = source_ref[...]


def merge_kernel(layout, *refs):
    out_refs = refs[-len(layout) :]
    rows = refs[0].shape[1]
    for out_ref, places in zip(out_refs, layout):
        for i, (source, block) in enumerate(places):
            keep_ref, arrived_ref = refs[2 * source], refs[2 * source + 1]
            total = keep_ref[block].astype(jnp.float32) + arrived_ref[block].astype(jnp.float32)
            out_ref[i * rows : (i + 1) * rows, :] = total.astype(jnp.bfloat16)


def pick_kernel(*refs):
    block_refs, out_refs = refs[: len(refs) // 2], refs[len(refs) // 2 :]
    at = lax.axis_index("ctx") ^ lax.axis_index("head")
    for m, out_ref in enumerate(out_refs):
        for j, block_ref in enumerate(block_refs):

            @pl.when((at ^ m) == j)
            def _(out_ref=out_ref, block_ref=block_ref):
                out_ref[...] = block_ref[...]


def last_kernel(*refs):
    out_ref = refs[-1]
    wide = refs[0].shape[1]
    for m in range(2):
        total = refs[m][...].astype(jnp.float32) + refs[m + 2][...].astype(jnp.float32)
        half = (lax.axis_index("head") & 1) ^ 1 ^ m
        out_ref[0, :, pl.ds(pl.multiple_of(half * wide, wide), wide)] = total.astype(jnp.bfloat16)


def call(kernel, out_shape, name, limit=24, **more):
    return pl.pallas_call(
        kernel,
        out_shape=out_shape,
        compiler_params=pltpu.CompilerParams(vmem_limit_bytes=limit * 2**20),
        cost_estimate=pl.CostEstimate(flops=1, bytes_accessed=1, transcendentals=0),
        name=name,
        **more,
    )


def on_device(sizes, queries, keys, values, gates, log_decay, segment_ids, norm_gain, out_weight):
    n_ctx, n_head, n_pipe = sizes
    rows, width = queries.shape[1:]
    heads = width // DH
    tokens = rows * n_ctx
    hops = min(n_ctx - 1, -(-(tokens // 4 - 1) // rows))

    def stay(array):
        return pltpu.with_memory_space_constraint(array, pltpu.HBM)

    rates = stay(jnp.swapaxes(log_decay, 1, 2))
    queries, keys, values, gates = map(stay, (queries, keys, values, gates))
    segment_ids, norm_gain, out_weight = map(stay, (segment_ids, norm_gain, out_weight))
    columns = out_weight.shape[2]
    side = heads
    wide = width

    def from_before(array, by):
        return lax.ppermute(array, "ctx", [(i, i + by) for i in range(n_ctx - by)])

    parts = 4 if side % 4 == 0 else 1
    state_shape = jax.ShapeDtypeStruct((wide + EXTRA, DH), jnp.bfloat16)
    state = call(
        state_kernel,
        state_shape,
        "shard_state",
        in_specs=[HBM] * 4,
        scratch_shapes=[
            pltpu.VMEM((rows, wide), jnp.bfloat16),
            pltpu.VMEM((rows, wide), jnp.bfloat16),
            pltpu.VMEM((heads, rows), jnp.float32),
            pltpu.VMEM((1, rows), jnp.int32),
            pltpu.SemaphoreType.DMA((parts, 2)),
            pltpu.SemaphoreType.DMA((2,)),
        ],
    )(keys, values, rates, segment_ids)

    def entering(state, first):
        incoming = from_before(state, 1)
        if hops > 1:
            decay = jnp.exp(jnp.sum(log_decay[0, :, first : first + side], axis=0))
            decay = decay.astype(jnp.bfloat16)
            total = incoming[:wide].reshape(side, DH, DH).astype(jnp.float32)
            through = jnp.ones((side,), jnp.float32)
            for by in range(2, hops + 1):
                through = through * from_before(decay, by - 1).astype(jnp.float32)
                far = from_before(state, by)
                same = jnp.where(far[wide, 0] == incoming[wide, 0], through, 0.0)
                far = far[:wide].reshape(side, DH, DH).astype(jnp.float32)
                total = total + same[:, None, None] * far
            total = total.reshape(wide, DH).astype(jnp.bfloat16)
            incoming = jnp.concatenate([total, incoming[wide:]], axis=0)
        return incoming

    inside, factor, reach, docs, query, weight = call(
        inside_kernel,
        (
            pltpu.VMEM((rows, width), jnp.float32),
            pltpu.VMEM((rows, width), jnp.float32),
            pltpu.VMEM((rows, heads), jnp.float32),
            pltpu.VMEM((rows, DH), jnp.float32),
            pltpu.VMEM((rows, width), jnp.bfloat16),
            pltpu.VMEM((width, columns), jnp.bfloat16),
        ),
        "inside",
        in_specs=[HBM] * 8,
        scratch_shapes=[
            pltpu.VMEM((rows, width), jnp.bfloat16),
            pltpu.VMEM((rows, width), jnp.bfloat16),
            pltpu.VMEM((rows, width), jnp.bfloat16),
            pltpu.VMEM((heads, rows), jnp.float32),
            pltpu.VMEM((1, rows), jnp.int32),
            pltpu.VMEM((1, width), jnp.float32),
            pltpu.SemaphoreType.DMA((8,)),
        ],
    )(queries, keys, values, gates, rates, segment_ids, norm_gain, out_weight)
    incoming = entering(state, 0)

    part = rows // 2
    normed = call(
        finish_kernel,
        (jax.ShapeDtypeStruct((part, width), jnp.bfloat16),) * 2,
        "finish",
    )(inside, factor, reach, docs, query, incoming)

    if n_ctx != 4 or n_head != 4 or n_pipe != 2:
        normed = lax.all_gather(jnp.concatenate(normed, axis=0), "ctx", axis=0, tiled=True)
        blocks = jnp.dot(normed, weight, preferred_element_type=jnp.float32).astype(jnp.bfloat16)
        blocks = lax.all_to_all(blocks.reshape(n_ctx, rows, columns), "ctx", 0, 0, tiled=True)
        blocks = blocks.reshape(n_head, n_ctx // n_head, rows, columns)
        blocks = lax.all_to_all(blocks, "head", 0, 0, tiled=True)
        total = jnp.sum(blocks.astype(jnp.float32), axis=0).astype(jnp.bfloat16)
        total = jnp.swapaxes(total, 0, 1).reshape(1, rows, -1)
        return lax.ppermute(total, "pipe", [(s, (s + 1) % n_pipe) for s in range(n_pipe)])

    def moved(array, target):
        names = ("ctx", "head", "pipe")
        spots = [(i, j, s) for i in range(n_ctx) for j in range(n_head) for s in range(n_pipe)]
        place = {spot: at for at, spot in enumerate(spots)}
        return lax.ppermute(array, names, [(place[spot], place[target(*spot)]) for spot in spots])

    def swapped(array, by):
        return moved(array, lambda i, j, s: (i ^ by, j, s))

    single = jax.ShapeDtypeStruct((rows, columns // 2), jnp.bfloat16)

    def project(picked, other, after=()):
        shape = jax.ShapeDtypeStruct((len(picked), part, columns // 2), jnp.bfloat16)
        specs = [VMEM] * (len(picked) + 1) + [ANY] * len(after)
        kernel = functools.partial(project_kernel, other)
        return call(kernel, shape, "project", in_specs=specs)(*picked, weight, *after)

    def partner(send):
        return moved(send, lambda i, j, s: (i, j ^ 1, s))

    def merge(layout, sums, after=()):
        specs = [VMEM] * len(sums) + [ANY] * len(after)
        kernel = functools.partial(merge_kernel, layout)
        return call(kernel, (single,) * len(layout), "merge", in_specs=specs)(*sums, *after)

    upper, lower = normed
    upper_1, lower_2 = swapped(upper, 1), swapped(lower, 2)
    whole = (((0, 0), (0, 1)),)

    def hold(pair, after):
        shape = jax.ShapeDtypeStruct((part, width), jnp.bfloat16)
        specs = [VMEM] * 2 + [ANY] * len(after)
        return call(hold_kernel, (shape,) * 2, "hold", in_specs=specs)(*pair, *after)

    own_send = project((upper, lower), 1)
    own = merge(whole, (project((upper, lower), 0), partner(own_send)))
    upper, lower = hold((upper, lower), (own_send,))
    lower_1, upper_2 = swapped(lower, 1), swapped(upper, 2)
    held = hold((upper_1, lower_2), (lower_1, upper_2))
    beside = (upper_1, lower_1, upper_2, lower_2)
    beside = merge(
        (((0, 0), (0, 1)), ((0, 2), (0, 3))),
        (project(beside, 0), partner(project(beside, 1, own))),
    )
    across = (swapped(held[0], 2), swapped(held[1], 1))
    across = merge(whole, (project(across, 0), partner(project(across, 1))), beside[:1])
    blocks = [
        swapped(block, k) if k else block for k, block in enumerate((*own, *beside, *across))
    ]
    picked = call(pick_kernel, (single,) * n_head, "pick")(*blocks)
    arrived = [moved(picked[m], lambda i, j, s, m=m: (i, j ^ m, s)) for m in (3, 2, 1)]
    out = jax.ShapeDtypeStruct((1, rows, columns), jnp.bfloat16)
    out = call(last_kernel, out, "last")(*arrived, picked[0])
    return moved(out, lambda i, j, s: (i, j, 1 - s))


def solution(mesh):
    sizes = tuple(mesh.shape[axis] for axis in ("ctx", "head", "pipe"))
    return jax.shard_map(
        functools.partial(on_device, sizes),
        mesh=mesh,
        in_specs=(
            P("pipe", "ctx", "head"),
            P("pipe", "ctx", "head"),
            P("pipe", "ctx", "head"),
            P("pipe", "ctx", "head"),
            P("pipe", "ctx", "head"),
            P("pipe", "ctx"),
            P("pipe", "head"),
            P("pipe", "head", "ctx"),
        ),
        out_specs=P("pipe", "ctx", "head"),
        check_vma=False,
    )
```

```python
import functools
import math

import jax
import jax.numpy as jnp
from jax import lax
from jax.experimental import pallas as pl
from jax.experimental.pallas import tpu as pltpu
from jax.sharding import PartitionSpec as P

DH = 128
EXTRA = 16
VMEM = pl.BlockSpec(memory_space=pltpu.VMEM)
ANY = pl.BlockSpec(memory_space=pl.ANY)
HBM = pl.BlockSpec(memory_space=pltpu.HBM)


def dot(a, b, contract=((1,), (0,)), precision=None):
    return lax.dot_general(
        a, b, (contract, ((), ())), preferred_element_type=jnp.float32, precision=precision
    )


def running_sums(rate):
    rows = rate.shape[1]
    upper = (
        lax.broadcasted_iota(jnp.int32, (rows, rows), 0)
        <= lax.broadcasted_iota(jnp.int32, (rows, rows), 1)
    ).astype(jnp.float32)
    across = dot(rate, upper, precision=lax.Precision.HIGHEST)
    columns = dot(upper, rate, ((0,), (1,)), precision=lax.Precision.HIGHEST)
    return columns, across


def own_fading(doc, across, key_ref, value_ref, first, out_ref):
    rows = doc.shape[1]
    wide = out_ref.shape[0] - EXTRA
    last_doc = doc[:, rows - 1 :]
    fading = jnp.where(doc == last_doc, jnp.exp(across[:, rows - 1 :] - across), 0.0)
    fading_columns = fading.T
    out_ref[wide:, :] = jnp.broadcast_to(
        (last_doc + 1).astype(jnp.float32), (EXTRA, DH)
    ).astype(jnp.bfloat16)
    for k in range(wide // DH):
        h = first + k
        span = slice(h * DH, (h + 1) * DH)
        faded = (key_ref[:, span].astype(jnp.float32) * fading_columns[:, h : h + 1]).astype(
            jnp.bfloat16
        )
        out_ref[k * DH : (k + 1) * DH, :] = dot(faded, value_ref[:, span], ((0,), (0,))).astype(
            jnp.bfloat16
        )


def state_kernel(
    key_hbm,
    value_hbm,
    rate_hbm,
    doc_hbm,
    *refs,
):
    out_ref, key_ref, value_ref, rate_ref, doc_ref, sems, small = refs[-7:]
    rows = rate_ref.shape[1]
    wide = key_ref.shape[1]
    parts = sems.shape[0]
    piece = wide // parts
    copies = [
        pltpu.make_async_copy(rate_hbm.at[0], rate_ref, small.at[0]),
        pltpu.make_async_copy(doc_hbm, doc_ref, small.at[1]),
    ]
    pieces = []
    for part in range(parts):
        span = pl.ds(part * piece, piece)
        pieces.append(
            [
                pltpu.make_async_copy(
                    key_hbm.at[0, :, span], key_ref.at[:, span], sems.at[part, 0]
                ),
                pltpu.make_async_copy(
                    value_hbm.at[0, :, span], value_ref.at[:, span], sems.at[part, 1]
                ),
            ]
        )
    for copy in copies + sum(pieces, []):
        copy.start()
    for copy in copies:
        copy.wait()
    columns, across = running_sums(rate_ref[...])
    for part in range(parts):
        for copy in pieces[part]:
            copy.wait()
    own_fading(doc_ref[...], across, key_ref, value_ref, 0, out_ref)


def inside_kernel(
    query_hbm,
    key_hbm,
    value_hbm,
    gate_hbm,
    rate_hbm,
    doc_hbm,
    gain_hbm,
    weight_hbm,
    out_ref,
    factor_ref,
    reach_ref,
    doc_out_ref,
    query_ref,
    weight_ref,
    key_ref,
    value_ref,
    gate_ref,
    rate_ref,
    doc_ref,
    gain_ref,
    sems,
):
    sources = [rate_hbm.at[0], doc_hbm, gain_hbm, query_hbm.at[0], key_hbm.at[0], value_hbm.at[0]]
    sources += [gate_hbm.at[0], weight_hbm.at[0]]
    targets = [rate_ref, doc_ref, gain_ref, query_ref, key_ref, value_ref, gate_ref, weight_ref]
    copies = [
        pltpu.make_async_copy(source, target, sems.at[i])
        for i, (source, target) in enumerate(zip(sources, targets))
    ]
    for copy in copies:
        copy.start()
    for copy in copies[:3]:
        copy.wait()
    heads, rows = rate_ref.shape
    columns, across = running_sums(rate_ref[...])
    reach_ref[...] = jnp.exp(columns)
    doc_across = jnp.broadcast_to(doc_ref[...].astype(jnp.float32) + 1.0, (rows, rows))
    doc_out_ref[...] = doc_across.T
    allowed = (
        lax.broadcasted_iota(jnp.int32, (rows, rows), 0)
        >= lax.broadcasted_iota(jnp.int32, (rows, rows), 1)
    ) & (doc_across == doc_across.T)
    for copy in copies[3:6]:
        copy.wait()
    for h in range(heads):
        span = slice(h * DH, (h + 1) * DH)
        gaps = columns[:, h : h + 1] - across[h : h + 1, :]
        weights = jnp.where(allowed, jnp.exp(jnp.where(allowed, gaps, 0.0)), 0.0)
        scores = dot(query_ref[:, span], key_ref[:, span], ((1,), (1,)))
        mixed = (scores * weights).astype(jnp.bfloat16)
        out_ref[:, span] = dot(mixed, value_ref[:, span])
    copies[6].wait()
    for h in range(heads):
        span = slice(h * DH, (h + 1) * DH)
        gate = jax.nn.sigmoid(gate_ref[:, span].astype(jnp.float32))
        factor_ref[:, span] = gain_ref[:, span] * gate
    copies[7].wait()


def finish_kernel(
    first_row, inside_ref, factor_ref, reach_ref, doc_ref, query_ref, state_ref, out_ref
):
    heads = reach_ref.shape[1]
    here = slice(first_row, first_row + out_ref.shape[0])
    incoming = state_ref[heads * DH :, :].astype(jnp.float32)[0:1, :]
    reached = (doc_ref[here, :] == incoming).astype(jnp.float32)
    for h in range(heads):
        span = slice(h * DH, (h + 1) * DH)
        reaches = reach_ref[here, h : h + 1] * reached
        attended = inside_ref[here, span] + reaches * dot(query_ref[here, span], state_ref[span, :])
        scaling = lax.rsqrt(jnp.mean(attended * attended, axis=-1, keepdims=True) + 1e-06)
        out_ref[:, span] = (attended * scaling * factor_ref[here, span]).astype(jnp.bfloat16)


def project_kernel(other, *refs):
    out_ref = refs[-1]
    blocks, rows, columns = out_ref.shape
    pieces, weight_ref = refs[:blocks], refs[blocks]
    half = (lax.axis_index("head") & 1) ^ other
    wide = math.gcd(columns, 256)
    everything = jnp.concatenate([piece[...] for piece in pieces], axis=0)
    for start in range(0, columns, wide):
        span = pl.ds(pl.multiple_of(half * columns + start, wide), wide)
        result = dot(everything, weight_ref[:, span]).astype(jnp.bfloat16)
        for j in range(blocks):
            out_ref[j, :, start : start + wide] = result[j * rows : (j + 1) * rows]


def hold_kernel(source_ref, *refs):
    refs[-1][...] = source_ref[...]


def merge_kernel(layout, *refs):
    out_refs = refs[-len(layout) :]
    rows = refs[0].shape[1]
    for out_ref, places in zip(out_refs, layout):
        for i, (source, block) in enumerate(places):
            keep_ref, arrived_ref = refs[2 * source], refs[2 * source + 1]
            total = keep_ref[block].astype(jnp.float32) + arrived_ref[block].astype(jnp.float32)
            out_ref[i * rows : (i + 1) * rows, :] = total.astype(jnp.bfloat16)


def pick_kernel(*refs):
    block_refs, out_refs = refs[: len(refs) // 2], refs[len(refs) // 2 :]
    at = lax.axis_index("ctx") ^ lax.axis_index("head")
    for m, out_ref in enumerate(out_refs):
        for j, block_ref in enumerate(block_refs):

            @pl.when((at ^ m) == j)
            def _(out_ref=out_ref, block_ref=block_ref):
                out_ref[...] = block_ref[...]


def last_kernel(*refs):
    out_ref = refs[-1]
    wide = refs[0].shape[1]
    for m in range(2):
        total = refs[m][...].astype(jnp.float32) + refs[m + 2][...].astype(jnp.float32)
        half = (lax.axis_index("head") & 1) ^ 1 ^ m
        out_ref[0, :, pl.ds(pl.multiple_of(half * wide, wide), wide)] = total.astype(jnp.bfloat16)


def call(kernel, out_shape, name, limit=24, **more):
    return pl.pallas_call(
        kernel,
        out_shape=out_shape,
        compiler_params=pltpu.CompilerParams(vmem_limit_bytes=limit * 2**20),
        cost_estimate=pl.CostEstimate(flops=1, bytes_accessed=1, transcendentals=0),
        name=name,
        **more,
    )


def on_device(sizes, queries, keys, values, gates, log_decay, segment_ids, norm_gain, out_weight):
    n_ctx, n_head, n_pipe = sizes
    rows, width = queries.shape[1:]
    heads = width // DH
    tokens = rows * n_ctx
    hops = min(n_ctx - 1, -(-(tokens // 4 - 1) // rows))

    def stay(array):
        return pltpu.with_memory_space_constraint(array, pltpu.HBM)

    rates = stay(jnp.swapaxes(log_decay, 1, 2))
    queries, keys, values, gates = map(stay, (queries, keys, values, gates))
    segment_ids, norm_gain, out_weight = map(stay, (segment_ids, norm_gain, out_weight))
    columns = out_weight.shape[2]
    side = heads
    wide = width

    def from_before(array, by):
        return lax.ppermute(array, "ctx", [(i, i + by) for i in range(n_ctx - by)])

    parts = 4 if side % 4 == 0 else 1
    state_shape = jax.ShapeDtypeStruct((wide + EXTRA, DH), jnp.bfloat16)
    state = call(
        state_kernel,
        state_shape,
        "shard_state",
        in_specs=[HBM] * 4,
        scratch_shapes=[
            pltpu.VMEM((rows, wide), jnp.bfloat16),
            pltpu.VMEM((rows, wide), jnp.bfloat16),
            pltpu.VMEM((heads, rows), jnp.float32),
            pltpu.VMEM((1, rows), jnp.int32),
            pltpu.SemaphoreType.DMA((parts, 2)),
            pltpu.SemaphoreType.DMA((2,)),
        ],
    )(keys, values, rates, segment_ids)

    def entering(state, first):
        incoming = from_before(state, 1)
        if hops > 1:
            decay = jnp.exp(jnp.sum(log_decay[0, :, first : first + side], axis=0))
            decay = decay.astype(jnp.bfloat16)
            total = incoming[:wide].reshape(side, DH, DH).astype(jnp.float32)
            through = jnp.ones((side,), jnp.float32)
            for by in range(2, hops + 1):
                through = through * from_before(decay, by - 1).astype(jnp.float32)
                far = from_before(state, by)
                same = jnp.where(far[wide, 0] == incoming[wide, 0], through, 0.0)
                far = far[:wide].reshape(side, DH, DH).astype(jnp.float32)
                total = total + same[:, None, None] * far
            total = total.reshape(wide, DH).astype(jnp.bfloat16)
            incoming = jnp.concatenate([total, incoming[wide:]], axis=0)
        return incoming

    inside, factor, reach, docs, query, weight = call(
        inside_kernel,
        (
            pltpu.VMEM((rows, width), jnp.float32),
            pltpu.VMEM((rows, width), jnp.float32),
            pltpu.VMEM((rows, heads), jnp.float32),
            pltpu.VMEM((rows, DH), jnp.float32),
            pltpu.VMEM((rows, width), jnp.bfloat16),
            pltpu.VMEM((width, columns), jnp.bfloat16),
        ),
        "inside",
        in_specs=[HBM] * 8,
        scratch_shapes=[
            pltpu.VMEM((rows, width), jnp.bfloat16),
            pltpu.VMEM((rows, width), jnp.bfloat16),
            pltpu.VMEM((rows, width), jnp.bfloat16),
            pltpu.VMEM((heads, rows), jnp.float32),
            pltpu.VMEM((1, rows), jnp.int32),
            pltpu.VMEM((1, width), jnp.float32),
            pltpu.SemaphoreType.DMA((8,)),
        ],
    )(queries, keys, values, gates, rates, segment_ids, norm_gain, out_weight)
    incoming = entering(state, 0)

    part = rows // 2
    piece = jax.ShapeDtypeStruct((part, width), jnp.bfloat16)

    def finish(first_row):
        kernel = functools.partial(finish_kernel, first_row)
        return call(kernel, piece, "finish")(inside, factor, reach, docs, query, incoming)

    normed = [finish(0), finish(part)]

    if n_ctx != 4 or n_head != 4 or n_pipe != 2:
        normed = lax.all_gather(jnp.concatenate(normed, axis=0), "ctx", axis=0, tiled=True)
        blocks = jnp.dot(normed, weight, preferred_element_type=jnp.float32).astype(jnp.bfloat16)
        blocks = lax.all_to_all(blocks.reshape(n_ctx, rows, columns), "ctx", 0, 0, tiled=True)
        blocks = blocks.reshape(n_head, n_ctx // n_head, rows, columns)
        blocks = lax.all_to_all(blocks, "head", 0, 0, tiled=True)
        total = jnp.sum(blocks.astype(jnp.float32), axis=0).astype(jnp.bfloat16)
        total = jnp.swapaxes(total, 0, 1).reshape(1, rows, -1)
        return lax.ppermute(total, "pipe", [(s, (s + 1) % n_pipe) for s in range(n_pipe)])

    def moved(array, target):
        names = ("ctx", "head", "pipe")
        spots = [(i, j, s) for i in range(n_ctx) for j in range(n_head) for s in range(n_pipe)]
        place = {spot: at for at, spot in enumerate(spots)}
        return lax.ppermute(array, names, [(place[spot], place[target(*spot)]) for spot in spots])

    def swapped(array, by):
        return moved(array, lambda i, j, s: (i ^ by, j, s))

    single = jax.ShapeDtypeStruct((rows, columns // 2), jnp.bfloat16)

    def project(picked, other, after=()):
        shape = jax.ShapeDtypeStruct((len(picked), part, columns // 2), jnp.bfloat16)
        specs = [VMEM] * (len(picked) + 1) + [ANY] * len(after)
        kernel = functools.partial(project_kernel, other)
        return call(kernel, shape, "project", in_specs=specs)(*picked, weight, *after)

    def partner(send):
        return moved(send, lambda i, j, s: (i, j ^ 1, s))

    def merge(layout, sums, after=()):
        specs = [VMEM] * len(sums) + [ANY] * len(after)
        kernel = functools.partial(merge_kernel, layout)
        return call(kernel, (single,) * len(layout), "merge", in_specs=specs)(*sums, *after)

    def hold(array, *after):
        specs = [VMEM] + [ANY] * len(after)
        return call(hold_kernel, piece, "hold", in_specs=specs)(array, *after)

    upper, lower = normed
    whole = (((0, 0), (0, 1)),)
    upper_1, upper_2 = swapped(upper, 1), swapped(upper, 2)
    own_send = project((upper, lower), 1)
    own = merge(whole, (project((upper, lower), 0), partner(own_send)))
    lower = hold(lower, own_send)
    lower_1, lower_2 = swapped(lower, 1), swapped(lower, 2)
    near = (upper_1, upper_2)
    near_sum = (project(near, 0), partner(project(near, 1, own)))
    later = (lower_1, lower_2)
    later_sum = (project(later, 0), partner(project(later, 1, near_sum[1:])))
    beside = merge((((0, 0), (1, 0)), ((0, 1), (1, 1))), near_sum + later_sum)
    across = (swapped(hold(upper_1, lower_1, lower_2), 2), swapped(lower_2, 1))
    across_sum = (project(across, 0), partner(project(across, 1, beside[:1])))
    across = merge(whole, across_sum, beside[:1])
    blocks = [
        swapped(block, k) if k else block for k, block in enumerate((*own, *beside, *across))
    ]
    picked = call(pick_kernel, (single,) * n_head, "pick")(*blocks)
    arrived = [moved(picked[m], lambda i, j, s, m=m: (i, j ^ m, s)) for m in (3, 2, 1)]
    out = jax.ShapeDtypeStruct((1, rows, columns), jnp.bfloat16)
    out = call(last_kernel, out, "last")(*arrived, picked[0])
    return moved(out, lambda i, j, s: (i, j, 1 - s))


def solution(mesh):
    sizes = tuple(mesh.shape[axis] for axis in ("ctx", "head", "pipe"))
    return jax.shard_map(
        functools.partial(on_device, sizes),
        mesh=mesh,
        in_specs=(
            P("pipe", "ctx", "head"),
            P("pipe", "ctx", "head"),
            P("pipe", "ctx", "head"),
            P("pipe", "ctx", "head"),
            P("pipe", "ctx", "head"),
            P("pipe", "ctx"),
            P("pipe", "head"),
            P("pipe", "head", "ctx"),
        ),
        out_specs=P("pipe", "ctx", "head"),
        check_vma=False,
    )
```

```python
import functools
import math

import jax
import jax.numpy as jnp
from jax import lax
from jax.experimental import pallas as pl
from jax.experimental.pallas import tpu as pltpu
from jax.sharding import PartitionSpec as P

DH = 128
EXTRA = 16
VMEM = pl.BlockSpec(memory_space=pltpu.VMEM)
ANY = pl.BlockSpec(memory_space=pl.ANY)
HBM = pl.BlockSpec(memory_space=pltpu.HBM)


def dot(a, b, contract=((1,), (0,)), precision=None):
    return lax.dot_general(
        a, b, (contract, ((), ())), preferred_element_type=jnp.float32, precision=precision
    )


def running_sums(rate):
    rows = rate.shape[1]
    upper = (
        lax.broadcasted_iota(jnp.int32, (rows, rows), 0)
        <= lax.broadcasted_iota(jnp.int32, (rows, rows), 1)
    ).astype(jnp.float32)
    across = dot(rate, upper, precision=lax.Precision.HIGHEST)
    columns = dot(upper, rate, ((0,), (1,)), precision=lax.Precision.HIGHEST)
    return columns, across


def own_fading(doc, across, key_ref, value_ref, first, out_ref):
    rows = doc.shape[1]
    wide = out_ref.shape[0] - EXTRA
    last_doc = doc[:, rows - 1 :]
    fading = jnp.where(doc == last_doc, jnp.exp(across[:, rows - 1 :] - across), 0.0)
    fading_columns = fading.T
    out_ref[wide:, :] = jnp.broadcast_to(
        (last_doc + 1).astype(jnp.float32), (EXTRA, DH)
    ).astype(jnp.bfloat16)
    for k in range(wide // DH):
        h = first + k
        span = slice(h * DH, (h + 1) * DH)
        faded = (key_ref[:, span].astype(jnp.float32) * fading_columns[:, h : h + 1]).astype(
            jnp.bfloat16
        )
        out_ref[k * DH : (k + 1) * DH, :] = dot(faded, value_ref[:, span], ((0,), (0,))).astype(
            jnp.bfloat16
        )


def state_kernel(
    key_hbm,
    value_hbm,
    rate_hbm,
    doc_hbm,
    *refs,
):
    out_ref, key_ref, value_ref, rate_ref, doc_ref, sems, small = refs[-7:]
    rows = rate_ref.shape[1]
    wide = key_ref.shape[1]
    parts = sems.shape[0]
    piece = wide // parts
    copies = [
        pltpu.make_async_copy(rate_hbm.at[0], rate_ref, small.at[0]),
        pltpu.make_async_copy(doc_hbm, doc_ref, small.at[1]),
    ]
    pieces = []
    for part in range(parts):
        span = pl.ds(part * piece, piece)
        pieces.append(
            [
                pltpu.make_async_copy(
                    key_hbm.at[0, :, span], key_ref.at[:, span], sems.at[part, 0]
                ),
                pltpu.make_async_copy(
                    value_hbm.at[0, :, span], value_ref.at[:, span], sems.at[part, 1]
                ),
            ]
        )
    for copy in copies + sum(pieces, []):
        copy.start()
    for copy in copies:
        copy.wait()
    columns, across = running_sums(rate_ref[...])
    for part in range(parts):
        for copy in pieces[part]:
            copy.wait()
    own_fading(doc_ref[...], across, key_ref, value_ref, 0, out_ref)


def inside_kernel(
    query_hbm,
    key_hbm,
    value_hbm,
    gate_hbm,
    rate_hbm,
    doc_hbm,
    gain_hbm,
    weight_hbm,
    out_ref,
    factor_ref,
    doc_out_ref,
    query_ref,
    weight_ref,
    key_ref,
    value_ref,
    gate_ref,
    rate_ref,
    doc_ref,
    gain_ref,
    sems,
):
    sources = [rate_hbm.at[0], doc_hbm, gain_hbm, query_hbm.at[0], key_hbm.at[0], value_hbm.at[0]]
    sources += [gate_hbm.at[0], weight_hbm.at[0]]
    targets = [rate_ref, doc_ref, gain_ref, query_ref, key_ref, value_ref, gate_ref, weight_ref]
    copies = [
        pltpu.make_async_copy(source, target, sems.at[i])
        for i, (source, target) in enumerate(zip(sources, targets))
    ]
    for copy in copies:
        copy.start()
    for copy in copies[:3]:
        copy.wait()
    heads, rows = rate_ref.shape
    columns, across = running_sums(rate_ref[...])
    reach = jnp.exp(columns)
    doc_across = jnp.broadcast_to(doc_ref[...].astype(jnp.float32) + 1.0, (rows, rows))
    doc_out_ref[...] = doc_across.T
    allowed = (
        lax.broadcasted_iota(jnp.int32, (rows, rows), 0)
        >= lax.broadcasted_iota(jnp.int32, (rows, rows), 1)
    ) & (doc_across == doc_across.T)
    for copy in copies[3:6]:
        copy.wait()
    for h in range(heads):
        span = slice(h * DH, (h + 1) * DH)
        gaps = columns[:, h : h + 1] - across[h : h + 1, :]
        weights = jnp.where(allowed, jnp.exp(jnp.where(allowed, gaps, 0.0)), 0.0)
        scores = dot(query_ref[:, span], key_ref[:, span], ((1,), (1,)))
        mixed = (scores * weights).astype(jnp.bfloat16)
        out_ref[:, span] = dot(mixed, value_ref[:, span])
        reached = query_ref[:, span].astype(jnp.float32) * reach[:, h : h + 1]
        query_ref[:, span] = reached.astype(jnp.bfloat16)
    copies[6].wait()
    for h in range(heads):
        span = slice(h * DH, (h + 1) * DH)
        gate = jax.nn.sigmoid(gate_ref[:, span].astype(jnp.float32))
        factor_ref[:, span] = gain_ref[:, span] * gate
    copies[7].wait()


def finish_kernel(inside_ref, factor_ref, doc_ref, query_ref, state_ref, *out_refs):
    width = inside_ref.shape[1]
    part = out_refs[0].shape[0]
    incoming = state_ref[width:, :].astype(jnp.float32)[0:1, :]
    reached = (doc_ref[...] == incoming).astype(jnp.float32)
    average = jnp.full((DH, DH), 1.0 / DH, jnp.bfloat16)
    for start in range(0, width, DH):
        span = slice(start, start + DH)
        attended = inside_ref[:, span] + reached * dot(query_ref[:, span], state_ref[span, :])
        mean = dot((attended * attended).astype(jnp.bfloat16), average)
        scaling = lax.rsqrt(mean + 1e-06) * factor_ref[:, span]
        normed = (attended * scaling).astype(jnp.bfloat16)
        for i, out_ref in enumerate(out_refs):
            out_ref[:, span] = normed[i * part : (i + 1) * part]


def project_kernel(other, *refs):
    out_ref = refs[-1]
    blocks, rows, columns = out_ref.shape
    pieces, weight_ref = refs[:blocks], refs[blocks]
    half = (lax.axis_index("head") & 1) ^ other
    wide = math.gcd(columns, 256)
    everything = jnp.concatenate([piece[...] for piece in pieces], axis=0)
    for start in range(0, columns, wide):
        span = pl.ds(pl.multiple_of(half * columns + start, wide), wide)
        result = dot(everything, weight_ref[:, span]).astype(jnp.bfloat16)
        for j in range(blocks):
            out_ref[j, :, start : start + wide] = result[j * rows : (j + 1) * rows]


def hold_kernel(upper_ref, lower_ref, *refs):
    for source_ref, out_ref in zip((upper_ref, lower_ref), refs[-2:]):
        out_ref[...] = source_ref[...]


def merge_kernel(layout, *refs):
    out_refs = refs[-len(layout) :]
    rows = refs[0].shape[1]
    for out_ref, places in zip(out_refs, layout):
        for i, (source, block) in enumerate(places):
            keep_ref, arrived_ref = refs[2 * source], refs[2 * source + 1]
            total = keep_ref[block].astype(jnp.float32) + arrived_ref[block].astype(jnp.float32)
            out_ref[i * rows : (i + 1) * rows, :] = total.astype(jnp.bfloat16)


def pick_kernel(*refs):
    count = lax.axis_size("head")
    block_refs, out_refs = refs[: -count], refs[-count:]
    at = lax.axis_index("ctx") ^ lax.axis_index("head")
    for m, out_ref in enumerate(out_refs):
        for j in range(count):

            @pl.when((at ^ m) == j)
            def _(out_ref=out_ref, j=j):
                if j < count - 1:
                    out_ref[...] = block_refs[j][...]
                else:
                    out_ref[...] = jnp.concatenate([ref[...] for ref in block_refs[j:]], axis=0)


def last_kernel(*refs):
    out_ref = refs[-1]
    wide = refs[0].shape[1]
    for m in range(2):
        total = refs[m][...].astype(jnp.float32) + refs[m + 2][...].astype(jnp.float32)
        half = (lax.axis_index("head") & 1) ^ 1 ^ m
        out_ref[0, :, pl.ds(pl.multiple_of(half * wide, wide), wide)] = total.astype(jnp.bfloat16)


def call(kernel, out_shape, name, limit=24, **more):
    return pl.pallas_call(
        kernel,
        out_shape=out_shape,
        compiler_params=pltpu.CompilerParams(vmem_limit_bytes=limit * 2**20),
        cost_estimate=pl.CostEstimate(flops=1, bytes_accessed=1, transcendentals=0),
        name=name,
        **more,
    )


def on_device(sizes, queries, keys, values, gates, log_decay, segment_ids, norm_gain, out_weight):
    n_ctx, n_head, n_pipe = sizes
    rows, width = queries.shape[1:]
    heads = width // DH
    tokens = rows * n_ctx
    hops = min(n_ctx - 1, -(-(tokens // 4 - 1) // rows))

    def stay(array):
        return pltpu.with_memory_space_constraint(array, pltpu.HBM)

    rates = stay(jnp.swapaxes(log_decay, 1, 2))
    queries, keys, values, gates = map(stay, (queries, keys, values, gates))
    segment_ids, norm_gain, out_weight = map(stay, (segment_ids, norm_gain, out_weight))
    columns = out_weight.shape[2]
    side = heads
    wide = width

    def from_before(array, by):
        return lax.ppermute(array, "ctx", [(i, i + by) for i in range(n_ctx - by)])

    parts = 4 if side % 4 == 0 else 1
    state_shape = jax.ShapeDtypeStruct((wide + EXTRA, DH), jnp.bfloat16)
    state = call(
        state_kernel,
        state_shape,
        "shard_state",
        in_specs=[HBM] * 4,
        scratch_shapes=[
            pltpu.VMEM((rows, wide), jnp.bfloat16),
            pltpu.VMEM((rows, wide), jnp.bfloat16),
            pltpu.VMEM((heads, rows), jnp.float32),
            pltpu.VMEM((1, rows), jnp.int32),
            pltpu.SemaphoreType.DMA((parts, 2)),
            pltpu.SemaphoreType.DMA((2,)),
        ],
    )(keys, values, rates, segment_ids)

    def entering(state, first):
        incoming = from_before(state, 1)
        if hops > 1:
            decay = jnp.exp(jnp.sum(log_decay[0, :, first : first + side], axis=0))
            decay = decay.astype(jnp.bfloat16)
            total = incoming[:wide].reshape(side, DH, DH).astype(jnp.float32)
            through = jnp.ones((side,), jnp.float32)
            for by in range(2, hops + 1):
                through = through * from_before(decay, by - 1).astype(jnp.float32)
                far = from_before(state, by)
                same = jnp.where(far[wide, 0] == incoming[wide, 0], through, 0.0)
                far = far[:wide].reshape(side, DH, DH).astype(jnp.float32)
                total = total + same[:, None, None] * far
            total = total.reshape(wide, DH).astype(jnp.bfloat16)
            incoming = jnp.concatenate([total, incoming[wide:]], axis=0)
        return incoming

    inside, factor, docs, query, weight = call(
        inside_kernel,
        (
            pltpu.VMEM((rows, width), jnp.float32),
            pltpu.VMEM((rows, width), jnp.float32),
            pltpu.VMEM((rows, DH), jnp.float32),
            pltpu.VMEM((rows, width), jnp.bfloat16),
            pltpu.VMEM((width, columns), jnp.bfloat16),
        ),
        "inside",
        in_specs=[HBM] * 8,
        scratch_shapes=[
            pltpu.VMEM((rows, width), jnp.bfloat16),
            pltpu.VMEM((rows, width), jnp.bfloat16),
            pltpu.VMEM((rows, width), jnp.bfloat16),
            pltpu.VMEM((heads, rows), jnp.float32),
            pltpu.VMEM((1, rows), jnp.int32),
            pltpu.VMEM((1, width), jnp.float32),
            pltpu.SemaphoreType.DMA((8,)),
        ],
    )(queries, keys, values, gates, rates, segment_ids, norm_gain, out_weight)
    incoming = entering(state, 0)

    part = rows // 2
    normed = call(
        finish_kernel,
        (jax.ShapeDtypeStruct((part, width), jnp.bfloat16),) * 2,
        "finish",
    )(inside, factor, docs, query, incoming)

    if n_ctx != 4 or n_head != 4 or n_pipe != 2:
        normed = lax.all_gather(jnp.concatenate(normed, axis=0), "ctx", axis=0, tiled=True)
        blocks = jnp.dot(normed, weight, preferred_element_type=jnp.float32).astype(jnp.bfloat16)
        blocks = lax.all_to_all(blocks.reshape(n_ctx, rows, columns), "ctx", 0, 0, tiled=True)
        blocks = blocks.reshape(n_head, n_ctx // n_head, rows, columns)
        blocks = lax.all_to_all(blocks, "head", 0, 0, tiled=True)
        total = jnp.sum(blocks.astype(jnp.float32), axis=0).astype(jnp.bfloat16)
        total = jnp.swapaxes(total, 0, 1).reshape(1, rows, -1)
        return lax.ppermute(total, "pipe", [(s, (s + 1) % n_pipe) for s in range(n_pipe)])

    def moved(array, target):
        names = ("ctx", "head", "pipe")
        spots = [(i, j, s) for i in range(n_ctx) for j in range(n_head) for s in range(n_pipe)]
        place = {spot: at for at, spot in enumerate(spots)}
        return lax.ppermute(array, names, [(place[spot], place[target(*spot)]) for spot in spots])

    def swapped(array, by):
        return moved(array, lambda i, j, s: (i ^ by, j, s))

    single = jax.ShapeDtypeStruct((rows, columns // 2), jnp.bfloat16)

    def project(picked, other, after=()):
        shape = jax.ShapeDtypeStruct((len(picked), part, columns // 2), jnp.bfloat16)
        specs = [VMEM] * (len(picked) + 1) + [ANY] * len(after)
        kernel = functools.partial(project_kernel, other)
        return call(kernel, shape, "project", in_specs=specs)(*picked, weight, *after)

    def partner(send):
        return moved(send, lambda i, j, s: (i, j ^ 1, s))

    def merge(layout, sums, after=()):
        specs = [VMEM] * len(sums) + [ANY] * len(after)
        kernel = functools.partial(merge_kernel, layout)
        shapes = [jax.ShapeDtypeStruct((part * len(x), columns // 2), jnp.bfloat16) for x in layout]
        return call(kernel, tuple(shapes), "merge", in_specs=specs)(*sums, *after)

    upper, lower = normed
    upper_1, lower_2 = swapped(upper, 1), swapped(lower, 2)
    whole = (((0, 0), (0, 1)),)

    def hold(pair, after):
        shape = jax.ShapeDtypeStruct((part, width), jnp.bfloat16)
        specs = [VMEM] * 2 + [ANY] * len(after)
        return call(hold_kernel, (shape,) * 2, "hold", in_specs=specs)(*pair, *after)

    own_send = project((upper, lower), 1)
    own = merge(whole, (project((upper, lower), 0), partner(own_send)))
    upper, lower = hold((upper, lower), (own_send,))
    lower_1, upper_2 = swapped(lower, 1), swapped(upper, 2)
    held = hold((upper_1, lower_2), (lower_1, upper_2, *own))
    beside = (upper_1, lower_1, upper_2, lower_2)
    beside_send, beside_keep = project(beside, 1, own), project(beside, 0)
    beside = merge(
        (((0, 0), (0, 1)), ((0, 2), (0, 3))),
        (beside_keep, partner(beside_send)),
    )
    across = (swapped(held[0], 2), swapped(held[1], 1))
    across_sum = (project(across, 0), partner(project(across, 1, (beside_keep,))))
    across = merge((((0, 0),), ((0, 1),)), across_sum, beside[:1])
    blocks = [*own, *(swapped(block, k + 1) for k, block in enumerate(beside))]
    blocks += [swapped(block, 3) for block in across]
    picked = call(pick_kernel, (single,) * n_head, "pick")(*blocks)
    arrived = [moved(picked[m], lambda i, j, s, m=m: (i, j ^ m, s)) for m in (3, 2, 1)]
    out = jax.ShapeDtypeStruct((1, rows, columns), jnp.bfloat16)
    out = call(last_kernel, out, "last")(*arrived, picked[0])
    return moved(out, lambda i, j, s: (i, j, 1 - s))


def solution(mesh):
    sizes = tuple(mesh.shape[axis] for axis in ("ctx", "head", "pipe"))
    return jax.shard_map(
        functools.partial(on_device, sizes),
        mesh=mesh,
        in_specs=(
            P("pipe", "ctx", "head"),
            P("pipe", "ctx", "head"),
            P("pipe", "ctx", "head"),
            P("pipe", "ctx", "head"),
            P("pipe", "ctx", "head"),
            P("pipe", "ctx"),
            P("pipe", "head"),
            P("pipe", "head", "ctx"),
        ),
        out_specs=P("pipe", "ctx", "head"),
        check_vma=False,
    )
```

```python
import functools
import math

import jax
import jax.numpy as jnp
from jax import lax
from jax.experimental import pallas as pl
from jax.experimental.pallas import tpu as pltpu
from jax.sharding import PartitionSpec as P

DH = 128
EXTRA = 16
VMEM = pl.BlockSpec(memory_space=pltpu.VMEM)
ANY = pl.BlockSpec(memory_space=pl.ANY)
HBM = pl.BlockSpec(memory_space=pltpu.HBM)


def dot(a, b, contract=((1,), (0,)), precision=None):
    return lax.dot_general(
        a, b, (contract, ((), ())), preferred_element_type=jnp.float32, precision=precision
    )


def running_sums(rate):
    rows = rate.shape[1]
    upper = (
        lax.broadcasted_iota(jnp.int32, (rows, rows), 0)
        <= lax.broadcasted_iota(jnp.int32, (rows, rows), 1)
    ).astype(jnp.float32)
    across = dot(rate, upper, precision=lax.Precision.HIGHEST)
    columns = dot(upper, rate, ((0,), (1,)), precision=lax.Precision.HIGHEST)
    return columns, across


def own_fading(doc, across, key_ref, value_ref, first, out_ref):
    rows = doc.shape[1]
    wide = out_ref.shape[0] - EXTRA
    last_doc = doc[:, rows - 1 :]
    fading = jnp.where(doc == last_doc, jnp.exp(across[:, rows - 1 :] - across), 0.0)
    fading_columns = fading.T
    out_ref[wide:, :] = jnp.broadcast_to(
        (last_doc + 1).astype(jnp.float32), (EXTRA, DH)
    ).astype(jnp.bfloat16)
    for k in range(wide // DH):
        h = first + k
        span = slice(h * DH, (h + 1) * DH)
        faded = (key_ref[:, span].astype(jnp.float32) * fading_columns[:, h : h + 1]).astype(
            jnp.bfloat16
        )
        out_ref[k * DH : (k + 1) * DH, :] = dot(faded, value_ref[:, span], ((0,), (0,))).astype(
            jnp.bfloat16
        )


def state_kernel(
    key_hbm,
    value_hbm,
    rate_hbm,
    doc_hbm,
    *refs,
):
    out_ref, key_ref, value_ref, rate_ref, doc_ref, sems, small = refs[-7:]
    rows = rate_ref.shape[1]
    wide = key_ref.shape[1]
    parts = sems.shape[0]
    piece = wide // parts
    copies = [
        pltpu.make_async_copy(rate_hbm.at[0], rate_ref, small.at[0]),
        pltpu.make_async_copy(doc_hbm, doc_ref, small.at[1]),
    ]
    pieces = []
    for part in range(parts):
        span = pl.ds(part * piece, piece)
        pieces.append(
            [
                pltpu.make_async_copy(
                    key_hbm.at[0, :, span], key_ref.at[:, span], sems.at[part, 0]
                ),
                pltpu.make_async_copy(
                    value_hbm.at[0, :, span], value_ref.at[:, span], sems.at[part, 1]
                ),
            ]
        )
    for copy in copies + sum(pieces, []):
        copy.start()
    for copy in copies:
        copy.wait()
    columns, across = running_sums(rate_ref[...])
    for part in range(parts):
        for copy in pieces[part]:
            copy.wait()
    own_fading(doc_ref[...], across, key_ref, value_ref, 0, out_ref)


def inside_kernel(
    query_hbm,
    key_hbm,
    value_hbm,
    gate_hbm,
    rate_hbm,
    doc_hbm,
    gain_hbm,
    weight_hbm,
    out_ref,
    factor_ref,
    doc_out_ref,
    query_ref,
    weight_ref,
    key_ref,
    value_ref,
    gate_ref,
    rate_ref,
    doc_ref,
    gain_ref,
    sems,
):
    sources = [rate_hbm.at[0], doc_hbm, gain_hbm, query_hbm.at[0], key_hbm.at[0], value_hbm.at[0]]
    sources += [gate_hbm.at[0], weight_hbm.at[0]]
    targets = [rate_ref, doc_ref, gain_ref, query_ref, key_ref, value_ref, gate_ref, weight_ref]
    copies = [
        pltpu.make_async_copy(source, target, sems.at[i])
        for i, (source, target) in enumerate(zip(sources, targets))
    ]
    for copy in copies:
        copy.start()
    for copy in copies[:3]:
        copy.wait()
    heads, rows = rate_ref.shape
    columns, across = running_sums(rate_ref[...])
    reach = jnp.exp(columns)
    doc_across = jnp.broadcast_to(doc_ref[...].astype(jnp.float32) + 1.0, (rows, rows))
    doc_out_ref[...] = doc_across.T
    allowed = (
        lax.broadcasted_iota(jnp.int32, (rows, rows), 0)
        >= lax.broadcasted_iota(jnp.int32, (rows, rows), 1)
    ) & (doc_across == doc_across.T)
    for copy in copies[3:6]:
        copy.wait()
    for h in range(heads):
        span = slice(h * DH, (h + 1) * DH)
        gaps = columns[:, h : h + 1] - across[h : h + 1, :]
        weights = jnp.where(allowed, jnp.exp(jnp.where(allowed, gaps, 0.0)), 0.0)
        scores = dot(query_ref[:, span], key_ref[:, span], ((1,), (1,)))
        mixed = (scores * weights).astype(jnp.bfloat16)
        out_ref[:, span] = dot(mixed, value_ref[:, span])
        reached = query_ref[:, span].astype(jnp.float32) * reach[:, h : h + 1]
        query_ref[:, span] = reached.astype(jnp.bfloat16)
    copies[6].wait()
    for h in range(heads):
        span = slice(h * DH, (h + 1) * DH)
        gate = jax.nn.sigmoid(gate_ref[:, span].astype(jnp.float32))
        factor_ref[:, span] = gain_ref[:, span] * gate
    copies[7].wait()


def finish_kernel(inside_ref, factor_ref, doc_ref, query_ref, state_ref, *out_refs):
    width = inside_ref.shape[1]
    part = out_refs[0].shape[0]
    incoming = state_ref[width:, :].astype(jnp.float32)[0:1, :]
    reached = (doc_ref[...] == incoming).astype(jnp.float32)
    average = jnp.full((DH, DH), 1.0 / DH, jnp.bfloat16)
    for start in range(0, width, DH):
        span = slice(start, start + DH)
        attended = inside_ref[:, span] + reached * dot(query_ref[:, span], state_ref[span, :])
        mean = dot((attended * attended).astype(jnp.bfloat16), average)
        scaling = lax.rsqrt(mean + 1e-06) * factor_ref[:, span]
        normed = (attended * scaling).astype(jnp.bfloat16)
        for i, out_ref in enumerate(out_refs):
            out_ref[:, span] = normed[i * part : (i + 1) * part]


def project_kernel(other, *refs):
    out_ref = refs[-1]
    blocks, rows, columns = out_ref.shape
    pieces, weight_ref = refs[:blocks], refs[blocks]
    half = (lax.axis_index("head") & 1) ^ other
    wide = math.gcd(columns, 256)
    everything = jnp.concatenate([piece[...] for piece in pieces], axis=0)
    for start in range(0, columns, wide):
        span = pl.ds(pl.multiple_of(half * columns + start, wide), wide)
        result = dot(everything, weight_ref[:, span]).astype(jnp.bfloat16)
        for j in range(blocks):
            out_ref[j, :, start : start + wide] = result[j * rows : (j + 1) * rows]


def hold_kernel(upper_ref, lower_ref, *refs):
    for source_ref, out_ref in zip((upper_ref, lower_ref), refs[-2:]):
        out_ref[...] = source_ref[...]


def merge_kernel(layout, *refs):
    out_refs = refs[-len(layout) :]
    rows = refs[0].shape[1]
    for out_ref, places in zip(out_refs, layout):
        for i, (source, block) in enumerate(places):
            keep_ref, arrived_ref = refs[2 * source], refs[2 * source + 1]
            total = keep_ref[block].astype(jnp.float32) + arrived_ref[block].astype(jnp.float32)
            out_ref[i * rows : (i + 1) * rows, :] = total.astype(jnp.bfloat16)


def pick_kernel(*refs):
    count = lax.axis_size("head")
    block_refs, out_refs = refs[: -count], refs[-count:]
    at = lax.axis_index("ctx") ^ lax.axis_index("head")
    for m, out_ref in enumerate(out_refs):
        for j in range(count):

            @pl.when((at ^ m) == j)
            def _(out_ref=out_ref, j=j):
                if j < count - 1:
                    out_ref[...] = block_refs[j][...]
                else:
                    out_ref[...] = jnp.concatenate([ref[...] for ref in block_refs[j:]], axis=0)


def last_kernel(*refs):
    out_ref = refs[-1]
    wide = refs[0].shape[1]
    for m in range(2):
        total = refs[m][...].astype(jnp.float32) + refs[m + 2][...].astype(jnp.float32)
        half = (lax.axis_index("head") & 1) ^ 1 ^ m
        out_ref[0, :, pl.ds(pl.multiple_of(half * wide, wide), wide)] = total.astype(jnp.bfloat16)


def call(kernel, out_shape, name, limit=24, **more):
    return pl.pallas_call(
        kernel,
        out_shape=out_shape,
        compiler_params=pltpu.CompilerParams(vmem_limit_bytes=limit * 2**20),
        cost_estimate=pl.CostEstimate(flops=1, bytes_accessed=1, transcendentals=0),
        name=name,
        **more,
    )


def on_device(sizes, queries, keys, values, gates, log_decay, segment_ids, norm_gain, out_weight):
    n_ctx, n_head, n_pipe = sizes
    rows, width = queries.shape[1:]
    heads = width // DH
    tokens = rows * n_ctx
    hops = min(n_ctx - 1, -(-(tokens // 4 - 1) // rows))

    def stay(array):
        return pltpu.with_memory_space_constraint(array, pltpu.HBM)

    rates = stay(jnp.swapaxes(log_decay, 1, 2))
    queries, keys, values, gates = map(stay, (queries, keys, values, gates))
    segment_ids, norm_gain, out_weight = map(stay, (segment_ids, norm_gain, out_weight))
    columns = out_weight.shape[2]
    side = heads
    wide = width

    def from_before(array, by):
        return lax.ppermute(array, "ctx", [(i, i + by) for i in range(n_ctx - by)])

    parts = 4 if side % 4 == 0 else 1
    state_shape = jax.ShapeDtypeStruct((wide + EXTRA, DH), jnp.bfloat16)
    state = call(
        state_kernel,
        state_shape,
        "shard_state",
        in_specs=[HBM] * 4,
        scratch_shapes=[
            pltpu.VMEM((rows, wide), jnp.bfloat16),
            pltpu.VMEM((rows, wide), jnp.bfloat16),
            pltpu.VMEM((heads, rows), jnp.float32),
            pltpu.VMEM((1, rows), jnp.int32),
            pltpu.SemaphoreType.DMA((parts, 2)),
            pltpu.SemaphoreType.DMA((2,)),
        ],
    )(keys, values, rates, segment_ids)

    def entering(state, first):
        incoming = from_before(state, 1)
        if hops > 1:
            decay = jnp.exp(jnp.sum(log_decay[0, :, first : first + side], axis=0))
            decay = decay.astype(jnp.bfloat16)
            total = incoming[:wide].reshape(side, DH, DH).astype(jnp.float32)
            through = jnp.ones((side,), jnp.float32)
            for by in range(2, hops + 1):
                through = through * from_before(decay, by - 1).astype(jnp.float32)
                far = from_before(state, by)
                same = jnp.where(far[wide, 0] == incoming[wide, 0], through, 0.0)
                far = far[:wide].reshape(side, DH, DH).astype(jnp.float32)
                total = total + same[:, None, None] * far
            total = total.reshape(wide, DH).astype(jnp.bfloat16)
            incoming = jnp.concatenate([total, incoming[wide:]], axis=0)
        return incoming

    inside, factor, docs, query, weight = call(
        inside_kernel,
        (
            pltpu.VMEM((rows, width), jnp.float32),
            pltpu.VMEM((rows, width), jnp.float32),
            pltpu.VMEM((rows, DH), jnp.float32),
            pltpu.VMEM((rows, width), jnp.bfloat16),
            pltpu.VMEM((width, columns), jnp.bfloat16),
        ),
        "inside",
        in_specs=[HBM] * 8,
        scratch_shapes=[
            pltpu.VMEM((rows, width), jnp.bfloat16),
            pltpu.VMEM((rows, width), jnp.bfloat16),
            pltpu.VMEM((rows, width), jnp.bfloat16),
            pltpu.VMEM((heads, rows), jnp.float32),
            pltpu.VMEM((1, rows), jnp.int32),
            pltpu.VMEM((1, width), jnp.float32),
            pltpu.SemaphoreType.DMA((8,)),
        ],
    )(queries, keys, values, gates, rates, segment_ids, norm_gain, out_weight)
    incoming = entering(state, 0)

    part = rows // 2
    normed = call(
        finish_kernel,
        (jax.ShapeDtypeStruct((part, width), jnp.bfloat16),) * 2,
        "finish",
    )(inside, factor, docs, query, incoming)

    if n_ctx != 4 or n_head != 4 or n_pipe != 2:
        normed = lax.all_gather(jnp.concatenate(normed, axis=0), "ctx", axis=0, tiled=True)
        blocks = jnp.dot(normed, weight, preferred_element_type=jnp.float32).astype(jnp.bfloat16)
        blocks = lax.all_to_all(blocks.reshape(n_ctx, rows, columns), "ctx", 0, 0, tiled=True)
        blocks = blocks.reshape(n_head, n_ctx // n_head, rows, columns)
        blocks = lax.all_to_all(blocks, "head", 0, 0, tiled=True)
        total = jnp.sum(blocks.astype(jnp.float32), axis=0).astype(jnp.bfloat16)
        total = jnp.swapaxes(total, 0, 1).reshape(1, rows, -1)
        return lax.ppermute(total, "pipe", [(s, (s + 1) % n_pipe) for s in range(n_pipe)])

    def moved(array, target):
        names = ("ctx", "head", "pipe")
        spots = [(i, j, s) for i in range(n_ctx) for j in range(n_head) for s in range(n_pipe)]
        place = {spot: at for at, spot in enumerate(spots)}
        return lax.ppermute(array, names, [(place[spot], place[target(*spot)]) for spot in spots])

    def swapped(array, by):
        return moved(array, lambda i, j, s: (i ^ by, j, s))

    single = jax.ShapeDtypeStruct((rows, columns // 2), jnp.bfloat16)

    def project(picked, other, after=()):
        shape = jax.ShapeDtypeStruct((len(picked), part, columns // 2), jnp.bfloat16)
        specs = [VMEM] * (len(picked) + 1) + [ANY] * len(after)
        kernel = functools.partial(project_kernel, other)
        return call(kernel, shape, "project", in_specs=specs)(*picked, weight, *after)

    def partner(send):
        return moved(send, lambda i, j, s: (i, j ^ 1, s))

    def merge(layout, sums, after=()):
        specs = [VMEM] * len(sums) + [ANY] * len(after)
        kernel = functools.partial(merge_kernel, layout)
        shapes = [jax.ShapeDtypeStruct((part * len(x), columns // 2), jnp.bfloat16) for x in layout]
        return call(kernel, tuple(shapes), "merge", in_specs=specs)(*sums, *after)

    upper, lower = normed
    upper_1, lower_2 = swapped(upper, 1), swapped(lower, 2)
    whole = (((0, 0), (0, 1)),)

    def hold(pair, after):
        shape = jax.ShapeDtypeStruct((part, width), jnp.bfloat16)
        specs = [VMEM] * 2 + [ANY] * len(after)
        return call(hold_kernel, (shape,) * 2, "hold", in_specs=specs)(*pair, *after)

    own_send = project((upper, lower), 1)
    own = merge(whole, (project((upper, lower), 0), partner(own_send)))
    lower_1, upper_2 = swapped(lower, 1), swapped(upper, 2)
    held = hold((upper_1, lower_2), (lower_1, upper_2, *own))
    beside = (upper_1, lower_1, upper_2, lower_2)
    beside_send, beside_keep = project(beside, 1, own), project(beside, 0)
    beside = merge(
        (((0, 0), (0, 1)), ((0, 2), (0, 3))),
        (beside_keep, partner(beside_send)),
    )
    across = (swapped(held[0], 2), swapped(held[1], 1))
    blocks = [*own, *(swapped(block, k + 1) for k, block in enumerate(beside))]
    sent, done = beside_keep, beside[0]
    for piece in across:
        send = project((piece,), 1, (sent,))
        (done,) = merge((((0, 0),),), (project((piece,), 0), partner(send)), (done,))
        blocks.append(swapped(done, 3))
        sent = send
    picked = call(pick_kernel, (single,) * n_head, "pick")(*blocks)
    arrived = [moved(picked[m], lambda i, j, s, m=m: (i, j ^ m, s)) for m in (3, 2, 1)]
    out = jax.ShapeDtypeStruct((1, rows, columns), jnp.bfloat16)
    out = call(last_kernel, out, "last")(*arrived, picked[0])
    return moved(out, lambda i, j, s: (i, j, 1 - s))


def solution(mesh):
    sizes = tuple(mesh.shape[axis] for axis in ("ctx", "head", "pipe"))
    return jax.shard_map(
        functools.partial(on_device, sizes),
        mesh=mesh,
        in_specs=(
            P("pipe", "ctx", "head"),
            P("pipe", "ctx", "head"),
            P("pipe", "ctx", "head"),
            P("pipe", "ctx", "head"),
            P("pipe", "ctx", "head"),
            P("pipe", "ctx"),
            P("pipe", "head"),
            P("pipe", "head", "ctx"),
        ),
        out_specs=P("pipe", "ctx", "head"),
        check_vma=False,
    )
```

```python
import functools
import math

import jax
import jax.numpy as jnp
from jax import lax
from jax.experimental import pallas as pl
from jax.experimental.pallas import tpu as pltpu
from jax.sharding import PartitionSpec as P

DH = 128
EXTRA = 16
VMEM = pl.BlockSpec(memory_space=pltpu.VMEM)
ANY = pl.BlockSpec(memory_space=pl.ANY)
HBM = pl.BlockSpec(memory_space=pltpu.HBM)


def dot(a, b, contract=((1,), (0,)), precision=None):
    return lax.dot_general(
        a, b, (contract, ((), ())), preferred_element_type=jnp.float32, precision=precision
    )


def running_sums(rate):
    rows = rate.shape[1]
    upper = (
        lax.broadcasted_iota(jnp.int32, (rows, rows), 0)
        <= lax.broadcasted_iota(jnp.int32, (rows, rows), 1)
    ).astype(jnp.float32)
    across = dot(rate, upper, precision=lax.Precision.HIGHEST)
    columns = dot(upper, rate, ((0,), (1,)), precision=lax.Precision.HIGHEST)
    return columns, across


def own_fading(doc, across, key_ref, value_ref, first, out_ref):
    rows = doc.shape[1]
    wide = out_ref.shape[0] - EXTRA
    last_doc = doc[:, rows - 1 :]
    fading = jnp.where(doc == last_doc, jnp.exp(across[:, rows - 1 :] - across), 0.0)
    fading_columns = fading.T
    out_ref[wide:, :] = jnp.broadcast_to(
        (last_doc + 1).astype(jnp.float32), (EXTRA, DH)
    ).astype(jnp.bfloat16)
    for k in range(wide // DH):
        h = first + k
        span = slice(h * DH, (h + 1) * DH)
        faded = (key_ref[:, span].astype(jnp.float32) * fading_columns[:, h : h + 1]).astype(
            jnp.bfloat16
        )
        out_ref[k * DH : (k + 1) * DH, :] = dot(faded, value_ref[:, span], ((0,), (0,))).astype(
            jnp.bfloat16
        )


def state_kernel(
    key_hbm,
    value_hbm,
    rate_hbm,
    doc_hbm,
    *refs,
):
    out_ref, key_ref, value_ref, rate_ref, doc_ref, sems, small = refs[-7:]
    rows = rate_ref.shape[1]
    wide = key_ref.shape[1]
    parts = sems.shape[0]
    piece = wide // parts
    copies = [
        pltpu.make_async_copy(rate_hbm.at[0], rate_ref, small.at[0]),
        pltpu.make_async_copy(doc_hbm, doc_ref, small.at[1]),
    ]
    pieces = []
    for part in range(parts):
        span = pl.ds(part * piece, piece)
        pieces.append(
            [
                pltpu.make_async_copy(
                    key_hbm.at[0, :, span], key_ref.at[:, span], sems.at[part, 0]
                ),
                pltpu.make_async_copy(
                    value_hbm.at[0, :, span], value_ref.at[:, span], sems.at[part, 1]
                ),
            ]
        )
    for copy in copies + sum(pieces, []):
        copy.start()
    for copy in copies:
        copy.wait()
    columns, across = running_sums(rate_ref[...])
    for part in range(parts):
        for copy in pieces[part]:
            copy.wait()
    own_fading(doc_ref[...], across, key_ref, value_ref, 0, out_ref)


def inside_kernel(
    query_hbm,
    key_hbm,
    value_hbm,
    gate_hbm,
    rate_hbm,
    doc_hbm,
    gain_hbm,
    weight_hbm,
    out_ref,
    factor_ref,
    doc_out_ref,
    query_ref,
    weight_ref,
    key_ref,
    value_ref,
    gate_ref,
    rate_ref,
    doc_ref,
    gain_ref,
    sems,
):
    sources = [rate_hbm.at[0], doc_hbm, gain_hbm, query_hbm.at[0], key_hbm.at[0], value_hbm.at[0]]
    sources += [gate_hbm.at[0], weight_hbm.at[0]]
    targets = [rate_ref, doc_ref, gain_ref, query_ref, key_ref, value_ref, gate_ref, weight_ref]
    copies = [
        pltpu.make_async_copy(source, target, sems.at[i])
        for i, (source, target) in enumerate(zip(sources, targets))
    ]
    for copy in copies:
        copy.start()
    for copy in copies[:3]:
        copy.wait()
    heads, rows = rate_ref.shape
    columns, across = running_sums(rate_ref[...])
    reach = jnp.exp(columns)
    doc_across = jnp.broadcast_to(doc_ref[...].astype(jnp.float32) + 1.0, (rows, rows))
    doc_out_ref[...] = doc_across.T
    allowed = (
        lax.broadcasted_iota(jnp.int32, (rows, rows), 0)
        >= lax.broadcasted_iota(jnp.int32, (rows, rows), 1)
    ) & (doc_across == doc_across.T)
    for copy in copies[3:6]:
        copy.wait()
    for h in range(heads):
        span = slice(h * DH, (h + 1) * DH)
        gaps = columns[:, h : h + 1] - across[h : h + 1, :]
        weights = jnp.where(allowed, jnp.exp(jnp.where(allowed, gaps, 0.0)), 0.0)
        scores = dot(query_ref[:, span], key_ref[:, span], ((1,), (1,)))
        mixed = (scores * weights).astype(jnp.bfloat16)
        out_ref[:, span] = dot(mixed, value_ref[:, span])
        reached = query_ref[:, span].astype(jnp.float32) * reach[:, h : h + 1]
        query_ref[:, span] = reached.astype(jnp.bfloat16)
    copies[6].wait()
    for h in range(heads):
        span = slice(h * DH, (h + 1) * DH)
        gate = jax.nn.sigmoid(gate_ref[:, span].astype(jnp.float32))
        factor_ref[:, span] = gain_ref[:, span] * gate
    copies[7].wait()


def finish_kernel(inside_ref, factor_ref, doc_ref, query_ref, state_ref, *out_refs):
    width = inside_ref.shape[1]
    part = out_refs[0].shape[0]
    incoming = state_ref[width:, :].astype(jnp.float32)[0:1, :]
    reached = (doc_ref[...] == incoming).astype(jnp.float32)
    average = jnp.full((DH, DH), 1.0 / DH, jnp.bfloat16)
    for start in range(0, width, DH):
        span = slice(start, start + DH)
        attended = inside_ref[:, span] + reached * dot(query_ref[:, span], state_ref[span, :])
        mean = dot((attended * attended).astype(jnp.bfloat16), average)
        scaling = lax.rsqrt(mean + 1e-06) * factor_ref[:, span]
        normed = (attended * scaling).astype(jnp.bfloat16)
        for i, out_ref in enumerate(out_refs):
            out_ref[:, span] = normed[i * part : (i + 1) * part]


def project_kernel(other, *refs):
    out_ref = refs[-1]
    blocks, rows, columns = out_ref.shape
    pieces, weight_ref = refs[:blocks], refs[blocks]
    half = (lax.axis_index("head") & 1) ^ other
    wide = math.gcd(columns, 256)
    everything = jnp.concatenate([piece[...] for piece in pieces], axis=0)
    for start in range(0, columns, wide):
        span = pl.ds(pl.multiple_of(half * columns + start, wide), wide)
        result = dot(everything, weight_ref[:, span]).astype(jnp.bfloat16)
        for j in range(blocks):
            out_ref[j, :, start : start + wide] = result[j * rows : (j + 1) * rows]


def hold_kernel(upper_ref, lower_ref, *refs):
    for source_ref, out_ref in zip((upper_ref, lower_ref), refs[-2:]):
        out_ref[...] = source_ref[...]


def merge_kernel(layout, *refs):
    out_refs = refs[-len(layout) :]
    rows = refs[0].shape[1]
    for out_ref, places in zip(out_refs, layout):
        for i, (source, block) in enumerate(places):
            keep_ref, arrived_ref = refs[2 * source], refs[2 * source + 1]
            total = keep_ref[block].astype(jnp.float32) + arrived_ref[block].astype(jnp.float32)
            out_ref[i * rows : (i + 1) * rows, :] = total.astype(jnp.bfloat16)


def pick_kernel(*refs):
    count = lax.axis_size("head")
    block_refs, out_refs = refs[: -count], refs[-count:]
    at = lax.axis_index("ctx") ^ lax.axis_index("head")
    for m, out_ref in enumerate(out_refs):
        for j in range(count):

            @pl.when((at ^ m) == j)
            def _(out_ref=out_ref, j=j):
                if j < count - 1:
                    out_ref[...] = block_refs[j][...]
                else:
                    out_ref[...] = jnp.concatenate([ref[...] for ref in block_refs[j:]], axis=0)


def last_kernel(*refs):
    out_ref = refs[-1]
    wide = refs[0].shape[1]
    for m in range(2):
        total = refs[m][...].astype(jnp.float32) + refs[m + 2][...].astype(jnp.float32)
        half = (lax.axis_index("head") & 1) ^ 1 ^ m
        out_ref[0, :, pl.ds(pl.multiple_of(half * wide, wide), wide)] = total.astype(jnp.bfloat16)


def call(kernel, out_shape, name, limit=24, **more):
    return pl.pallas_call(
        kernel,
        out_shape=out_shape,
        compiler_params=pltpu.CompilerParams(vmem_limit_bytes=limit * 2**20),
        cost_estimate=pl.CostEstimate(flops=1, bytes_accessed=1, transcendentals=0),
        name=name,
        **more,
    )


def on_device(sizes, queries, keys, values, gates, log_decay, segment_ids, norm_gain, out_weight):
    n_ctx, n_head, n_pipe = sizes
    rows, width = queries.shape[1:]
    heads = width // DH
    tokens = rows * n_ctx
    hops = min(n_ctx - 1, -(-(tokens // 4 - 1) // rows))

    def stay(array):
        return pltpu.with_memory_space_constraint(array, pltpu.HBM)

    rates = stay(jnp.swapaxes(log_decay, 1, 2))
    queries, keys, values, gates = map(stay, (queries, keys, values, gates))
    segment_ids, norm_gain, out_weight = map(stay, (segment_ids, norm_gain, out_weight))
    columns = out_weight.shape[2]
    side = heads
    wide = width

    def from_before(array, by):
        return lax.ppermute(array, "ctx", [(i, i + by) for i in range(n_ctx - by)])

    parts = 4 if side % 4 == 0 else 1
    state_shape = jax.ShapeDtypeStruct((wide + EXTRA, DH), jnp.bfloat16)
    state = call(
        state_kernel,
        state_shape,
        "shard_state",
        in_specs=[HBM] * 4,
        scratch_shapes=[
            pltpu.VMEM((rows, wide), jnp.bfloat16),
            pltpu.VMEM((rows, wide), jnp.bfloat16),
            pltpu.VMEM((heads, rows), jnp.float32),
            pltpu.VMEM((1, rows), jnp.int32),
            pltpu.SemaphoreType.DMA((parts, 2)),
            pltpu.SemaphoreType.DMA((2,)),
        ],
    )(keys, values, rates, segment_ids)

    def entering(state, first):
        incoming = from_before(state, 1)
        if hops > 1:
            decay = jnp.exp(jnp.sum(log_decay[0, :, first : first + side], axis=0))
            decay = decay.astype(jnp.bfloat16)
            total = incoming[:wide].reshape(side, DH, DH).astype(jnp.float32)
            through = jnp.ones((side,), jnp.float32)
            for by in range(2, hops + 1):
                through = through * from_before(decay, by - 1).astype(jnp.float32)
                far = from_before(state, by)
                same = jnp.where(far[wide, 0] == incoming[wide, 0], through, 0.0)
                far = far[:wide].reshape(side, DH, DH).astype(jnp.float32)
                total = total + same[:, None, None] * far
            total = total.reshape(wide, DH).astype(jnp.bfloat16)
            incoming = jnp.concatenate([total, incoming[wide:]], axis=0)
        return incoming

    inside, factor, docs, query, weight = call(
        inside_kernel,
        (
            pltpu.VMEM((rows, width), jnp.float32),
            pltpu.VMEM((rows, width), jnp.float32),
            pltpu.VMEM((rows, DH), jnp.float32),
            pltpu.VMEM((rows, width), jnp.bfloat16),
            pltpu.VMEM((width, columns), jnp.bfloat16),
        ),
        "inside",
        in_specs=[HBM] * 8,
        scratch_shapes=[
            pltpu.VMEM((rows, width), jnp.bfloat16),
            pltpu.VMEM((rows, width), jnp.bfloat16),
            pltpu.VMEM((rows, width), jnp.bfloat16),
            pltpu.VMEM((heads, rows), jnp.float32),
            pltpu.VMEM((1, rows), jnp.int32),
            pltpu.VMEM((1, width), jnp.float32),
            pltpu.SemaphoreType.DMA((8,)),
        ],
    )(queries, keys, values, gates, rates, segment_ids, norm_gain, out_weight)
    incoming = entering(state, 0)

    part = rows // 2
    normed = call(
        finish_kernel,
        (jax.ShapeDtypeStruct((part, width), jnp.bfloat16),) * 2,
        "finish",
    )(inside, factor, docs, query, incoming)

    if n_ctx != 4 or n_head != 4 or n_pipe != 2:
        normed = lax.all_gather(jnp.concatenate(normed, axis=0), "ctx", axis=0, tiled=True)
        blocks = jnp.dot(normed, weight, preferred_element_type=jnp.float32).astype(jnp.bfloat16)
        blocks = lax.all_to_all(blocks.reshape(n_ctx, rows, columns), "ctx", 0, 0, tiled=True)
        blocks = blocks.reshape(n_head, n_ctx // n_head, rows, columns)
        blocks = lax.all_to_all(blocks, "head", 0, 0, tiled=True)
        total = jnp.sum(blocks.astype(jnp.float32), axis=0).astype(jnp.bfloat16)
        total = jnp.swapaxes(total, 0, 1).reshape(1, rows, -1)
        return lax.ppermute(total, "pipe", [(s, (s + 1) % n_pipe) for s in range(n_pipe)])

    def moved(array, target):
        names = ("ctx", "head", "pipe")
        spots = [(i, j, s) for i in range(n_ctx) for j in range(n_head) for s in range(n_pipe)]
        place = {spot: at for at, spot in enumerate(spots)}
        return lax.ppermute(array, names, [(place[spot], place[target(*spot)]) for spot in spots])

    def swapped(array, by):
        return moved(array, lambda i, j, s: (i ^ by, j, s))

    single = jax.ShapeDtypeStruct((rows, columns // 2), jnp.bfloat16)

    def project(picked, other, after=()):
        shape = jax.ShapeDtypeStruct((len(picked), part, columns // 2), jnp.bfloat16)
        specs = [VMEM] * (len(picked) + 1) + [ANY] * len(after)
        kernel = functools.partial(project_kernel, other)
        return call(kernel, shape, "project", in_specs=specs)(*picked, weight, *after)

    def partner(send):
        return moved(send, lambda i, j, s: (i, j ^ 1, s))

    def merge(layout, sums, after=()):
        specs = [VMEM] * len(sums) + [ANY] * len(after)
        kernel = functools.partial(merge_kernel, layout)
        shapes = [jax.ShapeDtypeStruct((part * len(x), columns // 2), jnp.bfloat16) for x in layout]
        return call(kernel, tuple(shapes), "merge", in_specs=specs)(*sums, *after)

    upper, lower = normed
    upper_1, lower_2 = swapped(upper, 1), swapped(lower, 2)
    whole = (((0, 0), (0, 1)),)

    def hold(pair, after):
        shape = jax.ShapeDtypeStruct((part, width), jnp.bfloat16)
        specs = [VMEM] * 2 + [ANY] * len(after)
        return call(hold_kernel, (shape,) * 2, "hold", in_specs=specs)(*pair, *after)

    own_send = project((upper, lower), 1)
    own = merge(whole, (project((upper, lower), 0), partner(own_send)))
    lower_1, upper_2 = swapped(lower, 1), swapped(upper, 2)
    held = hold((upper_1, lower_2), (lower_1, upper_2, *own))
    beside = (upper_1, lower_1, upper_2, lower_2)
    beside_send, beside_keep = project(beside, 1, own), project(beside, 0)
    beside = merge(
        (((0, 0), (0, 1)), ((0, 2), (0, 3))),
        (beside_keep, partner(beside_send)),
    )
    across = (swapped(held[0], 2), swapped(held[1], 1))
    across_sum = (project(across, 0), partner(project(across, 1, (beside_keep,))))
    across = merge(whole, across_sum, beside[:1])
    blocks = [swapped(block, k) if k else block for k, block in enumerate((*own, *beside, *across))]
    picked = call(pick_kernel, (single,) * n_head, "pick")(*blocks)
    arrived = [moved(picked[m], lambda i, j, s, m=m: (i, j ^ m, s)) for m in (3, 2, 1)]
    out = jax.ShapeDtypeStruct((1, rows, columns), jnp.bfloat16)
    out = call(last_kernel, out, "last")(*arrived, picked[0])
    return moved(out, lambda i, j, s: (i, j, 1 - s))


def solution(mesh):
    sizes = tuple(mesh.shape[axis] for axis in ("ctx", "head", "pipe"))
    return jax.shard_map(
        functools.partial(on_device, sizes),
        mesh=mesh,
        in_specs=(
            P("pipe", "ctx", "head"),
            P("pipe", "ctx", "head"),
            P("pipe", "ctx", "head"),
            P("pipe", "ctx", "head"),
            P("pipe", "ctx", "head"),
            P("pipe", "ctx"),
            P("pipe", "head"),
            P("pipe", "head", "ctx"),
        ),
        out_specs=P("pipe", "ctx", "head"),
        check_vma=False,
    )
```

```python
import functools
import math

import jax
import jax.numpy as jnp
from jax import lax
from jax.experimental import pallas as pl
from jax.experimental.pallas import tpu as pltpu
from jax.sharding import PartitionSpec as P

DH = 128
EXTRA = 16
VMEM = pl.BlockSpec(memory_space=pltpu.VMEM)
ANY = pl.BlockSpec(memory_space=pl.ANY)
HBM = pl.BlockSpec(memory_space=pltpu.HBM)


def dot(a, b, contract=((1,), (0,)), precision=None):
    return lax.dot_general(
        a, b, (contract, ((), ())), preferred_element_type=jnp.float32, precision=precision
    )


def running_sums(rate):
    rows = rate.shape[1]
    upper = (
        lax.broadcasted_iota(jnp.int32, (rows, rows), 0)
        <= lax.broadcasted_iota(jnp.int32, (rows, rows), 1)
    ).astype(jnp.float32)
    across = dot(rate, upper, precision=lax.Precision.HIGHEST)
    columns = dot(upper, rate, ((0,), (1,)), precision=lax.Precision.HIGHEST)
    return columns, across


def own_fading(doc, across, key_ref, value_ref, first, out_ref):
    rows = doc.shape[1]
    wide = out_ref.shape[0] - EXTRA
    last_doc = doc[:, rows - 1 :]
    fading = jnp.where(doc == last_doc, jnp.exp(across[:, rows - 1 :] - across), 0.0)
    fading_columns = fading.T
    out_ref[wide:, :] = jnp.broadcast_to(
        (last_doc + 1).astype(jnp.float32), (EXTRA, DH)
    ).astype(jnp.bfloat16)
    for k in range(wide // DH):
        h = first + k
        span = slice(h * DH, (h + 1) * DH)
        faded = (key_ref[:, span].astype(jnp.float32) * fading_columns[:, h : h + 1]).astype(
            jnp.bfloat16
        )
        out_ref[k * DH : (k + 1) * DH, :] = dot(faded, value_ref[:, span], ((0,), (0,))).astype(
            jnp.bfloat16
        )


def state_work(
    key_hbm,
    value_hbm,
    rate_hbm,
    doc_hbm,
    *refs,
):
    out_ref, key_ref, value_ref, rate_ref, doc_ref, sems, small = refs[-7:]
    rows = rate_ref.shape[1]
    wide = key_ref.shape[1]
    parts = sems.shape[0]
    piece = wide // parts
    copies = [
        pltpu.make_async_copy(rate_hbm.at[0], rate_ref, small.at[0]),
        pltpu.make_async_copy(doc_hbm, doc_ref, small.at[1]),
    ]
    pieces = []
    for part in range(parts):
        span = pl.ds(part * piece, piece)
        pieces.append(
            [
                pltpu.make_async_copy(
                    key_hbm.at[0, :, span], key_ref.at[:, span], sems.at[part, 0]
                ),
                pltpu.make_async_copy(
                    value_hbm.at[0, :, span], value_ref.at[:, span], sems.at[part, 1]
                ),
            ]
        )
    for copy in copies + sum(pieces, []):
        copy.start()
    for copy in copies:
        copy.wait()
    columns, across = running_sums(rate_ref[...])
    for part in range(parts):
        for copy in pieces[part]:
            copy.wait()
    own_fading(doc_ref[...], across, key_ref, value_ref, 0, out_ref)


def state_kernel(*refs):
    @pl.when(lax.axis_index("ctx") < lax.axis_size("ctx") - 1)
    def _():
        state_work(*refs)


def inside_kernel(
    query_hbm,
    key_hbm,
    value_hbm,
    gate_hbm,
    rate_hbm,
    doc_hbm,
    gain_hbm,
    weight_hbm,
    out_ref,
    factor_ref,
    doc_out_ref,
    query_ref,
    weight_ref,
    key_ref,
    value_ref,
    gate_ref,
    rate_ref,
    doc_ref,
    gain_ref,
    sems,
):
    sources = [rate_hbm.at[0], doc_hbm, gain_hbm, query_hbm.at[0], key_hbm.at[0], value_hbm.at[0]]
    sources += [gate_hbm.at[0], weight_hbm.at[0]]
    targets = [rate_ref, doc_ref, gain_ref, query_ref, key_ref, value_ref, gate_ref, weight_ref]
    copies = [
        pltpu.make_async_copy(source, target, sems.at[i])
        for i, (source, target) in enumerate(zip(sources, targets))
    ]
    for copy in copies:
        copy.start()
    for copy in copies[:3]:
        copy.wait()
    heads, rows = rate_ref.shape
    columns, across = running_sums(rate_ref[...])
    reach = jnp.exp(columns)
    doc_across = jnp.broadcast_to(doc_ref[...].astype(jnp.float32) + 1.0, (rows, rows))
    doc_out_ref[...] = doc_across.T
    allowed = (
        lax.broadcasted_iota(jnp.int32, (rows, rows), 0)
        >= lax.broadcasted_iota(jnp.int32, (rows, rows), 1)
    ) & (doc_across == doc_across.T)
    for copy in copies[3:6]:
        copy.wait()
    for h in range(heads):
        span = slice(h * DH, (h + 1) * DH)
        gaps = columns[:, h : h + 1] - across[h : h + 1, :]
        weights = jnp.where(allowed, jnp.exp(jnp.where(allowed, gaps, 0.0)), 0.0)
        scores = dot(query_ref[:, span], key_ref[:, span], ((1,), (1,)))
        mixed = (scores * weights).astype(jnp.bfloat16)
        out_ref[:, span] = dot(mixed, value_ref[:, span])
        reached = query_ref[:, span].astype(jnp.float32) * reach[:, h : h + 1]
        query_ref[:, span] = reached.astype(jnp.bfloat16)
    copies[6].wait()
    for h in range(heads):
        span = slice(h * DH, (h + 1) * DH)
        gate = jax.nn.sigmoid(gate_ref[:, span].astype(jnp.float32))
        factor_ref[:, span] = gain_ref[:, span] * gate
    copies[7].wait()


def finish_kernel(inside_ref, factor_ref, doc_ref, query_ref, state_ref, *out_refs):
    width = inside_ref.shape[1]
    part = out_refs[0].shape[0]
    incoming = state_ref[width:, :].astype(jnp.float32)[0:1, :]
    reached = (doc_ref[...] == incoming).astype(jnp.float32)
    average = jnp.full((DH, DH), 1.0 / DH, jnp.bfloat16)
    for start in range(0, width, DH):
        span = slice(start, start + DH)
        attended = inside_ref[:, span] + reached * dot(query_ref[:, span], state_ref[span, :])
        mean = dot((attended * attended).astype(jnp.bfloat16), average)
        scaling = lax.rsqrt(mean + 1e-06) * factor_ref[:, span]
        normed = (attended * scaling).astype(jnp.bfloat16)
        for i, out_ref in enumerate(out_refs):
            out_ref[:, span] = normed[i * part : (i + 1) * part]


def project_kernel(other, *refs):
    out_ref = refs[-1]
    blocks, rows, columns = out_ref.shape
    pieces, weight_ref = refs[:blocks], refs[blocks]
    half = (lax.axis_index("head") & 1) ^ other
    wide = math.gcd(columns, 256)
    everything = jnp.concatenate([piece[...] for piece in pieces], axis=0)
    for start in range(0, columns, wide):
        span = pl.ds(pl.multiple_of(half * columns + start, wide), wide)
        result = dot(everything, weight_ref[:, span]).astype(jnp.bfloat16)
        for j in range(blocks):
            out_ref[j, :, start : start + wide] = result[j * rows : (j + 1) * rows]


def hold_kernel(upper_ref, lower_ref, *refs):
    for source_ref, out_ref in zip((upper_ref, lower_ref), refs[-2:]):
        out_ref[...] = source_ref[...]


def merge_kernel(layout, *refs):
    out_refs = refs[-len(layout) :]
    rows = refs[0].shape[1]
    for out_ref, places in zip(out_refs, layout):
        for i, (source, block) in enumerate(places):
            keep_ref, arrived_ref = refs[2 * source], refs[2 * source + 1]
            total = keep_ref[block].astype(jnp.float32) + arrived_ref[block].astype(jnp.float32)
            out_ref[i * rows : (i + 1) * rows, :] = total.astype(jnp.bfloat16)


def pick_kernel(*refs):
    count = lax.axis_size("head")
    block_refs, out_refs = refs[: -count], refs[-count:]
    at = lax.axis_index("ctx") ^ lax.axis_index("head")
    for m, out_ref in enumerate(out_refs):
        for j in range(count):

            @pl.when((at ^ m) == j)
            def _(out_ref=out_ref, j=j):
                if j < count - 1:
                    out_ref[...] = block_refs[j][...]
                else:
                    out_ref[...] = jnp.concatenate([ref[...] for ref in block_refs[j:]], axis=0)


def last_kernel(*refs):
    out_ref = refs[-1]
    wide = refs[0].shape[1]
    for m in range(2):
        total = refs[m][...].astype(jnp.float32) + refs[m + 2][...].astype(jnp.float32)
        half = (lax.axis_index("head") & 1) ^ 1 ^ m
        out_ref[0, :, pl.ds(pl.multiple_of(half * wide, wide), wide)] = total.astype(jnp.bfloat16)


def call(kernel, out_shape, name, limit=24, **more):
    return pl.pallas_call(
        kernel,
        out_shape=out_shape,
        compiler_params=pltpu.CompilerParams(vmem_limit_bytes=limit * 2**20),
        cost_estimate=pl.CostEstimate(flops=1, bytes_accessed=1, transcendentals=0),
        name=name,
        **more,
    )


def on_device(sizes, queries, keys, values, gates, log_decay, segment_ids, norm_gain, out_weight):
    n_ctx, n_head, n_pipe = sizes
    rows, width = queries.shape[1:]
    heads = width // DH
    tokens = rows * n_ctx
    hops = min(n_ctx - 1, -(-(tokens // 4 - 1) // rows))

    def stay(array):
        return pltpu.with_memory_space_constraint(array, pltpu.HBM)

    rates = stay(jnp.swapaxes(log_decay, 1, 2))
    queries, keys, values, gates = map(stay, (queries, keys, values, gates))
    segment_ids, norm_gain, out_weight = map(stay, (segment_ids, norm_gain, out_weight))
    columns = out_weight.shape[2]
    side = heads
    wide = width

    def from_before(array, by):
        return lax.ppermute(array, "ctx", [(i, i + by) for i in range(n_ctx - by)])

    parts = 4 if side % 4 == 0 else 1
    state_shape = jax.ShapeDtypeStruct((wide + EXTRA, DH), jnp.bfloat16)
    state = call(
        state_kernel,
        state_shape,
        "shard_state",
        in_specs=[HBM] * 4,
        scratch_shapes=[
            pltpu.VMEM((rows, wide), jnp.bfloat16),
            pltpu.VMEM((rows, wide), jnp.bfloat16),
            pltpu.VMEM((heads, rows), jnp.float32),
            pltpu.VMEM((1, rows), jnp.int32),
            pltpu.SemaphoreType.DMA((parts, 2)),
            pltpu.SemaphoreType.DMA((2,)),
        ],
    )(keys, values, rates, segment_ids)

    def entering(state, first):
        incoming = from_before(state, 1)
        if hops > 1:
            decay = jnp.exp(jnp.sum(log_decay[0, :, first : first + side], axis=0))
            decay = decay.astype(jnp.bfloat16)
            total = incoming[:wide].reshape(side, DH, DH).astype(jnp.float32)
            through = jnp.ones((side,), jnp.float32)
            for by in range(2, hops + 1):
                through = through * from_before(decay, by - 1).astype(jnp.float32)
                far = from_before(state, by)
                same = jnp.where(far[wide, 0] == incoming[wide, 0], through, 0.0)
                far = far[:wide].reshape(side, DH, DH).astype(jnp.float32)
                total = total + same[:, None, None] * far
            total = total.reshape(wide, DH).astype(jnp.bfloat16)
            incoming = jnp.concatenate([total, incoming[wide:]], axis=0)
        return incoming

    inside, factor, docs, query, weight = call(
        inside_kernel,
        (
            pltpu.VMEM((rows, width), jnp.float32),
            pltpu.VMEM((rows, width), jnp.float32),
            pltpu.VMEM((rows, DH), jnp.float32),
            pltpu.VMEM((rows, width), jnp.bfloat16),
            pltpu.VMEM((width, columns), jnp.bfloat16),
        ),
        "inside",
        in_specs=[HBM] * 8,
        scratch_shapes=[
            pltpu.VMEM((rows, width), jnp.bfloat16),
            pltpu.VMEM((rows, width), jnp.bfloat16),
            pltpu.VMEM((rows, width), jnp.bfloat16),
            pltpu.VMEM((heads, rows), jnp.float32),
            pltpu.VMEM((1, rows), jnp.int32),
            pltpu.VMEM((1, width), jnp.float32),
            pltpu.SemaphoreType.DMA((8,)),
        ],
    )(queries, keys, values, gates, rates, segment_ids, norm_gain, out_weight)
    incoming = entering(state, 0)

    part = rows // 2
    normed = call(
        finish_kernel,
        (jax.ShapeDtypeStruct((part, width), jnp.bfloat16),) * 2,
        "finish",
    )(inside, factor, docs, query, incoming)

    if n_ctx != 4 or n_head != 4 or n_pipe != 2:
        normed = lax.all_gather(jnp.concatenate(normed, axis=0), "ctx", axis=0, tiled=True)
        blocks = jnp.dot(normed, weight, preferred_element_type=jnp.float32).astype(jnp.bfloat16)
        blocks = lax.all_to_all(blocks.reshape(n_ctx, rows, columns), "ctx", 0, 0, tiled=True)
        blocks = blocks.reshape(n_head, n_ctx // n_head, rows, columns)
        blocks = lax.all_to_all(blocks, "head", 0, 0, tiled=True)
        total = jnp.sum(blocks.astype(jnp.float32), axis=0).astype(jnp.bfloat16)
        total = jnp.swapaxes(total, 0, 1).reshape(1, rows, -1)
        return lax.ppermute(total, "pipe", [(s, (s + 1) % n_pipe) for s in range(n_pipe)])

    def moved(array, target):
        names = ("ctx", "head", "pipe")
        spots = [(i, j, s) for i in range(n_ctx) for j in range(n_head) for s in range(n_pipe)]
        place = {spot: at for at, spot in enumerate(spots)}
        return lax.ppermute(array, names, [(place[spot], place[target(*spot)]) for spot in spots])

    def swapped(array, by):
        return moved(array, lambda i, j, s: (i ^ by, j, s))

    single = jax.ShapeDtypeStruct((rows, columns // 2), jnp.bfloat16)

    def project(picked, other, after=()):
        shape = jax.ShapeDtypeStruct((len(picked), part, columns // 2), jnp.bfloat16)
        specs = [VMEM] * (len(picked) + 1) + [ANY] * len(after)
        kernel = functools.partial(project_kernel, other)
        return call(kernel, shape, "project", in_specs=specs)(*picked, weight, *after)

    def partner(send):
        return moved(send, lambda i, j, s: (i, j ^ 1, s))

    def merge(layout, sums, after=()):
        specs = [VMEM] * len(sums) + [ANY] * len(after)
        kernel = functools.partial(merge_kernel, layout)
        shapes = [jax.ShapeDtypeStruct((part * len(x), columns // 2), jnp.bfloat16) for x in layout]
        return call(kernel, tuple(shapes), "merge", in_specs=specs)(*sums, *after)

    upper, lower = normed
    upper_1, lower_2 = swapped(upper, 1), swapped(lower, 2)
    whole = (((0, 0), (0, 1)),)

    def hold(pair, after):
        shape = jax.ShapeDtypeStruct((part, width), jnp.bfloat16)
        specs = [VMEM] * 2 + [ANY] * len(after)
        return call(hold_kernel, (shape,) * 2, "hold", in_specs=specs)(*pair, *after)

    own_send = project((upper, lower), 1)
    own = merge(whole, (project((upper, lower), 0), partner(own_send)))
    lower_1, upper_2 = swapped(lower, 1), swapped(upper, 2)
    held = hold((upper_1, lower_2), (lower_1, upper_2, *own))
    beside = (upper_1, lower_1, upper_2, lower_2)
    beside_send, beside_keep = project(beside, 1, own), project(beside, 0)
    beside = merge(
        (((0, 0), (0, 1)), ((0, 2), (0, 3))),
        (beside_keep, partner(beside_send)),
    )
    across = (swapped(held[0], 2), swapped(held[1], 1))
    across_sum = (project(across, 0), partner(project(across, 1, (beside_keep,))))
    across = merge(whole, across_sum, beside[:1])
    blocks = [swapped(block, k) if k else block for k, block in enumerate((*own, *beside, *across))]
    picked = call(pick_kernel, (single,) * n_head, "pick")(*blocks)
    arrived = [moved(picked[m], lambda i, j, s, m=m: (i, j ^ m, s)) for m in (3, 2, 1)]
    out = jax.ShapeDtypeStruct((1, rows, columns), jnp.bfloat16)
    out = call(last_kernel, out, "last")(*arrived, picked[0])
    return moved(out, lambda i, j, s: (i, j, 1 - s))


def solution(mesh):
    sizes = tuple(mesh.shape[axis] for axis in ("ctx", "head", "pipe"))
    return jax.shard_map(
        functools.partial(on_device, sizes),
        mesh=mesh,
        in_specs=(
            P("pipe", "ctx", "head"),
            P("pipe", "ctx", "head"),
            P("pipe", "ctx", "head"),
            P("pipe", "ctx", "head"),
            P("pipe", "ctx", "head"),
            P("pipe", "ctx"),
            P("pipe", "head"),
            P("pipe", "head", "ctx"),
        ),
        out_specs=P("pipe", "ctx", "head"),
        check_vma=False,
    )
```

```python
import functools
import math

import jax
import jax.numpy as jnp
from jax import lax
from jax.experimental import pallas as pl
from jax.experimental.pallas import tpu as pltpu
from jax.sharding import PartitionSpec as P

DH = 128
EXTRA = 16
VMEM = pl.BlockSpec(memory_space=pltpu.VMEM)
ANY = pl.BlockSpec(memory_space=pl.ANY)
HBM = pl.BlockSpec(memory_space=pltpu.HBM)


def dot(a, b, contract=((1,), (0,)), precision=None):
    return lax.dot_general(
        a, b, (contract, ((), ())), preferred_element_type=jnp.float32, precision=precision
    )


def running_sums(rate):
    rows = rate.shape[1]
    upper = (
        lax.broadcasted_iota(jnp.int32, (rows, rows), 0)
        <= lax.broadcasted_iota(jnp.int32, (rows, rows), 1)
    ).astype(jnp.float32)
    across = dot(rate, upper, precision=lax.Precision.HIGHEST)
    columns = dot(upper, rate, ((0,), (1,)), precision=lax.Precision.HIGHEST)
    return columns, across


def own_fading(doc, across, key_ref, value_ref, first, out_ref):
    rows = doc.shape[1]
    wide = out_ref.shape[0] - EXTRA
    last_doc = doc[:, rows - 1 :]
    fading = jnp.where(doc == last_doc, jnp.exp(across[:, rows - 1 :] - across), 0.0)
    fading_columns = fading.T
    out_ref[wide:, :] = jnp.broadcast_to(
        (last_doc + 1).astype(jnp.float32), (EXTRA, DH)
    ).astype(jnp.bfloat16)
    for k in range(wide // DH):
        h = first + k
        span = slice(h * DH, (h + 1) * DH)
        faded = (key_ref[:, span].astype(jnp.float32) * fading_columns[:, h : h + 1]).astype(
            jnp.bfloat16
        )
        out_ref[k * DH : (k + 1) * DH, :] = dot(faded, value_ref[:, span], ((0,), (0,))).astype(
            jnp.bfloat16
        )


def state_work(
    key_hbm,
    value_hbm,
    rate_hbm,
    doc_hbm,
    *refs,
):
    out_ref, key_ref, value_ref, rate_ref, doc_ref, sems, small = refs[-7:]
    rows = rate_ref.shape[1]
    wide = key_ref.shape[1]
    parts = sems.shape[0]
    piece = wide // parts
    copies = [
        pltpu.make_async_copy(rate_hbm.at[0], rate_ref, small.at[0]),
        pltpu.make_async_copy(doc_hbm, doc_ref, small.at[1]),
    ]
    pieces = []
    for part in range(parts):
        span = pl.ds(part * piece, piece)
        pieces.append(
            [
                pltpu.make_async_copy(
                    key_hbm.at[0, :, span], key_ref.at[:, span], sems.at[part, 0]
                ),
                pltpu.make_async_copy(
                    value_hbm.at[0, :, span], value_ref.at[:, span], sems.at[part, 1]
                ),
            ]
        )
    for copy in copies + sum(pieces, []):
        copy.start()
    for copy in copies:
        copy.wait()
    columns, across = running_sums(rate_ref[...])
    for part in range(parts):
        for copy in pieces[part]:
            copy.wait()
    own_fading(doc_ref[...], across, key_ref, value_ref, 0, out_ref)


def state_kernel(*refs):
    @pl.when(lax.axis_index("ctx") < lax.axis_size("ctx") - 1)
    def _():
        state_work(*refs)


def inside_kernel(
    query_hbm,
    key_hbm,
    value_hbm,
    gate_hbm,
    rate_hbm,
    doc_hbm,
    gain_hbm,
    weight_hbm,
    out_ref,
    factor_ref,
    doc_out_ref,
    query_ref,
    weight_ref,
    key_ref,
    value_ref,
    gate_ref,
    rate_ref,
    doc_ref,
    gain_ref,
    sems,
):
    sources = [rate_hbm.at[0], doc_hbm, gain_hbm, query_hbm.at[0], key_hbm.at[0], value_hbm.at[0]]
    sources += [gate_hbm.at[0], weight_hbm.at[0]]
    targets = [rate_ref, doc_ref, gain_ref, query_ref, key_ref, value_ref, gate_ref, weight_ref]
    copies = [
        pltpu.make_async_copy(source, target, sems.at[i])
        for i, (source, target) in enumerate(zip(sources, targets))
    ]
    for copy in copies:
        copy.start()
    for copy in copies[:3]:
        copy.wait()
    heads, rows = rate_ref.shape
    columns, across = running_sums(rate_ref[...])
    reach = jnp.exp(columns)
    doc_across = jnp.broadcast_to(doc_ref[...].astype(jnp.float32) + 1.0, (rows, rows))
    doc_out_ref[...] = doc_across.T
    allowed = (
        lax.broadcasted_iota(jnp.int32, (rows, rows), 0)
        >= lax.broadcasted_iota(jnp.int32, (rows, rows), 1)
    ) & (doc_across == doc_across.T)
    for copy in copies[3:6]:
        copy.wait()
    for h in range(heads):
        span = slice(h * DH, (h + 1) * DH)
        gaps = columns[:, h : h + 1] - across[h : h + 1, :]
        weights = jnp.where(allowed, jnp.exp(jnp.where(allowed, gaps, 0.0)), 0.0)
        scores = dot(query_ref[:, span], key_ref[:, span], ((1,), (1,)))
        mixed = (scores * weights).astype(jnp.bfloat16)
        out_ref[:, span] = dot(mixed, value_ref[:, span])
        reached = query_ref[:, span].astype(jnp.float32) * reach[:, h : h + 1]
        query_ref[:, span] = reached.astype(jnp.bfloat16)
    copies[6].wait()
    for h in range(heads):
        span = slice(h * DH, (h + 1) * DH)
        gate = jax.nn.sigmoid(gate_ref[:, span].astype(jnp.float32))
        factor_ref[:, span] = gain_ref[:, span] * gate
    copies[7].wait()


def finish_kernel(inside_ref, factor_ref, doc_ref, query_ref, state_ref, *out_refs):
    width = inside_ref.shape[1]
    part = out_refs[0].shape[0]
    incoming = state_ref[width:, :].astype(jnp.float32)[0:1, :]
    reached = (doc_ref[...] == incoming).astype(jnp.float32)
    average = jnp.full((DH, DH), 1.0 / DH, jnp.bfloat16)
    for start in range(0, width, DH):
        span = slice(start, start + DH)
        attended = inside_ref[:, span] + reached * dot(query_ref[:, span], state_ref[span, :])
        mean = dot((attended * attended).astype(jnp.bfloat16), average)
        scaling = lax.rsqrt(mean + 1e-06) * factor_ref[:, span]
        normed = (attended * scaling).astype(jnp.bfloat16)
        for i, out_ref in enumerate(out_refs):
            out_ref[:, span] = normed[i * part : (i + 1) * part]


def project_kernel(other, *refs):
    out_ref = refs[-1]
    blocks, rows, columns = out_ref.shape
    pieces, weight_ref = refs[:blocks], refs[blocks]
    half = (lax.axis_index("head") & 1) ^ other
    wide = math.gcd(columns, 256)
    everything = jnp.concatenate([piece[...] for piece in pieces], axis=0)
    for start in range(0, columns, wide):
        span = pl.ds(pl.multiple_of(half * columns + start, wide), wide)
        result = dot(everything, weight_ref[:, span]).astype(jnp.bfloat16)
        for j in range(blocks):
            out_ref[j, :, start : start + wide] = result[j * rows : (j + 1) * rows]


def hold_kernel(upper_ref, lower_ref, *refs):
    for source_ref, out_ref in zip((upper_ref, lower_ref), refs[-2:]):
        out_ref[...] = source_ref[...]


def merge_kernel(layout, *refs):
    out_refs = refs[-len(layout) :]
    rows = refs[0].shape[1]
    for out_ref, places in zip(out_refs, layout):
        for i, (source, block) in enumerate(places):
            keep_ref, arrived_ref = refs[2 * source], refs[2 * source + 1]
            total = keep_ref[block].astype(jnp.float32) + arrived_ref[block].astype(jnp.float32)
            out_ref[i * rows : (i + 1) * rows, :] = total.astype(jnp.bfloat16)


def pick_kernel(*refs):
    count = lax.axis_size("head")
    block_refs, out_refs = refs[: -count], refs[-count:]
    at = lax.axis_index("ctx") ^ lax.axis_index("head")
    for m, out_ref in enumerate(out_refs):
        for j in range(count):

            @pl.when((at ^ m) == j)
            def _(out_ref=out_ref, j=j):
                if j < count - 1:
                    out_ref[...] = block_refs[j][...]
                else:
                    out_ref[...] = jnp.concatenate([ref[...] for ref in block_refs[j:]], axis=0)


def last_kernel(*refs):
    out_ref = refs[-1]
    wide = refs[0].shape[1]
    for m in range(2):
        total = refs[m][...].astype(jnp.float32) + refs[m + 2][...].astype(jnp.float32)
        half = (lax.axis_index("head") & 1) ^ 1 ^ m
        out_ref[0, :, pl.ds(pl.multiple_of(half * wide, wide), wide)] = total.astype(jnp.bfloat16)


def call(kernel, out_shape, name, limit=24, **more):
    return pl.pallas_call(
        kernel,
        out_shape=out_shape,
        compiler_params=pltpu.CompilerParams(vmem_limit_bytes=limit * 2**20),
        cost_estimate=pl.CostEstimate(flops=1, bytes_accessed=1, transcendentals=0),
        name=name,
        **more,
    )


def on_device(sizes, queries, keys, values, gates, log_decay, segment_ids, norm_gain, out_weight):
    n_ctx, n_head, n_pipe = sizes
    rows, width = queries.shape[1:]
    heads = width // DH
    tokens = rows * n_ctx
    hops = min(n_ctx - 1, -(-(tokens // 4 - 1) // rows))

    def stay(array):
        return pltpu.with_memory_space_constraint(array, pltpu.HBM)

    rates = stay(jnp.swapaxes(log_decay, 1, 2))
    queries, keys, values, gates = map(stay, (queries, keys, values, gates))
    segment_ids, norm_gain, out_weight = map(stay, (segment_ids, norm_gain, out_weight))
    columns = out_weight.shape[2]
    side = heads
    wide = width

    def from_before(array, by):
        return lax.ppermute(array, "ctx", [(i, i + by) for i in range(n_ctx - by)])

    parts = 4 if side % 4 == 0 else 1
    state_shape = jax.ShapeDtypeStruct((wide + EXTRA, DH), jnp.bfloat16)
    state = call(
        state_kernel,
        state_shape,
        "shard_state",
        in_specs=[HBM] * 4,
        scratch_shapes=[
            pltpu.VMEM((rows, wide), jnp.bfloat16),
            pltpu.VMEM((rows, wide), jnp.bfloat16),
            pltpu.VMEM((heads, rows), jnp.float32),
            pltpu.VMEM((1, rows), jnp.int32),
            pltpu.SemaphoreType.DMA((parts, 2)),
            pltpu.SemaphoreType.DMA((2,)),
        ],
    )(keys, values, rates, segment_ids)

    def entering(state, first):
        incoming = from_before(state, 1)
        if hops > 1:
            decay = jnp.exp(jnp.sum(log_decay[0, :, first : first + side], axis=0))
            decay = decay.astype(jnp.bfloat16)
            total = incoming[:wide].reshape(side, DH, DH).astype(jnp.float32)
            through = jnp.ones((side,), jnp.float32)
            for by in range(2, hops + 1):
                through = through * from_before(decay, by - 1).astype(jnp.float32)
                far = from_before(state, by)
                same = jnp.where(far[wide, 0] == incoming[wide, 0], through, 0.0)
                far = far[:wide].reshape(side, DH, DH).astype(jnp.float32)
                total = total + same[:, None, None] * far
            total = total.reshape(wide, DH).astype(jnp.bfloat16)
            incoming = jnp.concatenate([total, incoming[wide:]], axis=0)
        return incoming

    inside, factor, docs, query, weight = call(
        inside_kernel,
        (
            pltpu.VMEM((rows, width), jnp.float32),
            pltpu.VMEM((rows, width), jnp.float32),
            pltpu.VMEM((rows, DH), jnp.float32),
            pltpu.VMEM((rows, width), jnp.bfloat16),
            pltpu.VMEM((width, columns), jnp.bfloat16),
        ),
        "inside",
        in_specs=[HBM] * 8,
        scratch_shapes=[
            pltpu.VMEM((rows, width), jnp.bfloat16),
            pltpu.VMEM((rows, width), jnp.bfloat16),
            pltpu.VMEM((rows, width), jnp.bfloat16),
            pltpu.VMEM((heads, rows), jnp.float32),
            pltpu.VMEM((1, rows), jnp.int32),
            pltpu.VMEM((1, width), jnp.float32),
            pltpu.SemaphoreType.DMA((8,)),
        ],
    )(queries, keys, values, gates, rates, segment_ids, norm_gain, out_weight)
    incoming = entering(state, 0)

    part = rows // 2
    normed = call(
        finish_kernel,
        (jax.ShapeDtypeStruct((part, width), jnp.bfloat16),) * 2,
        "finish",
    )(inside, factor, docs, query, incoming)

    if n_ctx != 4 or n_head != 4 or n_pipe != 2:
        normed = lax.all_gather(jnp.concatenate(normed, axis=0), "ctx", axis=0, tiled=True)
        blocks = jnp.dot(normed, weight, preferred_element_type=jnp.float32).astype(jnp.bfloat16)
        blocks = lax.all_to_all(blocks.reshape(n_ctx, rows, columns), "ctx", 0, 0, tiled=True)
        blocks = blocks.reshape(n_head, n_ctx // n_head, rows, columns)
        blocks = lax.all_to_all(blocks, "head", 0, 0, tiled=True)
        total = jnp.sum(blocks.astype(jnp.float32), axis=0).astype(jnp.bfloat16)
        total = jnp.swapaxes(total, 0, 1).reshape(1, rows, -1)
        return lax.ppermute(total, "pipe", [(s, (s + 1) % n_pipe) for s in range(n_pipe)])

    def moved(array, target):
        names = ("ctx", "head", "pipe")
        spots = [(i, j, s) for i in range(n_ctx) for j in range(n_head) for s in range(n_pipe)]
        place = {spot: at for at, spot in enumerate(spots)}
        return lax.ppermute(array, names, [(place[spot], place[target(*spot)]) for spot in spots])

    def swapped(array, by):
        return moved(array, lambda i, j, s: (i ^ by, j, s))

    single = jax.ShapeDtypeStruct((rows, columns // 2), jnp.bfloat16)

    def project(picked, other, after=()):
        shape = jax.ShapeDtypeStruct((len(picked), part, columns // 2), jnp.bfloat16)
        specs = [VMEM] * (len(picked) + 1) + [ANY] * len(after)
        kernel = functools.partial(project_kernel, other)
        return call(kernel, shape, "project", in_specs=specs)(*picked, weight, *after)

    def partner(send):
        return moved(send, lambda i, j, s: (i, j ^ 1, s))

    def merge(layout, sums, after=()):
        specs = [VMEM] * len(sums) + [ANY] * len(after)
        kernel = functools.partial(merge_kernel, layout)
        shapes = [jax.ShapeDtypeStruct((part * len(x), columns // 2), jnp.bfloat16) for x in layout]
        return call(kernel, tuple(shapes), "merge", in_specs=specs)(*sums, *after)

    upper, lower = normed
    upper_1, lower_2 = swapped(upper, 1), swapped(lower, 2)
    whole = (((0, 0), (0, 1)),)

    def hold(pair, after):
        shape = jax.ShapeDtypeStruct((part, width), jnp.bfloat16)
        specs = [VMEM] * 2 + [ANY] * len(after)
        return call(hold_kernel, (shape,) * 2, "hold", in_specs=specs)(*pair, *after)

    own_send = project((upper, lower), 1)
    own = merge(whole, (project((upper, lower), 0), partner(own_send)))
    lower_1, upper_2 = swapped(lower, 1), swapped(upper, 2)
    held = hold((upper_1, lower_2), (lower_1, upper_2, *own))
    beside = (upper_1, lower_1, upper_2, lower_2)
    beside_send, beside_keep = project(beside, 1, own), project(beside, 0)
    beside_arrived = partner(beside_send)
    across = (swapped(held[0], 2), swapped(held[1], 1))
    across_sum = (project(across, 0), partner(project(across, 1, (beside_keep,))))
    across = merge(whole, across_sum)
    beside = merge(
        (((0, 0), (0, 1)), ((0, 2), (0, 3))), (beside_keep, beside_arrived), across
    )
    blocks = [swapped(block, k) if k else block for k, block in enumerate((*own, *beside, *across))]
    picked = call(pick_kernel, (single,) * n_head, "pick")(*blocks)
    arrived = [moved(picked[m], lambda i, j, s, m=m: (i, j ^ m, s)) for m in (3, 2, 1)]
    out = jax.ShapeDtypeStruct((1, rows, columns), jnp.bfloat16)
    out = call(last_kernel, out, "last")(*arrived, picked[0])
    return moved(out, lambda i, j, s: (i, j, 1 - s))


def solution(mesh):
    sizes = tuple(mesh.shape[axis] for axis in ("ctx", "head", "pipe"))
    return jax.shard_map(
        functools.partial(on_device, sizes),
        mesh=mesh,
        in_specs=(
            P("pipe", "ctx", "head"),
            P("pipe", "ctx", "head"),
            P("pipe", "ctx", "head"),
            P("pipe", "ctx", "head"),
            P("pipe", "ctx", "head"),
            P("pipe", "ctx"),
            P("pipe", "head"),
            P("pipe", "head", "ctx"),
        ),
        out_specs=P("pipe", "ctx", "head"),
        check_vma=False,
    )
```

```python
import functools
import math

import jax
import jax.numpy as jnp
from jax import lax
from jax.experimental import pallas as pl
from jax.experimental.pallas import tpu as pltpu
from jax.sharding import PartitionSpec as P

DH = 128
EXTRA = 16
VMEM = pl.BlockSpec(memory_space=pltpu.VMEM)
ANY = pl.BlockSpec(memory_space=pl.ANY)
HBM = pl.BlockSpec(memory_space=pltpu.HBM)


def dot(a, b, contract=((1,), (0,)), precision=None):
    return lax.dot_general(
        a, b, (contract, ((), ())), preferred_element_type=jnp.float32, precision=precision
    )


def running_sums(rate):
    rows = rate.shape[1]
    upper = (
        lax.broadcasted_iota(jnp.int32, (rows, rows), 0)
        <= lax.broadcasted_iota(jnp.int32, (rows, rows), 1)
    ).astype(jnp.float32)
    across = dot(rate, upper, precision=lax.Precision.HIGHEST)
    columns = dot(upper, rate, ((0,), (1,)), precision=lax.Precision.HIGHEST)
    return columns, across


def own_fading(doc, across, key_ref, value_ref, first, out_ref):
    rows = doc.shape[1]
    wide = out_ref.shape[0] - EXTRA
    last_doc = doc[:, rows - 1 :]
    fading = jnp.where(doc == last_doc, jnp.exp(across[:, rows - 1 :] - across), 0.0)
    fading_columns = fading.T
    out_ref[wide:, :] = jnp.broadcast_to(
        (last_doc + 1).astype(jnp.float32), (EXTRA, DH)
    ).astype(jnp.bfloat16)
    for k in range(wide // DH):
        h = first + k
        span = slice(h * DH, (h + 1) * DH)
        faded = (key_ref[:, span].astype(jnp.float32) * fading_columns[:, h : h + 1]).astype(
            jnp.bfloat16
        )
        out_ref[k * DH : (k + 1) * DH, :] = dot(faded, value_ref[:, span], ((0,), (0,))).astype(
            jnp.bfloat16
        )


def state_work(
    key_hbm,
    value_hbm,
    rate_hbm,
    doc_hbm,
    *refs,
):
    out_ref, key_ref, value_ref, rate_ref, doc_ref, sems, small = refs[-7:]
    rows = rate_ref.shape[1]
    wide = key_ref.shape[1]
    parts = sems.shape[0]
    piece = wide // parts
    copies = [
        pltpu.make_async_copy(rate_hbm.at[0], rate_ref, small.at[0]),
        pltpu.make_async_copy(doc_hbm, doc_ref, small.at[1]),
    ]
    pieces = []
    for part in range(parts):
        span = pl.ds(part * piece, piece)
        pieces.append(
            [
                pltpu.make_async_copy(
                    key_hbm.at[0, :, span], key_ref.at[:, span], sems.at[part, 0]
                ),
                pltpu.make_async_copy(
                    value_hbm.at[0, :, span], value_ref.at[:, span], sems.at[part, 1]
                ),
            ]
        )
    for copy in copies + sum(pieces, []):
        copy.start()
    for copy in copies:
        copy.wait()
    columns, across = running_sums(rate_ref[...])
    for part in range(parts):
        for copy in pieces[part]:
            copy.wait()
    own_fading(doc_ref[...], across, key_ref, value_ref, 0, out_ref)


def state_kernel(*refs):
    @pl.when(lax.axis_index("ctx") < lax.axis_size("ctx") - 1)
    def _():
        state_work(*refs)


def inside_kernel(
    query_hbm,
    key_hbm,
    value_hbm,
    gate_hbm,
    rate_hbm,
    doc_hbm,
    gain_hbm,
    weight_hbm,
    out_ref,
    factor_ref,
    doc_out_ref,
    query_ref,
    weight_ref,
    key_ref,
    value_ref,
    gate_ref,
    rate_ref,
    doc_ref,
    gain_ref,
    sems,
):
    sources = [rate_hbm.at[0], doc_hbm, gain_hbm, query_hbm.at[0], key_hbm.at[0], value_hbm.at[0]]
    sources += [gate_hbm.at[0], weight_hbm.at[0]]
    targets = [rate_ref, doc_ref, gain_ref, query_ref, key_ref, value_ref, gate_ref, weight_ref]
    copies = [
        pltpu.make_async_copy(source, target, sems.at[i])
        for i, (source, target) in enumerate(zip(sources, targets))
    ]
    for copy in copies:
        copy.start()
    for copy in copies[:3]:
        copy.wait()
    heads, rows = rate_ref.shape
    columns, across = running_sums(rate_ref[...])
    reach = jnp.exp(columns)
    doc_across = jnp.broadcast_to(doc_ref[...].astype(jnp.float32) + 1.0, (rows, rows))
    doc_out_ref[...] = doc_across.T
    allowed = (
        lax.broadcasted_iota(jnp.int32, (rows, rows), 0)
        >= lax.broadcasted_iota(jnp.int32, (rows, rows), 1)
    ) & (doc_across == doc_across.T)
    for copy in copies[3:6]:
        copy.wait()
    for h in range(heads):
        span = slice(h * DH, (h + 1) * DH)
        gaps = columns[:, h : h + 1] - across[h : h + 1, :]
        weights = jnp.where(allowed, jnp.exp(jnp.where(allowed, gaps, 0.0)), 0.0)
        scores = dot(query_ref[:, span], key_ref[:, span], ((1,), (1,)))
        mixed = (scores * weights).astype(jnp.bfloat16)
        out_ref[:, span] = dot(mixed, value_ref[:, span])
        reached = query_ref[:, span].astype(jnp.float32) * reach[:, h : h + 1]
        query_ref[:, span] = reached.astype(jnp.bfloat16)
    copies[6].wait()
    for h in range(heads):
        span = slice(h * DH, (h + 1) * DH)
        gate = jax.nn.sigmoid(gate_ref[:, span].astype(jnp.float32))
        factor_ref[:, span] = gain_ref[:, span] * gate
    copies[7].wait()


def finish_kernel(inside_ref, factor_ref, doc_ref, query_ref, state_ref, *out_refs):
    width = inside_ref.shape[1]
    part = out_refs[0].shape[0]
    incoming = state_ref[width:, :].astype(jnp.float32)[0:1, :]
    reached = (doc_ref[...] == incoming).astype(jnp.float32)
    average = jnp.full((DH, DH), 1.0 / DH, jnp.bfloat16)
    for start in range(0, width, DH):
        span = slice(start, start + DH)
        attended = inside_ref[:, span] + reached * dot(query_ref[:, span], state_ref[span, :])
        mean = dot((attended * attended).astype(jnp.bfloat16), average)
        scaling = lax.rsqrt(mean + 1e-06) * factor_ref[:, span]
        normed = (attended * scaling).astype(jnp.bfloat16)
        for i, out_ref in enumerate(out_refs):
            out_ref[:, span] = normed[i * part : (i + 1) * part]


def project_kernel(other, *refs):
    out_ref = refs[-1]
    blocks, rows, columns = out_ref.shape
    pieces, weight_ref = refs[:blocks], refs[blocks]
    half = (lax.axis_index("head") & 1) ^ other
    wide = math.gcd(columns, 256)
    everything = jnp.concatenate([piece[...] for piece in pieces], axis=0)
    for start in range(0, columns, wide):
        span = pl.ds(pl.multiple_of(half * columns + start, wide), wide)
        result = dot(everything, weight_ref[:, span]).astype(jnp.bfloat16)
        for j in range(blocks):
            out_ref[j, :, start : start + wide] = result[j * rows : (j + 1) * rows]


def hold_kernel(upper_ref, lower_ref, *refs):
    for source_ref, out_ref in zip((upper_ref, lower_ref), refs[-2:]):
        out_ref[...] = source_ref[...]


def merge_kernel(layout, *refs):
    out_refs = refs[-len(layout) :]
    rows = refs[0].shape[1]
    for out_ref, places in zip(out_refs, layout):
        for i, (source, block) in enumerate(places):
            keep_ref, arrived_ref = refs[2 * source], refs[2 * source + 1]
            total = keep_ref[block].astype(jnp.float32) + arrived_ref[block].astype(jnp.float32)
            out_ref[i * rows : (i + 1) * rows, :] = total.astype(jnp.bfloat16)


def pick_kernel(*refs):
    count = lax.axis_size("head")
    block_refs, out_refs = refs[: -count], refs[-count:]
    at = lax.axis_index("ctx") ^ lax.axis_index("head")
    for m, out_ref in enumerate(out_refs):
        for j in range(count):

            @pl.when((at ^ m) == j)
            def _(out_ref=out_ref, j=j):
                if j < count - 1:
                    out_ref[...] = block_refs[j][...]
                else:
                    out_ref[...] = jnp.concatenate([ref[...] for ref in block_refs[j:]], axis=0)


def last_kernel(*refs):
    out_ref = refs[-1]
    wide = refs[0].shape[1]
    for m in range(2):
        total = refs[m][...].astype(jnp.float32) + refs[m + 2][...].astype(jnp.float32)
        half = (lax.axis_index("head") & 1) ^ 1 ^ m
        out_ref[0, :, pl.ds(pl.multiple_of(half * wide, wide), wide)] = total.astype(jnp.bfloat16)


def call(kernel, out_shape, name, limit=24, **more):
    return pl.pallas_call(
        kernel,
        out_shape=out_shape,
        compiler_params=pltpu.CompilerParams(vmem_limit_bytes=limit * 2**20),
        cost_estimate=pl.CostEstimate(flops=1, bytes_accessed=1, transcendentals=0),
        name=name,
        **more,
    )


def on_device(sizes, queries, keys, values, gates, log_decay, segment_ids, norm_gain, out_weight):
    n_ctx, n_head, n_pipe = sizes
    rows, width = queries.shape[1:]
    heads = width // DH
    tokens = rows * n_ctx
    hops = min(n_ctx - 1, -(-(tokens // 4 - 1) // rows))

    def stay(array):
        return pltpu.with_memory_space_constraint(array, pltpu.HBM)

    rates = stay(jnp.swapaxes(log_decay, 1, 2))
    queries, keys, values, gates = map(stay, (queries, keys, values, gates))
    segment_ids, norm_gain, out_weight = map(stay, (segment_ids, norm_gain, out_weight))
    columns = out_weight.shape[2]
    side = heads
    wide = width

    def from_before(array, by):
        return lax.ppermute(array, "ctx", [(i, i + by) for i in range(n_ctx - by)])

    parts = 4 if side % 4 == 0 else 1
    state_shape = jax.ShapeDtypeStruct((wide + EXTRA, DH), jnp.bfloat16)
    state = call(
        state_kernel,
        state_shape,
        "shard_state",
        in_specs=[HBM] * 4,
        scratch_shapes=[
            pltpu.VMEM((rows, wide), jnp.bfloat16),
            pltpu.VMEM((rows, wide), jnp.bfloat16),
            pltpu.VMEM((heads, rows), jnp.float32),
            pltpu.VMEM((1, rows), jnp.int32),
            pltpu.SemaphoreType.DMA((parts, 2)),
            pltpu.SemaphoreType.DMA((2,)),
        ],
    )(keys, values, rates, segment_ids)

    def entering(state, first):
        incoming = from_before(state, 1)
        if hops > 1:
            decay = jnp.exp(jnp.sum(log_decay[0, :, first : first + side], axis=0))
            decay = decay.astype(jnp.bfloat16)
            total = incoming[:wide].reshape(side, DH, DH).astype(jnp.float32)
            through = jnp.ones((side,), jnp.float32)
            for by in range(2, hops + 1):
                through = through * from_before(decay, by - 1).astype(jnp.float32)
                far = from_before(state, by)
                same = jnp.where(far[wide, 0] == incoming[wide, 0], through, 0.0)
                far = far[:wide].reshape(side, DH, DH).astype(jnp.float32)
                total = total + same[:, None, None] * far
            total = total.reshape(wide, DH).astype(jnp.bfloat16)
            incoming = jnp.concatenate([total, incoming[wide:]], axis=0)
        return incoming

    inside, factor, docs, query, weight = call(
        inside_kernel,
        (
            pltpu.VMEM((rows, width), jnp.float32),
            pltpu.VMEM((rows, width), jnp.float32),
            pltpu.VMEM((rows, DH), jnp.float32),
            pltpu.VMEM((rows, width), jnp.bfloat16),
            pltpu.VMEM((width, columns), jnp.bfloat16),
        ),
        "inside",
        in_specs=[HBM] * 8,
        scratch_shapes=[
            pltpu.VMEM((rows, width), jnp.bfloat16),
            pltpu.VMEM((rows, width), jnp.bfloat16),
            pltpu.VMEM((rows, width), jnp.bfloat16),
            pltpu.VMEM((heads, rows), jnp.float32),
            pltpu.VMEM((1, rows), jnp.int32),
            pltpu.VMEM((1, width), jnp.float32),
            pltpu.SemaphoreType.DMA((8,)),
        ],
    )(queries, keys, values, gates, rates, segment_ids, norm_gain, out_weight)
    incoming = entering(state, 0)

    part = rows // 2
    normed = call(
        finish_kernel,
        (jax.ShapeDtypeStruct((part, width), jnp.bfloat16),) * 2,
        "finish",
    )(inside, factor, docs, query, incoming)

    if n_ctx != 4 or n_head != 4 or n_pipe != 2:
        normed = lax.all_gather(jnp.concatenate(normed, axis=0), "ctx", axis=0, tiled=True)
        blocks = jnp.dot(normed, weight, preferred_element_type=jnp.float32).astype(jnp.bfloat16)
        blocks = lax.all_to_all(blocks.reshape(n_ctx, rows, columns), "ctx", 0, 0, tiled=True)
        blocks = blocks.reshape(n_head, n_ctx // n_head, rows, columns)
        blocks = lax.all_to_all(blocks, "head", 0, 0, tiled=True)
        total = jnp.sum(blocks.astype(jnp.float32), axis=0).astype(jnp.bfloat16)
        total = jnp.swapaxes(total, 0, 1).reshape(1, rows, -1)
        return lax.ppermute(total, "pipe", [(s, (s + 1) % n_pipe) for s in range(n_pipe)])

    def moved(array, target):
        names = ("ctx", "head", "pipe")
        spots = [(i, j, s) for i in range(n_ctx) for j in range(n_head) for s in range(n_pipe)]
        place = {spot: at for at, spot in enumerate(spots)}
        return lax.ppermute(array, names, [(place[spot], place[target(*spot)]) for spot in spots])

    def swapped(array, by):
        return moved(array, lambda i, j, s: (i ^ by, j, s))

    single = jax.ShapeDtypeStruct((rows, columns // 2), jnp.bfloat16)

    def project(picked, other, after=()):
        shape = jax.ShapeDtypeStruct((len(picked), part, columns // 2), jnp.bfloat16)
        specs = [VMEM] * (len(picked) + 1) + [ANY] * len(after)
        kernel = functools.partial(project_kernel, other)
        return call(kernel, shape, "project", in_specs=specs)(*picked, weight, *after)

    def partner(send):
        return moved(send, lambda i, j, s: (i, j ^ 1, s))

    def merge(layout, sums, after=()):
        specs = [VMEM] * len(sums) + [ANY] * len(after)
        kernel = functools.partial(merge_kernel, layout)
        shapes = [jax.ShapeDtypeStruct((part * len(x), columns // 2), jnp.bfloat16) for x in layout]
        return call(kernel, tuple(shapes), "merge", in_specs=specs)(*sums, *after)

    upper, lower = normed
    upper_1, lower_2 = swapped(upper, 1), swapped(lower, 2)
    whole = (((0, 0), (0, 1)),)

    def hold(pair, after):
        shape = jax.ShapeDtypeStruct((part, width), jnp.bfloat16)
        specs = [VMEM] * 2 + [ANY] * len(after)
        return call(hold_kernel, (shape,) * 2, "hold", in_specs=specs)(*pair, *after)

    own_send = project((upper, lower), 1)
    own = merge(whole, (project((upper, lower), 0), partner(own_send)))
    lower_1, upper_2 = swapped(lower, 1), swapped(upper, 2)
    held = hold((upper_1, lower_2), (lower_1, upper_2, *own))
    beside = (upper_1, lower_1, upper_2, lower_2)
    beside_send, beside_keep = project(beside, 1, own), project(beside, 0)
    beside = merge(
        (((0, 0), (0, 1)), ((0, 2), (0, 3))),
        (beside_keep, partner(beside_send)),
    )
    across = (swapped(held[0], 2), swapped(held[1], 1))
    across_sum = (project(across, 0), partner(project(across, 1, (beside_keep,))))
    across = merge(whole, across_sum, beside[:1])
    blocks = [swapped(block, k) if k else block for k, block in enumerate((*own, *beside, *across))]
    picked = call(pick_kernel, (single,) * n_head, "pick")(*blocks)
    arrived = [moved(picked[m], lambda i, j, s, m=m: (i, j ^ m, s)) for m in (1, 2, 3)]
    out = jax.ShapeDtypeStruct((1, rows, columns), jnp.bfloat16)
    out = call(last_kernel, out, "last")(*arrived, picked[0])
    return moved(out, lambda i, j, s: (i, j, 1 - s))


def solution(mesh):
    sizes = tuple(mesh.shape[axis] for axis in ("ctx", "head", "pipe"))
    return jax.shard_map(
        functools.partial(on_device, sizes),
        mesh=mesh,
        in_specs=(
            P("pipe", "ctx", "head"),
            P("pipe", "ctx", "head"),
            P("pipe", "ctx", "head"),
            P("pipe", "ctx", "head"),
            P("pipe", "ctx", "head"),
            P("pipe", "ctx"),
            P("pipe", "head"),
            P("pipe", "head", "ctx"),
        ),
        out_specs=P("pipe", "ctx", "head"),
        check_vma=False,
    )
```

```python
import functools
import math

import jax
import jax.numpy as jnp
from jax import lax
from jax.experimental import pallas as pl
from jax.experimental.pallas import tpu as pltpu
from jax.sharding import PartitionSpec as P

DH = 128
EXTRA = 16
VMEM = pl.BlockSpec(memory_space=pltpu.VMEM)
ANY = pl.BlockSpec(memory_space=pl.ANY)
HBM = pl.BlockSpec(memory_space=pltpu.HBM)


def dot(a, b, contract=((1,), (0,)), precision=None):
    return lax.dot_general(
        a, b, (contract, ((), ())), preferred_element_type=jnp.float32, precision=precision
    )


def running_sums(rate):
    rows = rate.shape[1]
    upper = (
        lax.broadcasted_iota(jnp.int32, (rows, rows), 0)
        <= lax.broadcasted_iota(jnp.int32, (rows, rows), 1)
    ).astype(jnp.float32)
    across = dot(rate, upper, precision=lax.Precision.HIGHEST)
    columns = dot(upper, rate, ((0,), (1,)), precision=lax.Precision.HIGHEST)
    return columns, across


def own_fading(doc, across, key_ref, value_ref, first, out_ref):
    rows = doc.shape[1]
    wide = out_ref.shape[0] - EXTRA
    last_doc = doc[:, rows - 1 :]
    fading = jnp.where(doc == last_doc, jnp.exp(across[:, rows - 1 :] - across), 0.0)
    fading_columns = fading.T
    out_ref[wide:, :] = jnp.broadcast_to(
        (last_doc + 1).astype(jnp.float32), (EXTRA, DH)
    ).astype(jnp.bfloat16)
    for k in range(wide // DH):
        h = first + k
        span = slice(h * DH, (h + 1) * DH)
        faded = (key_ref[:, span].astype(jnp.float32) * fading_columns[:, h : h + 1]).astype(
            jnp.bfloat16
        )
        out_ref[k * DH : (k + 1) * DH, :] = dot(faded, value_ref[:, span], ((0,), (0,))).astype(
            jnp.bfloat16
        )


def state_work(
    key_hbm,
    value_hbm,
    rate_hbm,
    doc_hbm,
    *refs,
):
    out_ref, key_ref, value_ref, rate_ref, doc_ref, sems, small = refs[-7:]
    rows = rate_ref.shape[1]
    wide = key_ref.shape[1]
    parts = sems.shape[0]
    piece = wide // parts
    copies = [
        pltpu.make_async_copy(rate_hbm.at[0], rate_ref, small.at[0]),
        pltpu.make_async_copy(doc_hbm, doc_ref, small.at[1]),
    ]
    pieces = []
    for part in range(parts):
        span = pl.ds(part * piece, piece)
        pieces.append(
            [
                pltpu.make_async_copy(
                    key_hbm.at[0, :, span], key_ref.at[:, span], sems.at[part, 0]
                ),
                pltpu.make_async_copy(
                    value_hbm.at[0, :, span], value_ref.at[:, span], sems.at[part, 1]
                ),
            ]
        )
    for copy in copies + sum(pieces, []):
        copy.start()
    for copy in copies:
        copy.wait()
    columns, across = running_sums(rate_ref[...])
    for part in range(parts):
        for copy in pieces[part]:
            copy.wait()
    own_fading(doc_ref[...], across, key_ref, value_ref, 0, out_ref)


def state_kernel(*refs):
    @pl.when(lax.axis_index("ctx") < lax.axis_size("ctx") - 1)
    def _():
        state_work(*refs)


def inside_kernel(
    query_hbm,
    key_hbm,
    value_hbm,
    gate_hbm,
    rate_hbm,
    doc_hbm,
    gain_hbm,
    weight_hbm,
    out_ref,
    factor_ref,
    doc_out_ref,
    query_ref,
    weight_ref,
    key_ref,
    value_ref,
    gate_ref,
    rate_ref,
    doc_ref,
    gain_ref,
    sems,
):
    sources = [rate_hbm.at[0], doc_hbm, gain_hbm, query_hbm.at[0], key_hbm.at[0], value_hbm.at[0]]
    sources += [gate_hbm.at[0], weight_hbm.at[0]]
    targets = [rate_ref, doc_ref, gain_ref, query_ref, key_ref, value_ref, gate_ref, weight_ref]
    copies = [
        pltpu.make_async_copy(source, target, sems.at[i])
        for i, (source, target) in enumerate(zip(sources, targets))
    ]
    for copy in copies:
        copy.start()
    for copy in copies[:3]:
        copy.wait()
    heads, rows = rate_ref.shape
    columns, across = running_sums(rate_ref[...])
    reach = jnp.exp(columns)
    doc_across = jnp.broadcast_to(doc_ref[...].astype(jnp.float32) + 1.0, (rows, rows))
    doc_out_ref[...] = doc_across.T
    allowed = (
        lax.broadcasted_iota(jnp.int32, (rows, rows), 0)
        >= lax.broadcasted_iota(jnp.int32, (rows, rows), 1)
    ) & (doc_across == doc_across.T)
    for copy in copies[3:6]:
        copy.wait()
    for h in range(heads):
        span = slice(h * DH, (h + 1) * DH)
        gaps = columns[:, h : h + 1] - across[h : h + 1, :]
        weights = jnp.where(allowed, jnp.exp(jnp.where(allowed, gaps, 0.0)), 0.0)
        scores = dot(query_ref[:, span], key_ref[:, span], ((1,), (1,)))
        mixed = (scores * weights).astype(jnp.bfloat16)
        out_ref[:, span] = dot(mixed, value_ref[:, span])
        reached = query_ref[:, span].astype(jnp.float32) * reach[:, h : h + 1]
        query_ref[:, span] = reached.astype(jnp.bfloat16)
    copies[6].wait()
    for h in range(heads):
        span = slice(h * DH, (h + 1) * DH)
        gate = jax.nn.sigmoid(gate_ref[:, span].astype(jnp.float32))
        factor_ref[:, span] = gain_ref[:, span] * gate
    copies[7].wait()


def finish_kernel(inside_ref, factor_ref, doc_ref, query_ref, state_ref, *out_refs):
    width = inside_ref.shape[1]
    part = out_refs[0].shape[0]
    incoming = state_ref[width:, :].astype(jnp.float32)[0:1, :]
    reached = (doc_ref[...] == incoming).astype(jnp.float32)
    average = jnp.full((DH, DH), 1.0 / DH, jnp.bfloat16)
    for start in range(0, width, DH):
        span = slice(start, start + DH)
        attended = inside_ref[:, span] + reached * dot(query_ref[:, span], state_ref[span, :])
        mean = dot((attended * attended).astype(jnp.bfloat16), average)
        scaling = lax.rsqrt(mean + 1e-06) * factor_ref[:, span]
        normed = (attended * scaling).astype(jnp.bfloat16)
        for i, out_ref in enumerate(out_refs):
            out_ref[:, span] = normed[i * part : (i + 1) * part]


def project_kernel(other, *refs):
    out_ref = refs[-1]
    blocks, rows, columns = out_ref.shape
    pieces, weight_ref = refs[:blocks], refs[blocks]
    half = (lax.axis_index("head") & 1) ^ other
    wide = math.gcd(columns, 256)
    everything = jnp.concatenate([piece[...] for piece in pieces], axis=0)
    for start in range(0, columns, wide):
        span = pl.ds(pl.multiple_of(half * columns + start, wide), wide)
        result = dot(everything, weight_ref[:, span]).astype(jnp.bfloat16)
        for j in range(blocks):
            out_ref[j, :, start : start + wide] = result[j * rows : (j + 1) * rows]


def hold_kernel(upper_ref, lower_ref, *refs):
    for source_ref, out_ref in zip((upper_ref, lower_ref), refs[-2:]):
        out_ref[...] = source_ref[...]


def merge_kernel(layout, *refs):
    out_refs = refs[-len(layout) :]
    rows = refs[0].shape[1]
    for out_ref, places in zip(out_refs, layout):
        for i, (source, block) in enumerate(places):
            keep_ref, arrived_ref = refs[2 * source], refs[2 * source + 1]
            total = keep_ref[block].astype(jnp.float32) + arrived_ref[block].astype(jnp.float32)
            out_ref[i * rows : (i + 1) * rows, :] = total.astype(jnp.bfloat16)


def pick_kernel(*refs):
    count = lax.axis_size("head")
    block_refs, out_refs = refs[: -count], refs[-count:]
    at = lax.axis_index("ctx") ^ lax.axis_index("head")
    for m, out_ref in enumerate(out_refs):
        for j in range(count):

            @pl.when((at ^ m) == j)
            def _(out_ref=out_ref, j=j):
                if j < count - 1:
                    out_ref[...] = block_refs[j][...]
                else:
                    out_ref[...] = jnp.concatenate([ref[...] for ref in block_refs[j:]], axis=0)


def sum_kernel(one_ref, two_ref, out_ref):
    total = one_ref[...].astype(jnp.float32) + two_ref[...].astype(jnp.float32)
    out_ref[...] = total.astype(jnp.bfloat16)


def last_kernel(*refs):
    out_ref = refs[-1]
    wide = refs[0].shape[1]
    for m in range(2):
        half = (lax.axis_index("head") & 1) ^ m
        out_ref[0, :, pl.ds(pl.multiple_of(half * wide, wide), wide)] = refs[m][...]


def call(kernel, out_shape, name, limit=24, **more):
    return pl.pallas_call(
        kernel,
        out_shape=out_shape,
        compiler_params=pltpu.CompilerParams(vmem_limit_bytes=limit * 2**20),
        cost_estimate=pl.CostEstimate(flops=1, bytes_accessed=1, transcendentals=0),
        name=name,
        **more,
    )


def on_device(sizes, queries, keys, values, gates, log_decay, segment_ids, norm_gain, out_weight):
    n_ctx, n_head, n_pipe = sizes
    rows, width = queries.shape[1:]
    heads = width // DH
    tokens = rows * n_ctx
    hops = min(n_ctx - 1, -(-(tokens // 4 - 1) // rows))

    def stay(array):
        return pltpu.with_memory_space_constraint(array, pltpu.HBM)

    rates = stay(jnp.swapaxes(log_decay, 1, 2))
    queries, keys, values, gates = map(stay, (queries, keys, values, gates))
    segment_ids, norm_gain, out_weight = map(stay, (segment_ids, norm_gain, out_weight))
    columns = out_weight.shape[2]
    side = heads
    wide = width

    def from_before(array, by):
        return lax.ppermute(array, "ctx", [(i, i + by) for i in range(n_ctx - by)])

    parts = 4 if side % 4 == 0 else 1
    state_shape = jax.ShapeDtypeStruct((wide + EXTRA, DH), jnp.bfloat16)
    state = call(
        state_kernel,
        state_shape,
        "shard_state",
        in_specs=[HBM] * 4,
        scratch_shapes=[
            pltpu.VMEM((rows, wide), jnp.bfloat16),
            pltpu.VMEM((rows, wide), jnp.bfloat16),
            pltpu.VMEM((heads, rows), jnp.float32),
            pltpu.VMEM((1, rows), jnp.int32),
            pltpu.SemaphoreType.DMA((parts, 2)),
            pltpu.SemaphoreType.DMA((2,)),
        ],
    )(keys, values, rates, segment_ids)

    def entering(state, first):
        incoming = from_before(state, 1)
        if hops > 1:
            decay = jnp.exp(jnp.sum(log_decay[0, :, first : first + side], axis=0))
            decay = decay.astype(jnp.bfloat16)
            total = incoming[:wide].reshape(side, DH, DH).astype(jnp.float32)
            through = jnp.ones((side,), jnp.float32)
            for by in range(2, hops + 1):
                through = through * from_before(decay, by - 1).astype(jnp.float32)
                far = from_before(state, by)
                same = jnp.where(far[wide, 0] == incoming[wide, 0], through, 0.0)
                far = far[:wide].reshape(side, DH, DH).astype(jnp.float32)
                total = total + same[:, None, None] * far
            total = total.reshape(wide, DH).astype(jnp.bfloat16)
            incoming = jnp.concatenate([total, incoming[wide:]], axis=0)
        return incoming

    inside, factor, docs, query, weight = call(
        inside_kernel,
        (
            pltpu.VMEM((rows, width), jnp.float32),
            pltpu.VMEM((rows, width), jnp.float32),
            pltpu.VMEM((rows, DH), jnp.float32),
            pltpu.VMEM((rows, width), jnp.bfloat16),
            pltpu.VMEM((width, columns), jnp.bfloat16),
        ),
        "inside",
        in_specs=[HBM] * 8,
        scratch_shapes=[
            pltpu.VMEM((rows, width), jnp.bfloat16),
            pltpu.VMEM((rows, width), jnp.bfloat16),
            pltpu.VMEM((rows, width), jnp.bfloat16),
            pltpu.VMEM((heads, rows), jnp.float32),
            pltpu.VMEM((1, rows), jnp.int32),
            pltpu.VMEM((1, width), jnp.float32),
            pltpu.SemaphoreType.DMA((8,)),
        ],
    )(queries, keys, values, gates, rates, segment_ids, norm_gain, out_weight)
    incoming = entering(state, 0)

    part = rows // 2
    normed = call(
        finish_kernel,
        (jax.ShapeDtypeStruct((part, width), jnp.bfloat16),) * 2,
        "finish",
    )(inside, factor, docs, query, incoming)

    if n_ctx != 4 or n_head != 4 or n_pipe != 2:
        normed = lax.all_gather(jnp.concatenate(normed, axis=0), "ctx", axis=0, tiled=True)
        blocks = jnp.dot(normed, weight, preferred_element_type=jnp.float32).astype(jnp.bfloat16)
        blocks = lax.all_to_all(blocks.reshape(n_ctx, rows, columns), "ctx", 0, 0, tiled=True)
        blocks = blocks.reshape(n_head, n_ctx // n_head, rows, columns)
        blocks = lax.all_to_all(blocks, "head", 0, 0, tiled=True)
        total = jnp.sum(blocks.astype(jnp.float32), axis=0).astype(jnp.bfloat16)
        total = jnp.swapaxes(total, 0, 1).reshape(1, rows, -1)
        return lax.ppermute(total, "pipe", [(s, (s + 1) % n_pipe) for s in range(n_pipe)])

    def moved(array, target):
        names = ("ctx", "head", "pipe")
        spots = [(i, j, s) for i in range(n_ctx) for j in range(n_head) for s in range(n_pipe)]
        place = {spot: at for at, spot in enumerate(spots)}
        return lax.ppermute(array, names, [(place[spot], place[target(*spot)]) for spot in spots])

    def swapped(array, by):
        return moved(array, lambda i, j, s: (i ^ by, j, s))

    single = jax.ShapeDtypeStruct((rows, columns // 2), jnp.bfloat16)

    def project(picked, other, after=()):
        shape = jax.ShapeDtypeStruct((len(picked), part, columns // 2), jnp.bfloat16)
        specs = [VMEM] * (len(picked) + 1) + [ANY] * len(after)
        kernel = functools.partial(project_kernel, other)
        return call(kernel, shape, "project", in_specs=specs)(*picked, weight, *after)

    def partner(send):
        return moved(send, lambda i, j, s: (i, j ^ 1, s))

    def merge(layout, sums, after=()):
        specs = [VMEM] * len(sums) + [ANY] * len(after)
        kernel = functools.partial(merge_kernel, layout)
        shapes = [jax.ShapeDtypeStruct((part * len(x), columns // 2), jnp.bfloat16) for x in layout]
        return call(kernel, tuple(shapes), "merge", in_specs=specs)(*sums, *after)

    upper, lower = normed
    upper_1, lower_2 = swapped(upper, 1), swapped(lower, 2)
    whole = (((0, 0), (0, 1)),)

    def hold(pair, after):
        shape = jax.ShapeDtypeStruct((part, width), jnp.bfloat16)
        specs = [VMEM] * 2 + [ANY] * len(after)
        return call(hold_kernel, (shape,) * 2, "hold", in_specs=specs)(*pair, *after)

    own_send = project((upper, lower), 1)
    own = merge(whole, (project((upper, lower), 0), partner(own_send)))
    lower_1, upper_2 = swapped(lower, 1), swapped(upper, 2)
    held = hold((upper_1, lower_2), (lower_1, upper_2, *own))
    beside = (upper_1, lower_1, upper_2, lower_2)
    beside_send, beside_keep = project(beside, 1, own), project(beside, 0)
    beside = merge(
        (((0, 0), (0, 1)), ((0, 2), (0, 3))),
        (beside_keep, partner(beside_send)),
    )
    across = (swapped(held[0], 2), swapped(held[1], 1))
    across_sum = (project(across, 0), partner(project(across, 1, (beside_keep,))))
    across = merge(whole, across_sum, beside[:1])
    blocks = [swapped(block, k) if k else block for k, block in enumerate((*own, *beside, *across))]
    picked = call(pick_kernel, (single,) * n_head, "pick")(*blocks)
    arrived = [moved(picked[m], lambda i, j, s, m=m: (i, j ^ m, s)) for m in (1, 2, 3)]
    total = [call(sum_kernel, single, "sum")(picked[0], arrived[1])]
    total.append(call(sum_kernel, single, "sum")(arrived[0], arrived[2]))
    total = [moved(half, lambda i, j, s: (i, j, 1 - s)) for half in total]
    out = jax.ShapeDtypeStruct((1, rows, columns), jnp.bfloat16)
    return call(last_kernel, out, "last")(*total)


def solution(mesh):
    sizes = tuple(mesh.shape[axis] for axis in ("ctx", "head", "pipe"))
    return jax.shard_map(
        functools.partial(on_device, sizes),
        mesh=mesh,
        in_specs=(
            P("pipe", "ctx", "head"),
            P("pipe", "ctx", "head"),
            P("pipe", "ctx", "head"),
            P("pipe", "ctx", "head"),
            P("pipe", "ctx", "head"),
            P("pipe", "ctx"),
            P("pipe", "head"),
            P("pipe", "head", "ctx"),
        ),
        out_specs=P("pipe", "ctx", "head"),
        check_vma=False,
    )
```

```python
import functools
import math

import jax
import jax.numpy as jnp
from jax import lax
from jax.experimental import pallas as pl
from jax.experimental.pallas import tpu as pltpu
from jax.sharding import PartitionSpec as P

DH = 128
EXTRA = 16
VMEM = pl.BlockSpec(memory_space=pltpu.VMEM)
ANY = pl.BlockSpec(memory_space=pl.ANY)
HBM = pl.BlockSpec(memory_space=pltpu.HBM)


def dot(a, b, contract=((1,), (0,)), precision=None):
    return lax.dot_general(
        a, b, (contract, ((), ())), preferred_element_type=jnp.float32, precision=precision
    )


def running_sums(rate):
    rows = rate.shape[1]
    upper = (
        lax.broadcasted_iota(jnp.int32, (rows, rows), 0)
        <= lax.broadcasted_iota(jnp.int32, (rows, rows), 1)
    ).astype(jnp.float32)
    across = dot(rate, upper, precision=lax.Precision.HIGHEST)
    columns = dot(upper, rate, ((0,), (1,)), precision=lax.Precision.HIGHEST)
    return columns, across


def own_fading(doc, across, key_ref, value_ref, first, out_ref):
    rows = doc.shape[1]
    wide = out_ref.shape[0] - EXTRA
    last_doc = doc[:, rows - 1 :]
    fading = jnp.where(doc == last_doc, jnp.exp(across[:, rows - 1 :] - across), 0.0)
    fading_columns = fading.T
    out_ref[wide:, :] = jnp.broadcast_to(
        (last_doc + 1).astype(jnp.float32), (EXTRA, DH)
    ).astype(jnp.bfloat16)
    for k in range(wide // DH):
        h = first + k
        span = slice(h * DH, (h + 1) * DH)
        faded = (key_ref[:, span].astype(jnp.float32) * fading_columns[:, h : h + 1]).astype(
            jnp.bfloat16
        )
        out_ref[k * DH : (k + 1) * DH, :] = dot(faded, value_ref[:, span], ((0,), (0,))).astype(
            jnp.bfloat16
        )


def state_work(
    key_hbm,
    value_hbm,
    rate_hbm,
    doc_hbm,
    *refs,
):
    out_ref, key_ref, value_ref, rate_ref, doc_ref, sems, small = refs[-7:]
    rows = rate_ref.shape[1]
    wide = key_ref.shape[1]
    parts = sems.shape[0]
    piece = wide // parts
    copies = [
        pltpu.make_async_copy(rate_hbm.at[0], rate_ref, small.at[0]),
        pltpu.make_async_copy(doc_hbm, doc_ref, small.at[1]),
    ]
    pieces = []
    for part in range(parts):
        span = pl.ds(part * piece, piece)
        pieces.append(
            [
                pltpu.make_async_copy(
                    key_hbm.at[0, :, span], key_ref.at[:, span], sems.at[part, 0]
                ),
                pltpu.make_async_copy(
                    value_hbm.at[0, :, span], value_ref.at[:, span], sems.at[part, 1]
                ),
            ]
        )
    for copy in copies + sum(pieces, []):
        copy.start()
    for copy in copies:
        copy.wait()
    columns, across = running_sums(rate_ref[...])
    for part in range(parts):
        for copy in pieces[part]:
            copy.wait()
    own_fading(doc_ref[...], across, key_ref, value_ref, 0, out_ref)


def state_kernel(*refs):
    @pl.when(lax.axis_index("ctx") < lax.axis_size("ctx") - 1)
    def _():
        state_work(*refs)


def inside_kernel(
    query_hbm,
    key_hbm,
    value_hbm,
    gate_hbm,
    rate_hbm,
    doc_hbm,
    gain_hbm,
    weight_hbm,
    out_ref,
    factor_ref,
    doc_out_ref,
    query_ref,
    weight_ref,
    key_ref,
    value_ref,
    gate_ref,
    rate_ref,
    doc_ref,
    gain_ref,
    sems,
):
    sources = [rate_hbm.at[0], doc_hbm, gain_hbm, query_hbm.at[0], key_hbm.at[0], value_hbm.at[0]]
    sources += [gate_hbm.at[0], weight_hbm.at[0]]
    targets = [rate_ref, doc_ref, gain_ref, query_ref, key_ref, value_ref, gate_ref, weight_ref]
    copies = [
        pltpu.make_async_copy(source, target, sems.at[i])
        for i, (source, target) in enumerate(zip(sources, targets))
    ]
    for copy in copies:
        copy.start()
    for copy in copies[:3]:
        copy.wait()
    heads, rows = rate_ref.shape
    columns, across = running_sums(rate_ref[...])
    reach = jnp.exp(columns)
    doc_across = jnp.broadcast_to(doc_ref[...].astype(jnp.float32) + 1.0, (rows, rows))
    doc_out_ref[...] = doc_across.T
    allowed = (
        lax.broadcasted_iota(jnp.int32, (rows, rows), 0)
        >= lax.broadcasted_iota(jnp.int32, (rows, rows), 1)
    ) & (doc_across == doc_across.T)
    for copy in copies[3:6]:
        copy.wait()
    for h in range(heads):
        span = slice(h * DH, (h + 1) * DH)
        gaps = columns[:, h : h + 1] - across[h : h + 1, :]
        weights = jnp.where(allowed, jnp.exp(jnp.where(allowed, gaps, 0.0)), 0.0)
        scores = dot(query_ref[:, span], key_ref[:, span], ((1,), (1,)))
        mixed = (scores * weights).astype(jnp.bfloat16)
        out_ref[:, span] = dot(mixed, value_ref[:, span])
        reached = query_ref[:, span].astype(jnp.float32) * reach[:, h : h + 1]
        query_ref[:, span] = reached.astype(jnp.bfloat16)
    copies[6].wait()
    for h in range(heads):
        span = slice(h * DH, (h + 1) * DH)
        gate = jax.nn.sigmoid(gate_ref[:, span].astype(jnp.float32))
        factor_ref[:, span] = gain_ref[:, span] * gate
    copies[7].wait()


def finish_kernel(inside_ref, factor_ref, doc_ref, query_ref, state_ref, *out_refs):
    width = inside_ref.shape[1]
    part = out_refs[0].shape[0]
    incoming = state_ref[width:, :].astype(jnp.float32)[0:1, :]
    reached = (doc_ref[...] == incoming).astype(jnp.float32)
    average = jnp.full((DH, DH), 1.0 / DH, jnp.bfloat16)
    for start in range(0, width, DH):
        span = slice(start, start + DH)
        attended = inside_ref[:, span] + reached * dot(query_ref[:, span], state_ref[span, :])
        mean = dot((attended * attended).astype(jnp.bfloat16), average)
        scaling = lax.rsqrt(mean + 1e-06) * factor_ref[:, span]
        normed = (attended * scaling).astype(jnp.bfloat16)
        for i, out_ref in enumerate(out_refs):
            out_ref[:, span] = normed[i * part : (i + 1) * part]


def project_kernel(other, *refs):
    out_ref = refs[-1]
    blocks, rows, columns = out_ref.shape
    pieces, weight_ref = refs[:blocks], refs[blocks]
    half = (lax.axis_index("head") & 1) ^ other
    wide = math.gcd(columns, 256)
    everything = jnp.concatenate([piece[...] for piece in pieces], axis=0)
    for start in range(0, columns, wide):
        span = pl.ds(pl.multiple_of(half * columns + start, wide), wide)
        result = dot(everything, weight_ref[:, span]).astype(jnp.bfloat16)
        for j in range(blocks):
            out_ref[j, :, start : start + wide] = result[j * rows : (j + 1) * rows]


def hold_kernel(upper_ref, lower_ref, *refs):
    for source_ref, out_ref in zip((upper_ref, lower_ref), refs[-2:]):
        out_ref[...] = source_ref[...]


def merge_kernel(layout, *refs):
    out_refs = refs[-len(layout) :]
    rows = refs[0].shape[1]
    for out_ref, places in zip(out_refs, layout):
        for i, (source, block) in enumerate(places):
            keep_ref, arrived_ref = refs[2 * source], refs[2 * source + 1]
            total = keep_ref[block].astype(jnp.float32) + arrived_ref[block].astype(jnp.float32)
            out_ref[i * rows : (i + 1) * rows, :] = total.astype(jnp.bfloat16)


def pick_kernel(*refs):
    count = lax.axis_size("head")
    block_refs, out_refs = refs[: -count], refs[-count:]
    at = lax.axis_index("ctx") ^ lax.axis_index("head")
    for m, out_ref in enumerate(out_refs):
        for j in range(count):

            @pl.when((at ^ m) == j)
            def _(out_ref=out_ref, j=j):
                if j < count - 1:
                    out_ref[...] = block_refs[j][...]
                else:
                    out_ref[...] = jnp.concatenate([ref[...] for ref in block_refs[j:]], axis=0)


def sum_kernel(one_ref, two_ref, out_ref):
    total = one_ref[...].astype(jnp.float32) + two_ref[...].astype(jnp.float32)
    out_ref[...] = total.astype(jnp.bfloat16)


def last_kernel(*refs):
    out_ref = refs[-1]
    wide = refs[0].shape[1]
    for m in range(2):
        half = (lax.axis_index("head") & 1) ^ m
        out_ref[0, :, pl.ds(pl.multiple_of(half * wide, wide), wide)] = refs[m][...]


def call(kernel, out_shape, name, limit=24, **more):
    return pl.pallas_call(
        kernel,
        out_shape=out_shape,
        compiler_params=pltpu.CompilerParams(vmem_limit_bytes=limit * 2**20),
        cost_estimate=pl.CostEstimate(flops=1, bytes_accessed=1, transcendentals=0),
        name=name,
        **more,
    )


def on_device(sizes, queries, keys, values, gates, log_decay, segment_ids, norm_gain, out_weight):
    n_ctx, n_head, n_pipe = sizes
    rows, width = queries.shape[1:]
    heads = width // DH
    tokens = rows * n_ctx
    hops = min(n_ctx - 1, -(-(tokens // 4 - 1) // rows))

    def stay(array):
        return pltpu.with_memory_space_constraint(array, pltpu.HBM)

    rates = stay(jnp.swapaxes(log_decay, 1, 2))
    queries, keys, values, gates = map(stay, (queries, keys, values, gates))
    segment_ids, norm_gain, out_weight = map(stay, (segment_ids, norm_gain, out_weight))
    columns = out_weight.shape[2]
    side = heads
    wide = width

    def from_before(array, by):
        return lax.ppermute(array, "ctx", [(i, i + by) for i in range(n_ctx - by)])

    parts = 4 if side % 4 == 0 else 1
    state_shape = jax.ShapeDtypeStruct((wide + EXTRA, DH), jnp.bfloat16)
    state = call(
        state_kernel,
        state_shape,
        "shard_state",
        in_specs=[HBM] * 4,
        scratch_shapes=[
            pltpu.VMEM((rows, wide), jnp.bfloat16),
            pltpu.VMEM((rows, wide), jnp.bfloat16),
            pltpu.VMEM((heads, rows), jnp.float32),
            pltpu.VMEM((1, rows), jnp.int32),
            pltpu.SemaphoreType.DMA((parts, 2)),
            pltpu.SemaphoreType.DMA((2,)),
        ],
    )(keys, values, rates, segment_ids)

    def entering(state, first):
        incoming = from_before(state, 1)
        if hops > 1:
            decay = jnp.exp(jnp.sum(log_decay[0, :, first : first + side], axis=0))
            decay = decay.astype(jnp.bfloat16)
            total = incoming[:wide].reshape(side, DH, DH).astype(jnp.float32)
            through = jnp.ones((side,), jnp.float32)
            for by in range(2, hops + 1):
                through = through * from_before(decay, by - 1).astype(jnp.float32)
                far = from_before(state, by)
                same = jnp.where(far[wide, 0] == incoming[wide, 0], through, 0.0)
                far = far[:wide].reshape(side, DH, DH).astype(jnp.float32)
                total = total + same[:, None, None] * far
            total = total.reshape(wide, DH).astype(jnp.bfloat16)
            incoming = jnp.concatenate([total, incoming[wide:]], axis=0)
        return incoming

    inside, factor, docs, query, weight = call(
        inside_kernel,
        (
            pltpu.VMEM((rows, width), jnp.float32),
            pltpu.VMEM((rows, width), jnp.float32),
            pltpu.VMEM((rows, DH), jnp.float32),
            pltpu.VMEM((rows, width), jnp.bfloat16),
            pltpu.VMEM((width, columns), jnp.bfloat16),
        ),
        "inside",
        in_specs=[HBM] * 8,
        scratch_shapes=[
            pltpu.VMEM((rows, width), jnp.bfloat16),
            pltpu.VMEM((rows, width), jnp.bfloat16),
            pltpu.VMEM((rows, width), jnp.bfloat16),
            pltpu.VMEM((heads, rows), jnp.float32),
            pltpu.VMEM((1, rows), jnp.int32),
            pltpu.VMEM((1, width), jnp.float32),
            pltpu.SemaphoreType.DMA((8,)),
        ],
    )(queries, keys, values, gates, rates, segment_ids, norm_gain, out_weight)
    incoming = entering(state, 0)

    part = rows // 2
    normed = call(
        finish_kernel,
        (jax.ShapeDtypeStruct((part, width), jnp.bfloat16),) * 2,
        "finish",
    )(inside, factor, docs, query, incoming)

    if n_ctx != 4 or n_head != 4 or n_pipe != 2:
        normed = lax.all_gather(jnp.concatenate(normed, axis=0), "ctx", axis=0, tiled=True)
        blocks = jnp.dot(normed, weight, preferred_element_type=jnp.float32).astype(jnp.bfloat16)
        blocks = lax.all_to_all(blocks.reshape(n_ctx, rows, columns), "ctx", 0, 0, tiled=True)
        blocks = blocks.reshape(n_head, n_ctx // n_head, rows, columns)
        blocks = lax.all_to_all(blocks, "head", 0, 0, tiled=True)
        total = jnp.sum(blocks.astype(jnp.float32), axis=0).astype(jnp.bfloat16)
        total = jnp.swapaxes(total, 0, 1).reshape(1, rows, -1)
        return lax.ppermute(total, "pipe", [(s, (s + 1) % n_pipe) for s in range(n_pipe)])

    def moved(array, target):
        names = ("ctx", "head", "pipe")
        spots = [(i, j, s) for i in range(n_ctx) for j in range(n_head) for s in range(n_pipe)]
        place = {spot: at for at, spot in enumerate(spots)}
        return lax.ppermute(array, names, [(place[spot], place[target(*spot)]) for spot in spots])

    def swapped(array, by):
        return moved(array, lambda i, j, s: (i ^ by, j, s))

    single = jax.ShapeDtypeStruct((rows, columns // 2), jnp.bfloat16)

    def project(picked, other, after=()):
        shape = jax.ShapeDtypeStruct((len(picked), part, columns // 2), jnp.bfloat16)
        specs = [VMEM] * (len(picked) + 1) + [ANY] * len(after)
        kernel = functools.partial(project_kernel, other)
        return call(kernel, shape, "project", in_specs=specs)(*picked, weight, *after)

    def partner(send):
        return moved(send, lambda i, j, s: (i, j ^ 1, s))

    def merge(layout, sums, after=()):
        specs = [VMEM] * len(sums) + [ANY] * len(after)
        kernel = functools.partial(merge_kernel, layout)
        shapes = [jax.ShapeDtypeStruct((part * len(x), columns // 2), jnp.bfloat16) for x in layout]
        return call(kernel, tuple(shapes), "merge", in_specs=specs)(*sums, *after)

    upper, lower = normed
    upper_1, lower_2 = swapped(upper, 1), swapped(lower, 2)
    whole = (((0, 0), (0, 1)),)

    def hold(pair, after):
        shape = jax.ShapeDtypeStruct((part, width), jnp.bfloat16)
        specs = [VMEM] * 2 + [ANY] * len(after)
        return call(hold_kernel, (shape,) * 2, "hold", in_specs=specs)(*pair, *after)

    own_send = project((upper, lower), 1)
    own = merge(whole, (project((upper, lower), 0), partner(own_send)))
    lower_1, upper_2 = swapped(lower, 1), swapped(upper, 2)
    near, later = (upper_1, upper_2), (lower_1, lower_2)
    near_send, near_keep = project(near, 1, own), project(near, 0)
    held = hold((upper_1, lower_2), (lower_1, upper_2, *own, near_send, near_keep))
    later_send, later_keep = project(later, 1), project(later, 0)
    beside = merge(
        (((0, 0), (1, 0)), ((0, 1), (1, 1))),
        (near_keep, partner(near_send), later_keep, partner(later_send)),
    )
    across = (swapped(held[0], 2), swapped(held[1], 1))
    across_sum = (project(across, 0), partner(project(across, 1, (later_keep,))))
    across = merge(whole, across_sum, beside[:1])
    blocks = [swapped(block, k) if k else block for k, block in enumerate((*own, *beside, *across))]
    picked = call(pick_kernel, (single,) * n_head, "pick")(*blocks)
    arrived = [moved(picked[m], lambda i, j, s, m=m: (i, j ^ m, s)) for m in (1, 2, 3)]
    total = [call(sum_kernel, single, "sum")(picked[0], arrived[1])]
    total.append(call(sum_kernel, single, "sum")(arrived[0], arrived[2]))
    total = [moved(half, lambda i, j, s: (i, j, 1 - s)) for half in total]
    out = jax.ShapeDtypeStruct((1, rows, columns), jnp.bfloat16)
    return call(last_kernel, out, "last")(*total)


def solution(mesh):
    sizes = tuple(mesh.shape[axis] for axis in ("ctx", "head", "pipe"))
    return jax.shard_map(
        functools.partial(on_device, sizes),
        mesh=mesh,
        in_specs=(
            P("pipe", "ctx", "head"),
            P("pipe", "ctx", "head"),
            P("pipe", "ctx", "head"),
            P("pipe", "ctx", "head"),
            P("pipe", "ctx", "head"),
            P("pipe", "ctx"),
            P("pipe", "head"),
            P("pipe", "head", "ctx"),
        ),
        out_specs=P("pipe", "ctx", "head"),
        check_vma=False,
    )
```

```python
import functools
import math

import jax
import jax.numpy as jnp
from jax import lax
from jax.experimental import pallas as pl
from jax.experimental.pallas import tpu as pltpu
from jax.sharding import PartitionSpec as P

DH = 128
EXTRA = 16
VMEM = pl.BlockSpec(memory_space=pltpu.VMEM)
ANY = pl.BlockSpec(memory_space=pl.ANY)
HBM = pl.BlockSpec(memory_space=pltpu.HBM)


def dot(a, b, contract=((1,), (0,)), precision=None):
    return lax.dot_general(
        a, b, (contract, ((), ())), preferred_element_type=jnp.float32, precision=precision
    )


def running_sums(rate):
    rows = rate.shape[1]
    upper = (
        lax.broadcasted_iota(jnp.int32, (rows, rows), 0)
        <= lax.broadcasted_iota(jnp.int32, (rows, rows), 1)
    ).astype(jnp.float32)
    across = dot(rate, upper, precision=lax.Precision.HIGHEST)
    columns = dot(upper, rate, ((0,), (1,)), precision=lax.Precision.HIGHEST)
    return columns, across


def own_fading(doc, across, key_ref, value_ref, first, out_ref):
    rows = doc.shape[1]
    wide = out_ref.shape[0] - EXTRA
    last_doc = doc[:, rows - 1 :]
    fading = jnp.where(doc == last_doc, jnp.exp(across[:, rows - 1 :] - across), 0.0)
    fading_columns = fading.T
    out_ref[wide:, :] = jnp.broadcast_to(
        (last_doc + 1).astype(jnp.float32), (EXTRA, DH)
    ).astype(jnp.bfloat16)
    for k in range(wide // DH):
        h = first + k
        span = slice(h * DH, (h + 1) * DH)
        faded = (key_ref[:, span].astype(jnp.float32) * fading_columns[:, h : h + 1]).astype(
            jnp.bfloat16
        )
        out_ref[k * DH : (k + 1) * DH, :] = dot(faded, value_ref[:, span], ((0,), (0,))).astype(
            jnp.bfloat16
        )


def state_work(
    key_hbm,
    value_hbm,
    rate_hbm,
    doc_hbm,
    *refs,
):
    out_ref, key_ref, value_ref, rate_ref, doc_ref, sems, small = refs[-7:]
    rows = rate_ref.shape[1]
    wide = key_ref.shape[1]
    parts = sems.shape[0]
    piece = wide // parts
    copies = [
        pltpu.make_async_copy(rate_hbm.at[0], rate_ref, small.at[0]),
        pltpu.make_async_copy(doc_hbm, doc_ref, small.at[1]),
    ]
    pieces = []
    for part in range(parts):
        span = pl.ds(part * piece, piece)
        pieces.append(
            [
                pltpu.make_async_copy(
                    key_hbm.at[0, :, span], key_ref.at[:, span], sems.at[part, 0]
                ),
                pltpu.make_async_copy(
                    value_hbm.at[0, :, span], value_ref.at[:, span], sems.at[part, 1]
                ),
            ]
        )
    for copy in copies + sum(pieces, []):
        copy.start()
    for copy in copies:
        copy.wait()
    columns, across = running_sums(rate_ref[...])
    for part in range(parts):
        for copy in pieces[part]:
            copy.wait()
    own_fading(doc_ref[...], across, key_ref, value_ref, 0, out_ref)


def state_kernel(*refs):
    @pl.when(lax.axis_index("ctx") < lax.axis_size("ctx") - 1)
    def _():
        state_work(*refs)


def inside_kernel(
    query_hbm,
    key_hbm,
    value_hbm,
    gate_hbm,
    rate_hbm,
    doc_hbm,
    gain_hbm,
    weight_hbm,
    out_ref,
    factor_ref,
    doc_out_ref,
    query_ref,
    weight_ref,
    key_ref,
    value_ref,
    gate_ref,
    rate_ref,
    doc_ref,
    gain_ref,
    sems,
):
    sources = [rate_hbm.at[0], doc_hbm, gain_hbm, query_hbm.at[0], key_hbm.at[0], value_hbm.at[0]]
    sources += [gate_hbm.at[0], weight_hbm.at[0]]
    targets = [rate_ref, doc_ref, gain_ref, query_ref, key_ref, value_ref, gate_ref, weight_ref]
    copies = [
        pltpu.make_async_copy(source, target, sems.at[i])
        for i, (source, target) in enumerate(zip(sources, targets))
    ]
    for copy in copies:
        copy.start()
    for copy in copies[:3]:
        copy.wait()
    heads, rows = rate_ref.shape
    columns, across = running_sums(rate_ref[...])
    reach = jnp.exp(columns)
    doc_across = jnp.broadcast_to(doc_ref[...].astype(jnp.float32) + 1.0, (rows, rows))
    doc_out_ref[...] = doc_across.T
    allowed = (
        lax.broadcasted_iota(jnp.int32, (rows, rows), 0)
        >= lax.broadcasted_iota(jnp.int32, (rows, rows), 1)
    ) & (doc_across == doc_across.T)
    for copy in copies[3:6]:
        copy.wait()
    for h in range(heads):
        span = slice(h * DH, (h + 1) * DH)
        gaps = columns[:, h : h + 1] - across[h : h + 1, :]
        weights = jnp.where(allowed, jnp.exp(jnp.where(allowed, gaps, 0.0)), 0.0)
        scores = dot(query_ref[:, span], key_ref[:, span], ((1,), (1,)))
        mixed = (scores * weights).astype(jnp.bfloat16)
        out_ref[:, span] = dot(mixed, value_ref[:, span])
        reached = query_ref[:, span].astype(jnp.float32) * reach[:, h : h + 1]
        query_ref[:, span] = reached.astype(jnp.bfloat16)
    copies[6].wait()
    for h in range(heads):
        span = slice(h * DH, (h + 1) * DH)
        gate = jax.nn.sigmoid(gate_ref[:, span].astype(jnp.float32))
        factor_ref[:, span] = gain_ref[:, span] * gate
    copies[7].wait()


def finish_kernel(inside_ref, factor_ref, doc_ref, query_ref, state_ref, *out_refs):
    width = inside_ref.shape[1]
    part = out_refs[0].shape[0]
    incoming = state_ref[width:, :].astype(jnp.float32)[0:1, :]
    reached = (doc_ref[...] == incoming).astype(jnp.float32)
    average = jnp.full((DH, DH), 1.0 / DH, jnp.bfloat16)
    for start in range(0, width, DH):
        span = slice(start, start + DH)
        attended = inside_ref[:, span] + reached * dot(query_ref[:, span], state_ref[span, :])
        mean = dot((attended * attended).astype(jnp.bfloat16), average)
        scaling = lax.rsqrt(mean + 1e-06) * factor_ref[:, span]
        normed = (attended * scaling).astype(jnp.bfloat16)
        for i, out_ref in enumerate(out_refs):
            out_ref[:, span] = normed[i * part : (i + 1) * part]


def project_kernel(other, *refs):
    out_ref = refs[-1]
    blocks, rows, columns = out_ref.shape
    pieces, weight_ref = refs[:blocks], refs[blocks]
    half = (lax.axis_index("head") & 1) ^ other
    wide = math.gcd(columns, 256)
    everything = jnp.concatenate([piece[...] for piece in pieces], axis=0)
    for start in range(0, columns, wide):
        span = pl.ds(pl.multiple_of(half * columns + start, wide), wide)
        result = dot(everything, weight_ref[:, span]).astype(jnp.bfloat16)
        for j in range(blocks):
            out_ref[j, :, start : start + wide] = result[j * rows : (j + 1) * rows]


def hold_kernel(upper_ref, lower_ref, *refs):
    for source_ref, out_ref in zip((upper_ref, lower_ref), refs[-2:]):
        out_ref[...] = source_ref[...]


def merge_kernel(layout, *refs):
    out_refs = refs[-len(layout) :]
    rows = refs[0].shape[1]
    for out_ref, places in zip(out_refs, layout):
        for i, (source, block) in enumerate(places):
            keep_ref, arrived_ref = refs[2 * source], refs[2 * source + 1]
            total = keep_ref[block].astype(jnp.float32) + arrived_ref[block].astype(jnp.float32)
            out_ref[i * rows : (i + 1) * rows, :] = total.astype(jnp.bfloat16)


def pick_kernel(*refs):
    count = lax.axis_size("head")
    block_refs, out_refs = refs[: -count], refs[-count:]
    at = lax.axis_index("ctx") ^ lax.axis_index("head")
    for m, out_ref in enumerate(out_refs):
        for j in range(count):

            @pl.when((at ^ m) == j)
            def _(out_ref=out_ref, j=j):
                if j < count - 1:
                    out_ref[...] = block_refs[j][...]
                else:
                    out_ref[...] = jnp.concatenate([ref[...] for ref in block_refs[j:]], axis=0)


def sum_kernel(one_ref, two_ref, out_ref):
    total = one_ref[...].astype(jnp.float32) + two_ref[...].astype(jnp.float32)
    out_ref[...] = total.astype(jnp.bfloat16)


def last_kernel(*refs):
    out_ref = refs[-1]
    wide = refs[0].shape[1]
    for m in range(2):
        half = (lax.axis_index("head") & 1) ^ m
        out_ref[0, :, pl.ds(pl.multiple_of(half * wide, wide), wide)] = refs[m][...]


def call(kernel, out_shape, name, limit=24, **more):
    return pl.pallas_call(
        kernel,
        out_shape=out_shape,
        compiler_params=pltpu.CompilerParams(vmem_limit_bytes=limit * 2**20),
        cost_estimate=pl.CostEstimate(flops=1, bytes_accessed=1, transcendentals=0),
        name=name,
        **more,
    )


def on_device(sizes, queries, keys, values, gates, log_decay, segment_ids, norm_gain, out_weight):
    n_ctx, n_head, n_pipe = sizes
    rows, width = queries.shape[1:]
    heads = width // DH
    tokens = rows * n_ctx
    hops = min(n_ctx - 1, -(-(tokens // 4 - 1) // rows))

    def stay(array):
        return pltpu.with_memory_space_constraint(array, pltpu.HBM)

    rates = stay(jnp.swapaxes(log_decay, 1, 2))
    queries, keys, values, gates = map(stay, (queries, keys, values, gates))
    segment_ids, norm_gain, out_weight = map(stay, (segment_ids, norm_gain, out_weight))
    columns = out_weight.shape[2]
    side = heads
    wide = width

    def from_before(array, by):
        return lax.ppermute(array, "ctx", [(i, i + by) for i in range(n_ctx - by)])

    parts = 4 if side % 4 == 0 else 1
    state_shape = jax.ShapeDtypeStruct((wide + EXTRA, DH), jnp.bfloat16)
    state = call(
        state_kernel,
        state_shape,
        "shard_state",
        in_specs=[HBM] * 4,
        scratch_shapes=[
            pltpu.VMEM((rows, wide), jnp.bfloat16),
            pltpu.VMEM((rows, wide), jnp.bfloat16),
            pltpu.VMEM((heads, rows), jnp.float32),
            pltpu.VMEM((1, rows), jnp.int32),
            pltpu.SemaphoreType.DMA((parts, 2)),
            pltpu.SemaphoreType.DMA((2,)),
        ],
    )(keys, values, rates, segment_ids)

    def entering(state, first):
        incoming = from_before(state, 1)
        if hops > 1:
            decay = jnp.exp(jnp.sum(log_decay[0, :, first : first + side], axis=0))
            decay = decay.astype(jnp.bfloat16)
            total = incoming[:wide].reshape(side, DH, DH).astype(jnp.float32)
            through = jnp.ones((side,), jnp.float32)
            for by in range(2, hops + 1):
                through = through * from_before(decay, by - 1).astype(jnp.float32)
                far = from_before(state, by)
                same = jnp.where(far[wide, 0] == incoming[wide, 0], through, 0.0)
                far = far[:wide].reshape(side, DH, DH).astype(jnp.float32)
                total = total + same[:, None, None] * far
            total = total.reshape(wide, DH).astype(jnp.bfloat16)
            incoming = jnp.concatenate([total, incoming[wide:]], axis=0)
        return incoming

    inside, factor, docs, query, weight = call(
        inside_kernel,
        (
            pltpu.VMEM((rows, width), jnp.float32),
            pltpu.VMEM((rows, width), jnp.float32),
            pltpu.VMEM((rows, DH), jnp.float32),
            pltpu.VMEM((rows, width), jnp.bfloat16),
            pltpu.VMEM((width, columns), jnp.bfloat16),
        ),
        "inside",
        in_specs=[HBM] * 8,
        scratch_shapes=[
            pltpu.VMEM((rows, width), jnp.bfloat16),
            pltpu.VMEM((rows, width), jnp.bfloat16),
            pltpu.VMEM((rows, width), jnp.bfloat16),
            pltpu.VMEM((heads, rows), jnp.float32),
            pltpu.VMEM((1, rows), jnp.int32),
            pltpu.VMEM((1, width), jnp.float32),
            pltpu.SemaphoreType.DMA((8,)),
        ],
    )(queries, keys, values, gates, rates, segment_ids, norm_gain, out_weight)
    incoming = entering(state, 0)

    part = rows // 2
    normed = call(
        finish_kernel,
        (jax.ShapeDtypeStruct((part, width), jnp.bfloat16),) * 2,
        "finish",
    )(inside, factor, docs, query, incoming)

    if n_ctx != 4 or n_head != 4 or n_pipe != 2:
        normed = lax.all_gather(jnp.concatenate(normed, axis=0), "ctx", axis=0, tiled=True)
        blocks = jnp.dot(normed, weight, preferred_element_type=jnp.float32).astype(jnp.bfloat16)
        blocks = lax.all_to_all(blocks.reshape(n_ctx, rows, columns), "ctx", 0, 0, tiled=True)
        blocks = blocks.reshape(n_head, n_ctx // n_head, rows, columns)
        blocks = lax.all_to_all(blocks, "head", 0, 0, tiled=True)
        total = jnp.sum(blocks.astype(jnp.float32), axis=0).astype(jnp.bfloat16)
        total = jnp.swapaxes(total, 0, 1).reshape(1, rows, -1)
        return lax.ppermute(total, "pipe", [(s, (s + 1) % n_pipe) for s in range(n_pipe)])

    def moved(array, target):
        names = ("ctx", "head", "pipe")
        spots = [(i, j, s) for i in range(n_ctx) for j in range(n_head) for s in range(n_pipe)]
        place = {spot: at for at, spot in enumerate(spots)}
        return lax.ppermute(array, names, [(place[spot], place[target(*spot)]) for spot in spots])

    def swapped(array, by):
        return moved(array, lambda i, j, s: (i ^ by, j, s))

    single = jax.ShapeDtypeStruct((rows, columns // 2), jnp.bfloat16)

    def project(picked, other, after=()):
        shape = jax.ShapeDtypeStruct((len(picked), part, columns // 2), jnp.bfloat16)
        specs = [VMEM] * (len(picked) + 1) + [ANY] * len(after)
        kernel = functools.partial(project_kernel, other)
        return call(kernel, shape, "project", in_specs=specs)(*picked, weight, *after)

    def partner(send):
        return moved(send, lambda i, j, s: (i, j ^ 1, s))

    def merge(layout, sums, after=()):
        specs = [VMEM] * len(sums) + [ANY] * len(after)
        kernel = functools.partial(merge_kernel, layout)
        shapes = [jax.ShapeDtypeStruct((part * len(x), columns // 2), jnp.bfloat16) for x in layout]
        return call(kernel, tuple(shapes), "merge", in_specs=specs)(*sums, *after)

    upper, lower = normed
    upper_1, lower_2 = swapped(upper, 1), swapped(lower, 2)
    whole = (((0, 0), (0, 1)),)

    def hold(pair, after):
        shape = jax.ShapeDtypeStruct((part, width), jnp.bfloat16)
        specs = [VMEM] * 2 + [ANY] * len(after)
        return call(hold_kernel, (shape,) * 2, "hold", in_specs=specs)(*pair, *after)

    own_send = project((upper, lower), 1)
    own = merge(whole, (project((upper, lower), 0), partner(own_send)))
    lower_1, upper_2 = swapped(lower, 1), swapped(upper, 2)
    near, later = (upper_1, upper_2), (lower_1, lower_2)
    near_send, near_keep = project(near, 1, own), project(near, 0)
    held = hold((upper_1, lower_2), (lower_1, upper_2, *own, near_send, near_keep))
    later_send, later_keep = project(later, 1), project(later, 0)
    beside = merge(
        (((0, 0), (1, 0)), ((0, 1), (1, 1))),
        (near_keep, partner(near_send), later_keep, partner(later_send)),
    )
    across = (swapped(held[0], 2), swapped(held[1], 1))
    across_sum = (project(across, 0), partner(project(across, 1, (later_keep,))))
    across = merge(whole, across_sum, beside[:1])
    blocks = [swapped(block, k) if k else block for k, block in enumerate((*own, *beside, *across))]
    picked = call(pick_kernel, (single,) * n_head, "pick")(*blocks)
    arrived = [moved(picked[m], lambda i, j, s, m=m: (i, j ^ m, s)) for m in (1, 2, 3)]
    total = [call(sum_kernel, single, "sum")(picked[0], arrived[1])]
    total.append(call(sum_kernel, single, "sum")(arrived[2], arrived[0]))
    total = [moved(half, lambda i, j, s: (i, j, 1 - s)) for half in total]
    out = jax.ShapeDtypeStruct((1, rows, columns), jnp.bfloat16)
    return call(last_kernel, out, "last")(*total)


def solution(mesh):
    sizes = tuple(mesh.shape[axis] for axis in ("ctx", "head", "pipe"))
    return jax.shard_map(
        functools.partial(on_device, sizes),
        mesh=mesh,
        in_specs=(
            P("pipe", "ctx", "head"),
            P("pipe", "ctx", "head"),
            P("pipe", "ctx", "head"),
            P("pipe", "ctx", "head"),
            P("pipe", "ctx", "head"),
            P("pipe", "ctx"),
            P("pipe", "head"),
            P("pipe", "head", "ctx"),
        ),
        out_specs=P("pipe", "ctx", "head"),
        check_vma=False,
    )
```

```python
import functools
import math

import jax
import jax.numpy as jnp
from jax import lax
from jax.experimental import pallas as pl
from jax.experimental.pallas import tpu as pltpu
from jax.sharding import PartitionSpec as P

DH = 128
EXTRA = 16
VMEM = pl.BlockSpec(memory_space=pltpu.VMEM)
ANY = pl.BlockSpec(memory_space=pl.ANY)
HBM = pl.BlockSpec(memory_space=pltpu.HBM)


def dot(a, b, contract=((1,), (0,)), precision=None):
    return lax.dot_general(
        a, b, (contract, ((), ())), preferred_element_type=jnp.float32, precision=precision
    )


def running_sums(rate):
    rows = rate.shape[1]
    upper = (
        lax.broadcasted_iota(jnp.int32, (rows, rows), 0)
        <= lax.broadcasted_iota(jnp.int32, (rows, rows), 1)
    ).astype(jnp.float32)
    across = dot(rate, upper, precision=lax.Precision.HIGHEST)
    columns = dot(upper, rate, ((0,), (1,)), precision=lax.Precision.HIGHEST)
    return columns, across


def own_fading(doc, across, key_ref, value_ref, first, out_ref):
    rows = doc.shape[1]
    wide = out_ref.shape[0] - EXTRA
    last_doc = doc[:, rows - 1 :]
    fading = jnp.where(doc == last_doc, jnp.exp(across[:, rows - 1 :] - across), 0.0)
    fading_columns = fading.T
    out_ref[wide:, :] = jnp.broadcast_to(
        (last_doc + 1).astype(jnp.float32), (EXTRA, DH)
    ).astype(jnp.bfloat16)
    for k in range(wide // DH):
        h = first + k
        span = slice(h * DH, (h + 1) * DH)
        faded = (key_ref[:, span].astype(jnp.float32) * fading_columns[:, h : h + 1]).astype(
            jnp.bfloat16
        )
        out_ref[k * DH : (k + 1) * DH, :] = dot(faded, value_ref[:, span], ((0,), (0,))).astype(
            jnp.bfloat16
        )


def state_work(
    key_hbm,
    value_hbm,
    rate_hbm,
    doc_hbm,
    *refs,
):
    out_ref, key_ref, value_ref, rate_ref, doc_ref, sems, small = refs[-7:]
    rows = rate_ref.shape[1]
    wide = key_ref.shape[1]
    parts = sems.shape[0]
    piece = wide // parts
    copies = [
        pltpu.make_async_copy(rate_hbm.at[0], rate_ref, small.at[0]),
        pltpu.make_async_copy(doc_hbm, doc_ref, small.at[1]),
    ]
    pieces = []
    for part in range(parts):
        span = pl.ds(part * piece, piece)
        pieces.append(
            [
                pltpu.make_async_copy(
                    key_hbm.at[0, :, span], key_ref.at[:, span], sems.at[part, 0]
                ),
                pltpu.make_async_copy(
                    value_hbm.at[0, :, span], value_ref.at[:, span], sems.at[part, 1]
                ),
            ]
        )
    for copy in copies + sum(pieces, []):
        copy.start()
    for copy in copies:
        copy.wait()
    columns, across = running_sums(rate_ref[...])
    for part in range(parts):
        for copy in pieces[part]:
            copy.wait()
    own_fading(doc_ref[...], across, key_ref, value_ref, 0, out_ref)


def state_kernel(*refs):
    @pl.when(lax.axis_index("ctx") < lax.axis_size("ctx") - 1)
    def _():
        state_work(*refs)


def inside_kernel(
    query_hbm,
    key_hbm,
    value_hbm,
    gate_hbm,
    rate_hbm,
    doc_hbm,
    gain_hbm,
    weight_hbm,
    out_ref,
    factor_ref,
    doc_out_ref,
    query_ref,
    weight_ref,
    key_ref,
    value_ref,
    gate_ref,
    rate_ref,
    doc_ref,
    gain_ref,
    sems,
):
    sources = [rate_hbm.at[0], doc_hbm, gain_hbm, query_hbm.at[0], key_hbm.at[0], value_hbm.at[0]]
    sources += [gate_hbm.at[0], weight_hbm.at[0]]
    targets = [rate_ref, doc_ref, gain_ref, query_ref, key_ref, value_ref, gate_ref, weight_ref]
    copies = [
        pltpu.make_async_copy(source, target, sems.at[i])
        for i, (source, target) in enumerate(zip(sources, targets))
    ]
    for copy in copies:
        copy.start()
    for copy in copies[:3]:
        copy.wait()
    heads, rows = rate_ref.shape
    columns, across = running_sums(rate_ref[...])
    reach = jnp.exp(columns)
    doc_across = jnp.broadcast_to(doc_ref[...].astype(jnp.float32) + 1.0, (rows, rows))
    doc_out_ref[...] = doc_across.T
    allowed = (
        lax.broadcasted_iota(jnp.int32, (rows, rows), 0)
        >= lax.broadcasted_iota(jnp.int32, (rows, rows), 1)
    ) & (doc_across == doc_across.T)
    for copy in copies[3:6]:
        copy.wait()
    for h in range(heads):
        span = slice(h * DH, (h + 1) * DH)
        gaps = columns[:, h : h + 1] - across[h : h + 1, :]
        weights = jnp.where(allowed, jnp.exp(jnp.where(allowed, gaps, 0.0)), 0.0)
        scores = dot(query_ref[:, span], key_ref[:, span], ((1,), (1,)))
        mixed = (scores * weights).astype(jnp.bfloat16)
        out_ref[:, span] = dot(mixed, value_ref[:, span])
        reached = query_ref[:, span].astype(jnp.float32) * reach[:, h : h + 1]
        query_ref[:, span] = reached.astype(jnp.bfloat16)
    copies[6].wait()
    for h in range(heads):
        span = slice(h * DH, (h + 1) * DH)
        gate = jax.nn.sigmoid(gate_ref[:, span].astype(jnp.float32))
        factor_ref[:, span] = gain_ref[:, span] * gate
    copies[7].wait()


def finish_kernel(inside_ref, factor_ref, doc_ref, query_ref, state_ref, *out_refs):
    width = inside_ref.shape[1]
    part = out_refs[0].shape[0]
    incoming = state_ref[width:, :].astype(jnp.float32)[0:1, :]
    reached = (doc_ref[...] == incoming).astype(jnp.float32)
    average = jnp.full((DH, DH), 1.0 / DH, jnp.bfloat16)
    for start in range(0, width, DH):
        span = slice(start, start + DH)
        attended = inside_ref[:, span] + reached * dot(query_ref[:, span], state_ref[span, :])
        mean = dot((attended * attended).astype(jnp.bfloat16), average)
        scaling = lax.rsqrt(mean + 1e-06) * factor_ref[:, span]
        normed = (attended * scaling).astype(jnp.bfloat16)
        for i, out_ref in enumerate(out_refs):
            out_ref[:, span] = normed[i * part : (i + 1) * part]


def project_kernel(other, *refs):
    out_ref = refs[-1]
    blocks, rows, columns = out_ref.shape
    pieces, weight_ref = refs[:blocks], refs[blocks]
    half = (lax.axis_index("head") & 1) ^ other
    wide = math.gcd(columns, 256)
    everything = jnp.concatenate([piece[...] for piece in pieces], axis=0)
    for start in range(0, columns, wide):
        span = pl.ds(pl.multiple_of(half * columns + start, wide), wide)
        result = dot(everything, weight_ref[:, span]).astype(jnp.bfloat16)
        for j in range(blocks):
            out_ref[j, :, start : start + wide] = result[j * rows : (j + 1) * rows]


def hold_kernel(upper_ref, lower_ref, *refs):
    for source_ref, out_ref in zip((upper_ref, lower_ref), refs[-2:]):
        out_ref[...] = source_ref[...]


def merge_kernel(layout, *refs):
    out_refs = refs[-len(layout) :]
    rows = refs[0].shape[1]
    for out_ref, places in zip(out_refs, layout):
        for i, (source, block) in enumerate(places):
            keep_ref, arrived_ref = refs[2 * source], refs[2 * source + 1]
            total = keep_ref[block].astype(jnp.float32) + arrived_ref[block].astype(jnp.float32)
            out_ref[i * rows : (i + 1) * rows, :] = total.astype(jnp.bfloat16)


def pick_kernel(*refs):
    count = lax.axis_size("head")
    block_refs, out_refs = refs[: -count], refs[-count:]
    at = lax.axis_index("ctx") ^ lax.axis_index("head")
    for m, out_ref in enumerate(out_refs):
        for j in range(count):

            @pl.when((at ^ m) == j)
            def _(out_ref=out_ref, j=j):
                if j < count - 1:
                    out_ref[...] = block_refs[j][...]
                else:
                    out_ref[...] = jnp.concatenate([ref[...] for ref in block_refs[j:]], axis=0)


def sum_kernel(one_ref, two_ref, out_ref):
    total = one_ref[...].astype(jnp.float32) + two_ref[...].astype(jnp.float32)
    out_ref[...] = total.astype(jnp.bfloat16)


def last_kernel(one_ref, two_ref, out_ref, sems):
    wide = one_ref.shape[1]
    copies = []
    for m, half_ref in enumerate((one_ref, two_ref)):
        half = (lax.axis_index("head") & 1) ^ m
        span = pl.ds(pl.multiple_of(half * wide, wide), wide)
        copies.append(pltpu.make_async_copy(half_ref, out_ref.at[0, :, span], sems.at[m]))
    for copy in copies:
        copy.start()
    for copy in copies:
        copy.wait()


def call(kernel, out_shape, name, limit=24, **more):
    return pl.pallas_call(
        kernel,
        out_shape=out_shape,
        compiler_params=pltpu.CompilerParams(vmem_limit_bytes=limit * 2**20),
        cost_estimate=pl.CostEstimate(flops=1, bytes_accessed=1, transcendentals=0),
        name=name,
        **more,
    )


def on_device(sizes, queries, keys, values, gates, log_decay, segment_ids, norm_gain, out_weight):
    n_ctx, n_head, n_pipe = sizes
    rows, width = queries.shape[1:]
    heads = width // DH
    tokens = rows * n_ctx
    hops = min(n_ctx - 1, -(-(tokens // 4 - 1) // rows))

    def stay(array):
        return pltpu.with_memory_space_constraint(array, pltpu.HBM)

    rates = stay(jnp.swapaxes(log_decay, 1, 2))
    queries, keys, values, gates = map(stay, (queries, keys, values, gates))
    segment_ids, norm_gain, out_weight = map(stay, (segment_ids, norm_gain, out_weight))
    columns = out_weight.shape[2]
    side = heads
    wide = width

    def from_before(array, by):
        return lax.ppermute(array, "ctx", [(i, i + by) for i in range(n_ctx - by)])

    parts = 4 if side % 4 == 0 else 1
    state_shape = jax.ShapeDtypeStruct((wide + EXTRA, DH), jnp.bfloat16)
    state = call(
        state_kernel,
        state_shape,
        "shard_state",
        in_specs=[HBM] * 4,
        scratch_shapes=[
            pltpu.VMEM((rows, wide), jnp.bfloat16),
            pltpu.VMEM((rows, wide), jnp.bfloat16),
            pltpu.VMEM((heads, rows), jnp.float32),
            pltpu.VMEM((1, rows), jnp.int32),
            pltpu.SemaphoreType.DMA((parts, 2)),
            pltpu.SemaphoreType.DMA((2,)),
        ],
    )(keys, values, rates, segment_ids)

    def entering(state, first):
        incoming = from_before(state, 1)
        if hops > 1:
            decay = jnp.exp(jnp.sum(log_decay[0, :, first : first + side], axis=0))
            decay = decay.astype(jnp.bfloat16)
            total = incoming[:wide].reshape(side, DH, DH).astype(jnp.float32)
            through = jnp.ones((side,), jnp.float32)
            for by in range(2, hops + 1):
                through = through * from_before(decay, by - 1).astype(jnp.float32)
                far = from_before(state, by)
                same = jnp.where(far[wide, 0] == incoming[wide, 0], through, 0.0)
                far = far[:wide].reshape(side, DH, DH).astype(jnp.float32)
                total = total + same[:, None, None] * far
            total = total.reshape(wide, DH).astype(jnp.bfloat16)
            incoming = jnp.concatenate([total, incoming[wide:]], axis=0)
        return incoming

    inside, factor, docs, query, weight = call(
        inside_kernel,
        (
            pltpu.VMEM((rows, width), jnp.float32),
            pltpu.VMEM((rows, width), jnp.float32),
            pltpu.VMEM((rows, DH), jnp.float32),
            pltpu.VMEM((rows, width), jnp.bfloat16),
            pltpu.VMEM((width, columns), jnp.bfloat16),
        ),
        "inside",
        in_specs=[HBM] * 8,
        scratch_shapes=[
            pltpu.VMEM((rows, width), jnp.bfloat16),
            pltpu.VMEM((rows, width), jnp.bfloat16),
            pltpu.VMEM((rows, width), jnp.bfloat16),
            pltpu.VMEM((heads, rows), jnp.float32),
            pltpu.VMEM((1, rows), jnp.int32),
            pltpu.VMEM((1, width), jnp.float32),
            pltpu.SemaphoreType.DMA((8,)),
        ],
    )(queries, keys, values, gates, rates, segment_ids, norm_gain, out_weight)
    incoming = entering(state, 0)

    part = rows // 2
    normed = call(
        finish_kernel,
        (jax.ShapeDtypeStruct((part, width), jnp.bfloat16),) * 2,
        "finish",
    )(inside, factor, docs, query, incoming)

    if n_ctx != 4 or n_head != 4 or n_pipe != 2:
        normed = lax.all_gather(jnp.concatenate(normed, axis=0), "ctx", axis=0, tiled=True)
        blocks = jnp.dot(normed, weight, preferred_element_type=jnp.float32).astype(jnp.bfloat16)
        blocks = lax.all_to_all(blocks.reshape(n_ctx, rows, columns), "ctx", 0, 0, tiled=True)
        blocks = blocks.reshape(n_head, n_ctx // n_head, rows, columns)
        blocks = lax.all_to_all(blocks, "head", 0, 0, tiled=True)
        total = jnp.sum(blocks.astype(jnp.float32), axis=0).astype(jnp.bfloat16)
        total = jnp.swapaxes(total, 0, 1).reshape(1, rows, -1)
        return lax.ppermute(total, "pipe", [(s, (s + 1) % n_pipe) for s in range(n_pipe)])

    def moved(array, target):
        names = ("ctx", "head", "pipe")
        spots = [(i, j, s) for i in range(n_ctx) for j in range(n_head) for s in range(n_pipe)]
        place = {spot: at for at, spot in enumerate(spots)}
        return lax.ppermute(array, names, [(place[spot], place[target(*spot)]) for spot in spots])

    def swapped(array, by):
        return moved(array, lambda i, j, s: (i ^ by, j, s))

    single = jax.ShapeDtypeStruct((rows, columns // 2), jnp.bfloat16)

    def project(picked, other, after=()):
        shape = jax.ShapeDtypeStruct((len(picked), part, columns // 2), jnp.bfloat16)
        specs = [VMEM] * (len(picked) + 1) + [ANY] * len(after)
        kernel = functools.partial(project_kernel, other)
        return call(kernel, shape, "project", in_specs=specs)(*picked, weight, *after)

    def partner(send):
        return moved(send, lambda i, j, s: (i, j ^ 1, s))

    def merge(layout, sums, after=()):
        specs = [VMEM] * len(sums) + [ANY] * len(after)
        kernel = functools.partial(merge_kernel, layout)
        shapes = [jax.ShapeDtypeStruct((part * len(x), columns // 2), jnp.bfloat16) for x in layout]
        return call(kernel, tuple(shapes), "merge", in_specs=specs)(*sums, *after)

    upper, lower = normed
    upper_1, lower_2 = swapped(upper, 1), swapped(lower, 2)
    whole = (((0, 0), (0, 1)),)

    def hold(pair, after):
        shape = jax.ShapeDtypeStruct((part, width), jnp.bfloat16)
        specs = [VMEM] * 2 + [ANY] * len(after)
        return call(hold_kernel, (shape,) * 2, "hold", in_specs=specs)(*pair, *after)

    own_send = project((upper, lower), 1)
    own = merge(whole, (project((upper, lower), 0), partner(own_send)))
    lower_1, upper_2 = swapped(lower, 1), swapped(upper, 2)
    held = hold((upper_1, lower_2), (lower_1, upper_2, *own))
    beside = (upper_1, lower_1, upper_2, lower_2)
    beside_send, beside_keep = project(beside, 1, own), project(beside, 0)
    beside = merge(
        (((0, 0), (0, 1)), ((0, 2), (0, 3))),
        (beside_keep, partner(beside_send)),
    )
    across = (swapped(held[0], 2), swapped(held[1], 1))
    across_sum = (project(across, 0), partner(project(across, 1, (beside_keep,))))
    across = merge(whole, across_sum, beside[:1])
    blocks = [swapped(block, k) if k else block for k, block in enumerate((*own, *beside, *across))]
    picked = call(pick_kernel, (single,) * n_head, "pick")(*blocks)
    arrived = [moved(picked[m], lambda i, j, s, m=m: (i, j ^ m, s)) for m in (1, 2, 3)]
    total = [call(sum_kernel, single, "sum")(picked[0], arrived[1])]
    total.append(call(sum_kernel, single, "sum")(arrived[0], arrived[2]))
    total = [moved(half, lambda i, j, s: (i, j, 1 - s)) for half in total]
    out = jax.ShapeDtypeStruct((1, rows, columns), jnp.bfloat16)
    sems = [pltpu.SemaphoreType.DMA((2,))]
    return call(last_kernel, out, "last", out_specs=ANY, scratch_shapes=sems)(*total)


def solution(mesh):
    sizes = tuple(mesh.shape[axis] for axis in ("ctx", "head", "pipe"))
    return jax.shard_map(
        functools.partial(on_device, sizes),
        mesh=mesh,
        in_specs=(
            P("pipe", "ctx", "head"),
            P("pipe", "ctx", "head"),
            P("pipe", "ctx", "head"),
            P("pipe", "ctx", "head"),
            P("pipe", "ctx", "head"),
            P("pipe", "ctx"),
            P("pipe", "head"),
            P("pipe", "head", "ctx"),
        ),
        out_specs=P("pipe", "ctx", "head"),
        check_vma=False,
    )
```
